256 devices in a mesh: spin: 2 (over x_lo), band: 128 (over y, x_hi, z, core).
Axes of the slice: x: 4 (x_hi: 2, x_lo: 2; x = x_hi * 2 + x_lo), y: 4, z: 8, core: 2. Of those that a mesh axis runs over, the one named last changes fastest.
Arguments:
- orbitals: bfloat16 [256, 262144], P(('spin', 'band')), parts along dimension 0, may hold values from -6 to 6
- trial: bfloat16 [256, 262144], P(('spin', 'band')), parts along dimension 0, may hold values from -6 to 6
- occupations: int32 [256], P(('spin', 'band')), parts along dimension 0, may hold values 0 or 1
Outputs:
- exchange: bfloat16 [256, 262144], P(('spin', 'band')), parts along dimension 0
- projected: bfloat16 [256, 262144], P('spin', 'band'), parts along dimension 0
The draws below stay inside these ranges and needn't reach their ends.
There are 2 independent parts, one for each index of `spin`. The reference program is written for one: setup_inputs(seed, part) draws one part's arguments, and reference() takes and returns one part's arrays. A program takes and returns all parts, laid end to end along the dimension named above; each array names one. Nothing has to cross between parts.
All inputs are finite; a program needn't handle non-finite values. No bound on the sum of `occupations` on one device may be relied on, other than what follows from the above.
Results may differ from the reference program's by a relative error of at most 0.018.
Values may be sent and summed in bfloat16 or wider, within the bound.
No kernel may reach another device: no remote copies, remote signals or barrier semaphores. Data moves between devices by JAX's collectives and lax.ppermute only.
A program may use at most 64 MiB of HBM per device.

```python
import math
import jax
import jax.numpy as jnp
from jax import lax

NG = 64
ORB_DEV = 1
SHIFTS = 1
G = 262144
ORBITALS = 128
N_BAND = 128


def touch_ends(values, stream_key, smallest, high):
    longest = values.shape.index(max(values.shape))
    spots = []
    for shift in (0, 1):
        where = [jax.random.randint(jax.random.fold_in(stream_key, axis), (), 0, length) for axis, length in enumerate(values.shape)]
        where[longest] = (where[longest] + shift) % values.shape[longest]
        spots.append(tuple(where))
    return values.at[spots[0]].set(smallest).at[spots[1]].set(high)


def block_levels(rng, shape, shards, smallest, top_value):
    level, own = 1.0, jax.random.fold_in(rng, 6)
    for position, blocks in shards:
        draws = jnp.exp(jax.random.uniform(jax.random.fold_in(own, position), (blocks,), jnp.float32, smallest / len(shards), top_value / len(shards)))
        level = level * jnp.repeat(draws, shape[position] // blocks).reshape([-1 if axis == position else 1 for axis in range(len(shape))])
    return level


def bell_draw(stream_key, shape, scale, reach, pieces=(), held_as=jnp.bfloat16):
    array = jax.random.normal(stream_key, shape, jnp.float32) * scale
    if len(pieces) > 0:
        array = block_levels(stream_key, shape, pieces, -0.22, 0.18) * array
    return jnp.clip(array, min=-reach, max=reach).astype(held_as)


def setup_inputs(seed: int = 0, part: int = 0) -> dict:
    keys = jax.random.split(jax.random.key(seed), 4)
    own_keys = jax.random.split(jax.random.fold_in(keys[3], part), 4)
    return {
        "orbitals": bell_draw(own_keys[0], (ORBITALS, G), 1.0, 6.0, ((0, 128),)),
        "trial": bell_draw(own_keys[1], (ORBITALS, G), 1.0, 6.0, ((0, 128),)),
        "occupations": touch_ends((jax.random.randint(own_keys[2], (ORBITALS,), 0, 4) < 3).astype(jnp.int32), jax.random.fold_in(own_keys[2], 1), 0, 1),
    }


FRACTION = 0.25
OMEGA = 1.0

def cas_table(extent):
    indices = jnp.arange(extent, dtype=jnp.int32)
    products = indices[:, None] * indices[None, :] % extent
    phases = products.astype(jnp.float32) * (2.0 * math.pi / extent)
    return (jnp.cos(phases) + jnp.sin(phases)).astype(jnp.bfloat16)

def screened_kernel(extent):
    modes = jnp.arange(extent, dtype=jnp.int32)
    modes = jnp.where(2 * modes < extent, modes, modes - extent)
    wavenum = modes.astype(jnp.float32) * (2.0 * math.pi / extent)
    squares = wavenum * wavenum
    norm_sq = squares[:, None, None] + squares[None, :, None] + squares[None, None, :]
    bounded = jnp.where(norm_sq > 0, norm_sq, 1.0)
    screened = jnp.where(norm_sq > 0, 4.0 * math.pi / bounded * (1.0 - jnp.exp(-bounded / (4.0 * OMEGA * OMEGA))), math.pi / (OMEGA * OMEGA))
    return (screened / extent ** 3).reshape(-1)

def sweep(values, pattern, table):
    rounded = lax.optimization_barrier(values)
    return jnp.einsum(pattern, table.astype(jnp.float32), rounded.astype(jnp.float32), precision=lax.Precision.HIGHEST)

def screened_potential(density, table, kernel, extent):
    number = density.shape[0]
    values = density.reshape(number, extent, extent, extent)
    patterns = ('ga,pabc->pgbc', 'gb,pabc->pagc', 'gc,pabc->pabg')
    for pattern in patterns:
        values = sweep(values, pattern, table).astype(jnp.bfloat16)
    values = lax.optimization_barrier(values)
    values = (values.astype(jnp.float32) * kernel.reshape(extent, extent, extent)).astype(jnp.bfloat16)
    for ordinal, pattern in enumerate(patterns):
        values = sweep(values, pattern, table)
        if ordinal < 2:
            values = values.astype(jnp.bfloat16)
    return values.reshape(number, -1)

def reference(orbitals, trial, occupations):
    table = cas_table(NG)
    kernel = screened_kernel(NG)
    blocks = orbitals.reshape(N_BAND, ORB_DEV, G)
    fills = occupations.astype(jnp.float32).reshape(N_BAND, ORB_DEV)

    def one_block(block_index):
        own = lax.dynamic_index_in_dim(blocks, block_index, 0, keepdims=False)
        accumulated = jnp.zeros((ORB_DEV, G), jnp.float32)
        for offset in range(-SHIFTS, SHIFTS + 1):
            partner = ((block_index - offset) % N_BAND).astype(jnp.int32)
            visitors = lax.dynamic_index_in_dim(blocks, partner, 0, keepdims=False)
            partner_fill = lax.dynamic_index_in_dim(fills, partner, 0, keepdims=False)
            density = (own[:, None, :].astype(jnp.float32) * visitors[None, :, :].astype(jnp.float32)).astype(jnp.bfloat16)
            potential = screened_potential(density.reshape(ORB_DEV * ORB_DEV, G), table, kernel, NG).reshape(ORB_DEV, ORB_DEV, G)
            accumulated = accumulated + jnp.einsum('ijg,j,jg->ig', potential, partner_fill, visitors.astype(jnp.float32), precision=lax.Precision.HIGHEST)
        return (-FRACTION * accumulated).astype(jnp.bfloat16)
    exchange = lax.map(one_block, jnp.arange(N_BAND, dtype=jnp.int32)).reshape(ORBITALS, G)
    intersection = lax.dot_general(exchange, trial, (((1,), (1,)), ((), ())), preferred_element_type=jnp.float32) / math.sqrt(G)
    intersection_low = intersection.astype(jnp.bfloat16)
    projected = -(lax.dot_general(intersection_low, exchange, (((0,), (0,)), ((), ())), preferred_element_type=jnp.float32) / math.sqrt(ORBITALS))
    return (exchange, projected.astype(jnp.bfloat16))
```

```python
import functools
import math

import jax
import jax.numpy as jnp
import ml_dtypes
import numpy as np
from jax import lax
from jax.experimental import pallas as pl
from jax.experimental.pallas import tpu as pltpu
from jax.sharding import Mesh
from jax.sharding import PartitionSpec as P

NG = 64
G = NG**3
ROWS = G // 128
FRACTION = 0.25
OMEGA = 1.0
BAND = ("y", "x", "z", "core")
SPIN_BAND = ("spin",) + BAND
ORDER = np.concatenate([np.arange(0, NG, 2), np.arange(1, NG, 2)])
STEP = 4


def cas_table():
    indices = np.arange(NG)
    phases = (indices[:, None] * indices[None, :] % NG) * (2.0 * math.pi / NG)
    return (np.cos(phases) + np.sin(phases)).astype(np.float32).astype(ml_dtypes.bfloat16)


def screened_kernel():
    modes = np.arange(NG)
    modes = np.where(2 * modes < NG, modes, modes - NG)
    squares = (modes * (2.0 * math.pi / NG)) ** 2
    norm_sq = squares[:, None, None] + squares[None, :, None] + squares[None, None, :]
    bounded = np.where(norm_sq > 0, norm_sq, 1.0)
    screened = np.where(
        norm_sq > 0,
        4.0 * math.pi / bounded * (1.0 - np.exp(-bounded / (4.0 * OMEGA * OMEGA))),
        math.pi / (OMEGA * OMEGA),
    )
    return (screened / NG**3).astype(np.float32)


def constants():
    table = cas_table()
    mixed = table[ORDER][:, ORDER]
    blocks = np.kron(np.eye(4, dtype=np.float32), table.astype(np.float32)).astype(table.dtype)
    kernel = screened_kernel().transpose(1, 0, 2)[ORDER]
    return table, mixed, blocks, np.concatenate([kernel, kernel], axis=2)


def dot(left, right):
    return lax.dot_general(
        left, right, (((1,), (0,)), ((), ())), preferred_element_type=jnp.float32
    )


def exchange_body(
    own_ref, prev_ref, next_ref, fill_ref, table_ref, mixed_ref, blocks_ref, kernel_ref,
    out_ref, sides, middle, visitors, owner,
):
    lane = lax.broadcasted_iota(jnp.int32, (NG // 2, 128), 1)
    low = lane < 64
    low_wide = lax.broadcasted_iota(jnp.int32, (NG, 128), 1) < 64
    f32, bf16 = jnp.float32, jnp.bfloat16

    def forward(step, carry):
        for part in range(STEP):
            plane = step * STEP + part
            rows = pl.ds(pl.multiple_of(plane * 32, 32), 32)
            own, before, after = (
                ref[rows, :].astype(f32) for ref in (own_ref, prev_ref, next_ref)
            )
            own_turned, before_turned, after_turned = (
                pltpu.roll(value, 64, 1) for value in (own, before, after)
            )
            pairs = jnp.concatenate(
                [jnp.where(low, before, after_turned), jnp.where(low, before_turned, after)], axis=0
            )
            mine = jnp.concatenate(
                [jnp.where(low, own, own_turned), jnp.where(low, own_turned, own)], axis=0
            )
            wide = pl.ds(pl.multiple_of(plane * 64, 64), 64)
            visitors[wide, :] = pairs.astype(bf16)
            owner[wide, :] = mine.astype(bf16)
            density = jnp.concatenate([mine * pairs, mine * mine], axis=1).astype(bf16)
            values = dot(density, blocks_ref[...]).astype(bf16)
            values = dot(mixed_ref[...], values)
            sides[wide, :] = values[:, :128]
            middle[wide, :] = values[:, 128:]
        return carry

    lax.fori_loop(0, NG // STEP, forward, 0)

    def across(step, carry):
        for part in range(STEP):
            line = step * STEP + part
            rows = pl.ds(line, NG, stride=NG)
            values = jnp.concatenate([sides[rows, :], middle[rows, :]], axis=1).astype(bf16)
            values = dot(table_ref[...], values)
            kernel = kernel_ref[line]
            values = (values * jnp.concatenate([kernel, kernel], axis=1)).astype(bf16)
            values = dot(table_ref[...], values)
            sides[rows, :] = values[:, :128]
            middle[rows, :] = values[:, 128:]
        return carry

    lax.fori_loop(0, NG // STEP, across, 0)

    side_fill = jnp.where(low_wide, fill_ref[0], fill_ref[2])
    own_fill = jnp.where(low_wide, fill_ref[1], 0.0)

    def backward(step, carry):
        for part in range(STEP):
            plane = step * STEP + part
            wide = pl.ds(pl.multiple_of(plane * 64, 64), 64)
            values = jnp.concatenate([sides[wide, :], middle[wide, :]], axis=1).astype(bf16)
            values = dot(mixed_ref[...], values).astype(bf16)
            values = dot(values, blocks_ref[...])
            total = values[:, :128] * (visitors[wide, :].astype(f32) * side_fill)
            total = total + values[:, 128:] * (owner[wide, :].astype(f32) * own_fill)
            total = total + pltpu.roll(total, 64, 1)
            rows = pl.ds(pl.multiple_of(plane * 32, 32), 32)
            out_ref[rows, :] = jnp.where(low, total[:32], total[32:]).astype(bf16)
        return carry

    lax.fori_loop(0, NG // STEP, backward, 0)


def exchange_of(own, before, after, fills):
    table, mixed, blocks, kernel = (jnp.asarray(value) for value in constants())
    vmem = pl.BlockSpec(memory_space=pltpu.VMEM)
    return pl.pallas_call(
        exchange_body,
        out_shape=jax.ShapeDtypeStruct((ROWS, 128), jnp.bfloat16),
        in_specs=[vmem] * 3 + [pl.BlockSpec(memory_space=pltpu.SMEM)] + [vmem] * 4,
        out_specs=vmem,
        scratch_shapes=[
            pltpu.VMEM((NG * NG, 128), jnp.float32),
            pltpu.VMEM((NG * NG, 128), jnp.float32),
            pltpu.VMEM((NG * NG, 128), jnp.bfloat16),
            pltpu.VMEM((NG * NG, 128), jnp.bfloat16),
        ],
        compiler_params=pltpu.CompilerParams(vmem_limit_bytes=32 * 1024 * 1024),
        cost_estimate=pl.CostEstimate(
            flops=4 * 6 * 2 * G * NG, bytes_accessed=4 * 1024 * 1024, transcendentals=0
        ),
        name="exchange",
    )(own, before, after, fills, table, mixed, blocks, kernel)


def by_line_body(count, tiles_ref, out_ref, wide):
    wide[...] = tiles_ref[...].astype(jnp.float32)
    for line in range(16):
        rows = wide[pl.ds(line, count, stride=16), :]
        out_ref[pl.ds(line * count, count), :] = rows.astype(jnp.bfloat16)


def by_line(tiles):
    count = tiles.shape[0]
    vmem = pl.BlockSpec(memory_space=pltpu.VMEM)
    return pl.pallas_call(
        functools.partial(by_line_body, count),
        out_shape=jax.ShapeDtypeStruct((16 * count, 128), jnp.bfloat16),
        in_specs=[vmem],
        out_specs=vmem,
        scratch_shapes=[pltpu.VMEM((16 * count, 128), jnp.float32)],
        compiler_params=pltpu.CompilerParams(vmem_limit_bytes=16 * 1024 * 1024),
        cost_estimate=pl.CostEstimate(flops=0, bytes_accessed=2 * 1024 * 1024, transcendentals=0),
        name="by_line",
    )(tiles.reshape(16 * count, 128))


def intersection_body(tiles_ref, trial_ref, core_ref, lines_ref, mine_ref, other_ref, wide):
    by_line_body(128, tiles_ref, lines_ref, wide)
    total = jnp.zeros((128, 128), jnp.float32)
    for line in range(16):
        rows = pl.ds(line * 128, 128)
        total = total + lax.dot_general(
            trial_ref[rows, :], lines_ref[rows, :], (((1,), (1,)), ((), ())),
            preferred_element_type=jnp.float32,
        )
    total = total * (1.0 / math.sqrt(G))
    first = core_ref[0] == 0
    mine_ref[...] = jnp.where(first, total[:64], total[64:])
    other_ref[...] = jnp.where(first, total[64:], total[:64])


def intersection_of(tiles, trial_lines, core):
    vmem = pl.BlockSpec(memory_space=pltpu.VMEM)
    half = jax.ShapeDtypeStruct((64, 128), jnp.float32)
    return pl.pallas_call(
        intersection_body,
        out_shape=(jax.ShapeDtypeStruct((ROWS, 128), jnp.bfloat16), half, half),
        in_specs=[vmem, vmem, pl.BlockSpec(memory_space=pltpu.SMEM)],
        out_specs=(vmem, vmem, vmem),
        scratch_shapes=[pltpu.VMEM((ROWS, 128), jnp.float32)],
        compiler_params=pltpu.CompilerParams(vmem_limit_bytes=16 * 1024 * 1024),
        name="intersection",
    )(tiles.reshape(ROWS, 128), trial_lines, core)


def projected_body(lines_ref, mine_ref, other_ref, core_ref, out_ref):
    first = core_ref[0] == 0
    mine, other = mine_ref[...].astype(jnp.float32), other_ref[...].astype(jnp.float32)
    table = jnp.concatenate(
        [jnp.where(first, mine, other), jnp.where(first, other, mine)], axis=0
    ).astype(jnp.bfloat16)
    for line in range(16):
        rows = pl.ds(line * 128, 128)
        value = dot(table, lines_ref[rows, :]) * (-1.0 / math.sqrt(128))
        out_ref[:, rows] = value.astype(jnp.bfloat16)


def projected_of(lines, mine, other, core):
    vmem = pl.BlockSpec(memory_space=pltpu.VMEM)
    return pl.pallas_call(
        projected_body,
        out_shape=jax.ShapeDtypeStruct((128, ROWS), jnp.bfloat16),
        in_specs=[vmem, vmem, vmem, pl.BlockSpec(memory_space=pltpu.SMEM)],
        out_specs=vmem,
        compiler_params=pltpu.CompilerParams(vmem_limit_bytes=16 * 1024 * 1024),
        name="projected",
    )(lines, mine, other, core)


def passed_along(value, steps):
    count = lax.axis_size(BAND)
    return lax.ppermute(value, BAND, [(i, (i + steps) % count) for i in range(count)])


def swapped(value):
    return lax.ppermute(value, "core", [(0, 1), (1, 0)])


def summed_over(value, axes):
    peers = lax.axis_size(axes)
    copies = jnp.broadcast_to(value[None], (peers,) + value.shape)
    tiles = lax.all_to_all(copies, axes, 0, 0, tiled=True)
    return jnp.sum(tiles.astype(jnp.float32), axis=0).astype(jnp.bfloat16)


def to_slabs(rows):
    return lax.all_to_all(rows.reshape(128, 16, 128), BAND, 0, 0, tiled=True)


def local(orbitals, trial, occupations):
    own = orbitals.reshape(ROWS, 128)
    before, after = passed_along(own, 1), passed_along(own, -1)
    filled = occupations.astype(jnp.float32)
    fills = jnp.concatenate([passed_along(filled, 1), filled, passed_along(filled, -1)])
    trial_lines = by_line(to_slabs(trial.reshape(ROWS, 128)))
    exchange = exchange_of(own, before, after, -FRACTION * fills)
    core = lax.axis_index("core").astype(jnp.int32).reshape(1)
    lines, mine, other = intersection_of(to_slabs(exchange), trial_lines, core)
    half = (mine + swapped(other)).astype(jnp.bfloat16)
    half = summed_over(half, ("y", "x"))
    half = summed_over(half, "z")
    projected = projected_of(lines, half, swapped(half), core)
    return exchange.reshape(1, G), projected


def solution(mesh):
    finer = Mesh(mesh.devices.reshape(mesh.shape["spin"], 4, 2, 8, 2), SPIN_BAND)
    return jax.shard_map(
        local,
        mesh=finer,
        in_specs=(P(SPIN_BAND, None), P(SPIN_BAND, None), P(SPIN_BAND)),
        out_specs=(P(SPIN_BAND, None), P("spin", BAND)),
        check_vma=False,
    )
```

```python
import math

import jax
import jax.numpy as jnp
import ml_dtypes
import numpy as np
from jax import lax
from jax.experimental import pallas as pl
from jax.experimental.pallas import tpu as pltpu
from jax.sharding import Mesh
from jax.sharding import PartitionSpec as P

NG = 64
G = NG**3
ROWS = G // 128
FRACTION = 0.25
OMEGA = 1.0
BAND = ("y", "x", "z", "core")
SPIN_BAND = ("spin",) + BAND
ORDER = np.concatenate([np.arange(0, NG, 2), np.arange(1, NG, 2)])
STEP = 4
UNROLL = 8
PITCH = 72
EXCHANGE_FLOPS = 10**11
VMEM = pl.BlockSpec(memory_space=pltpu.VMEM)
SMEM = pl.BlockSpec(memory_space=pltpu.SMEM)


def cas_table():
    indices = np.arange(NG)
    phases = (indices[:, None] * indices[None, :] % NG) * (2.0 * math.pi / NG)
    return (np.cos(phases) + np.sin(phases)).astype(np.float32).astype(ml_dtypes.bfloat16)


def screened_kernel():
    modes = np.arange(NG)
    modes = np.where(2 * modes < NG, modes, modes - NG)
    squares = (modes * (2.0 * math.pi / NG)) ** 2
    norm_sq = squares[:, None, None] + squares[None, :, None] + squares[None, None, :]
    bounded = np.where(norm_sq > 0, norm_sq, 1.0)
    screened = np.where(
        norm_sq > 0,
        4.0 * math.pi / bounded * (1.0 - np.exp(-bounded / (4.0 * OMEGA * OMEGA))),
        math.pi / (OMEGA * OMEGA),
    )
    return (screened / NG**3).astype(np.float32)


def repeated(table):
    return np.kron(np.eye(STEP, dtype=np.float32), table.astype(np.float32)).astype(table.dtype)


def constants():
    table = cas_table()
    mixed = table[ORDER][:, ORDER]
    kernel = screened_kernel().transpose(1, 0, 2)[ORDER]
    return repeated(table), repeated(mixed), np.concatenate([kernel, kernel], axis=2)


def dot(left, right):
    return lax.dot_general(
        left, right, (((1,), (0,)), ((), ())), preferred_element_type=jnp.float32
    )


def pack_body(flat_ref, tiles_ref):
    def part(step, carry):
        columns = pl.ds(pl.multiple_of(step * 16384, 16384), 16384)
        rows = pl.ds(pl.multiple_of(step * 128, 128), 128)
        tiles_ref[rows, :] = flat_ref[0:1, columns].reshape(128, 128)
        return carry

    lax.fori_loop(0, 16, part, 0)


def unpack_body(tiles_ref, flat_ref):
    def part(step, carry):
        columns = pl.ds(pl.multiple_of(step * 16384, 16384), 16384)
        rows = pl.ds(pl.multiple_of(step * 128, 128), 128)
        value = tiles_ref[rows, :].astype(jnp.float32).reshape(1, 16384)
        flat_ref[0:1, columns] = value.astype(jnp.bfloat16)
        return carry

    lax.fori_loop(0, 16, part, 0)


def pack_flagged_body(flat_ref, flag_ref, tiles_ref):
    pack_body(flat_ref, tiles_ref)
    flag = jnp.full((16, 128), flag_ref[0], jnp.int32)
    tiles_ref[pl.ds(ROWS, 16), :] = flag.astype(jnp.float32).astype(jnp.bfloat16)


def pack_after_body(flat_ref, earlier_ref, tiles_ref):
    pack_body(flat_ref, tiles_ref)


def packed_after(flat, earlier):
    return pl.pallas_call(
        pack_after_body,
        out_shape=jax.ShapeDtypeStruct((ROWS, 128), jnp.bfloat16),
        in_specs=[VMEM, pl.BlockSpec(memory_space=pl.ANY)],
        out_specs=VMEM,
        compiler_params=pltpu.CompilerParams(vmem_limit_bytes=16 * 1024 * 1024),
        name="pack",
    )(flat, earlier)


def packed_with_flag(flat, flag):
    return pl.pallas_call(
        pack_flagged_body,
        out_shape=jax.ShapeDtypeStruct((ROWS + 16, 128), jnp.bfloat16),
        in_specs=[VMEM, SMEM],
        out_specs=VMEM,
        compiler_params=pltpu.CompilerParams(vmem_limit_bytes=16 * 1024 * 1024),
        name="pack_flagged",
    )(flat, flag)


def exchange_body(
    own_ref, prev_ref, next_ref, table_ref, mixed_ref, kernel_ref,
    out_ref, sides, middle, visitors, owner,
):
    f32, bf16 = jnp.float32, jnp.bfloat16
    low = lax.broadcasted_iota(jnp.int32, (NG // 2, 128), 1) < 64
    low_wide = lax.broadcasted_iota(jnp.int32, (NG, 128), 1) < 64

    def across_rows(plane):
        return pl.ds(pl.multiple_of(plane * PITCH, 8), NG)

    def forward(step, carry):
        densities = []
        for part in range(STEP):
            plane = step * STEP + part
            rows = pl.ds(pl.multiple_of(plane * 32, 32), 32)
            own, before, after = (
                ref[rows, :].astype(f32) for ref in (own_ref, prev_ref, next_ref)
            )
            own_turned, before_turned, after_turned = (
                pltpu.roll(value, 64, 1) for value in (own, before, after)
            )
            pairs = jnp.concatenate(
                [jnp.where(low, before, after_turned), jnp.where(low, before_turned, after)], axis=0
            )
            mine = jnp.concatenate(
                [jnp.where(low, own, own_turned), jnp.where(low, own_turned, own)], axis=0
            )
            wide = pl.ds(pl.multiple_of(plane * 64, 64), 64)
            visitors[wide, :] = pairs.astype(bf16)
            owner[wide, :] = mine.astype(bf16)
            densities.append(jnp.concatenate([mine * pairs, mine * mine], axis=1).astype(bf16))
        values = dot(jnp.concatenate(densities, axis=0), table_ref[...]).astype(bf16)
        values = dot(mixed_ref[...], values)
        for part in range(STEP):
            rows = across_rows(step * STEP + part)
            sides[rows, :] = values[part * 64 : part * 64 + 64, :128]
            middle[rows, :] = values[part * 64 : part * 64 + 64, 128:]
        return carry

    lax.fori_loop(0, NG // STEP, forward, 0, unroll=UNROLL)

    def across(step, carry):
        lines = [pl.ds(step * STEP + part, NG, stride=PITCH) for part in range(STEP)]
        values = jnp.concatenate(
            [jnp.concatenate([sides[rows, :], middle[rows, :]], axis=1) for rows in lines], axis=0
        ).astype(bf16)
        values = dot(table_ref[...], values)
        kernel = jnp.concatenate([kernel_ref[step * STEP + part] for part in range(STEP)], axis=0)
        values = (values * jnp.concatenate([kernel, kernel], axis=1)).astype(bf16)
        values = dot(table_ref[...], values)
        for part, rows in enumerate(lines):
            sides[rows, :] = values[part * 64 : part * 64 + 64, :128]
            middle[rows, :] = values[part * 64 : part * 64 + 64, 128:]
        return carry

    lax.fori_loop(0, NG // STEP, across, 0, unroll=UNROLL)

    own_fill, prev_fill, next_fill = (
        ref[pl.ds(ROWS, 16), :].astype(f32)[:1] * -FRACTION
        for ref in (own_ref, prev_ref, next_ref)
    )
    side_fill = jnp.where(low_wide, prev_fill, next_fill)
    own_fill = jnp.where(low_wide, own_fill, 0.0)

    def backward(step, carry):
        planes = [step * STEP + part for part in range(STEP)]
        values = jnp.concatenate(
            [
                jnp.concatenate(
                    [sides[across_rows(plane), :], middle[across_rows(plane), :]], axis=1
                )
                for plane in planes
            ],
            axis=0,
        ).astype(bf16)
        values = dot(mixed_ref[...], values).astype(bf16)
        values = dot(values, table_ref[...])
        for part, plane in enumerate(planes):
            wide = pl.ds(pl.multiple_of(plane * 64, 64), 64)
            potential = values[part * 64 : part * 64 + 64]
            total = potential[:, :128] * (visitors[wide, :].astype(f32) * side_fill)
            total = total + potential[:, 128:] * (owner[wide, :].astype(f32) * own_fill)
            total = total + pltpu.roll(total, 64, 1)
            rows = pl.ds(pl.multiple_of(plane * 32, 32), 32)
            out_ref[rows, :] = jnp.where(low, total[:32], total[32:]).astype(bf16)
        return carry

    lax.fori_loop(0, NG // STEP, backward, 0, unroll=UNROLL)


def exchange_of(own, before, after):
    table, mixed, kernel = (jnp.asarray(value) for value in constants())
    return pl.pallas_call(
        exchange_body,
        out_shape=jax.ShapeDtypeStruct((ROWS, 128), jnp.bfloat16),
        in_specs=[VMEM] * 6,
        out_specs=VMEM,
        scratch_shapes=[
            pltpu.VMEM((NG * PITCH, 128), jnp.float32),
            pltpu.VMEM((NG * PITCH, 128), jnp.float32),
            pltpu.VMEM((NG * NG, 128), jnp.bfloat16),
            pltpu.VMEM((NG * NG, 128), jnp.bfloat16),
        ],
        compiler_params=pltpu.CompilerParams(vmem_limit_bytes=32 * 1024 * 1024),
        cost_estimate=pl.CostEstimate(
            flops=EXCHANGE_FLOPS, bytes_accessed=4 * 1024 * 1024, transcendentals=0
        ),
        name="exchange",
    )(own, before, after, table, mixed, kernel)


def by_line_body(tiles_ref, out_ref, wide):
    wide[...] = tiles_ref[...].astype(jnp.float32)
    for line in range(16):
        rows = wide[pl.ds(line, 128, stride=16), :]
        out_ref[pl.ds(line * 128, 128), :] = rows.astype(jnp.bfloat16)


def aside_body(tiles_ref, exchange_ref, lines_ref, flat_ref, wide):
    by_line_body(tiles_ref, lines_ref, wide)
    unpack_body(exchange_ref, flat_ref)


def beside_slabs(tiles, exchange):
    return pl.pallas_call(
        aside_body,
        out_shape=(
            jax.ShapeDtypeStruct((ROWS, 128), jnp.bfloat16),
            jax.ShapeDtypeStruct((1, G), jnp.bfloat16),
        ),
        in_specs=[VMEM, VMEM],
        out_specs=(VMEM, VMEM),
        scratch_shapes=[pltpu.VMEM((ROWS, 128), jnp.float32)],
        compiler_params=pltpu.CompilerParams(vmem_limit_bytes=16 * 1024 * 1024),
        name="beside_slabs",
    )(tiles.reshape(ROWS, 128), exchange)


def intersection_body(tiles_ref, trial_ref, core_ref, lines_ref, mine_ref, other_ref, wide):
    by_line_body(tiles_ref, lines_ref, wide)
    total = jnp.zeros((128, 128), jnp.float32)
    for line in range(16):
        rows = pl.ds(line * 128, 128)
        total = total + lax.dot_general(
            trial_ref[rows, :], lines_ref[rows, :], (((1,), (1,)), ((), ())),
            preferred_element_type=jnp.float32,
        )
    total = total * (1.0 / math.sqrt(G))
    first = core_ref[0] == 0
    mine_ref[...] = jnp.where(first, total[:64], total[64:])
    other_ref[...] = jnp.where(first, total[64:], total[:64])


def intersection_of(tiles, trial_lines, core):
    half = jax.ShapeDtypeStruct((64, 128), jnp.float32)
    return pl.pallas_call(
        intersection_body,
        out_shape=(jax.ShapeDtypeStruct((ROWS, 128), jnp.bfloat16), half, half),
        in_specs=[VMEM, VMEM, SMEM],
        out_specs=(VMEM, VMEM, VMEM),
        scratch_shapes=[pltpu.VMEM((ROWS, 128), jnp.float32)],
        compiler_params=pltpu.CompilerParams(vmem_limit_bytes=16 * 1024 * 1024),
        name="intersection",
    )(tiles.reshape(ROWS, 128), trial_lines, core)


def projected_body(lines_ref, mine_ref, other_ref, core_ref, out_ref):
    first = core_ref[0] == 0
    mine, other = mine_ref[...].astype(jnp.float32), other_ref[...].astype(jnp.float32)
    table = jnp.concatenate(
        [jnp.where(first, mine, other), jnp.where(first, other, mine)], axis=0
    ).astype(jnp.bfloat16)
    for line in range(16):
        rows = pl.ds(line * 128, 128)
        value = dot(table, lines_ref[rows, :]) * (-1.0 / math.sqrt(128))
        out_ref[:, rows] = value.astype(jnp.bfloat16)


def projected_of(lines, mine, other, core):
    return pl.pallas_call(
        projected_body,
        out_shape=jax.ShapeDtypeStruct((128, ROWS), jnp.bfloat16),
        in_specs=[VMEM, VMEM, VMEM, SMEM],
        out_specs=VMEM,
        compiler_params=pltpu.CompilerParams(vmem_limit_bytes=16 * 1024 * 1024),
        name="projected",
    )(lines, mine, other, core)


def passed_along(value, steps):
    count = lax.axis_size(BAND)
    return lax.ppermute(value, BAND, [(i, (i + steps) % count) for i in range(count)])


def swapped(value):
    return lax.ppermute(value, "core", [(0, 1), (1, 0)])


def summed_over(value, axes):
    peers = lax.axis_size(axes)
    copies = jnp.broadcast_to(value[None], (peers,) + value.shape)
    tiles = lax.all_to_all(copies, axes, 0, 0, tiled=True)
    return jnp.sum(tiles.astype(jnp.float32), axis=0).astype(jnp.bfloat16)


def to_slabs(rows):
    return lax.all_to_all(rows.reshape(128, 16, 128), BAND, 0, 0, tiled=True)


def local(orbitals, trial, occupations):
    own = packed_with_flag(orbitals, occupations)
    before, after = passed_along(own, 1), passed_along(own, -1)
    trial_tiles = to_slabs(packed_after(trial, own))
    exchange = exchange_of(own, before, after)
    exchange_tiles = to_slabs(exchange)
    trial_lines, flat = beside_slabs(trial_tiles, exchange)
    core = lax.axis_index("core").astype(jnp.int32).reshape(1)
    lines, mine, other = intersection_of(exchange_tiles, trial_lines, core)
    half = (mine + swapped(other)).astype(jnp.bfloat16)
    half = summed_over(half, ("y", "x"))
    half = summed_over(half, "z")
    projected = projected_of(lines, half, swapped(half), core)
    return flat, projected


def solution(mesh):
    finer = Mesh(mesh.devices.reshape(mesh.shape["spin"], 4, 2, 8, 2), SPIN_BAND)
    return jax.shard_map(
        local,
        mesh=finer,
        in_specs=(P(SPIN_BAND, None), P(SPIN_BAND, None), P(SPIN_BAND)),
        out_specs=(P(SPIN_BAND, None), P("spin", BAND)),
        check_vma=False,
    )
```

```python
import math

import jax
import jax.numpy as jnp
import ml_dtypes
import numpy as np
from jax import lax
from jax.experimental import pallas as pl
from jax.experimental.pallas import tpu as pltpu
from jax.sharding import Mesh
from jax.sharding import PartitionSpec as P

NG = 64
G = NG**3
ROWS = G // 128
FRACTION = 0.25
OMEGA = 1.0
BAND = ("y", "x", "z", "core")
SPIN_BAND = ("spin",) + BAND
ORDER = np.concatenate([np.arange(0, NG, 2), np.arange(1, NG, 2)])
STEP = 4
SPAN = 2 * STEP
PITCH = 72
OWN_FLOPS = 10**10
VMEM = pl.BlockSpec(memory_space=pltpu.VMEM)
SMEM = pl.BlockSpec(memory_space=pltpu.SMEM)


def cas_table():
    indices = np.arange(NG)
    phases = (indices[:, None] * indices[None, :] % NG) * (2.0 * math.pi / NG)
    return (np.cos(phases) + np.sin(phases)).astype(np.float32).astype(ml_dtypes.bfloat16)


def screened_kernel():
    modes = np.arange(NG)
    modes = np.where(2 * modes < NG, modes, modes - NG)
    squares = (modes * (2.0 * math.pi / NG)) ** 2
    norm_sq = squares[:, None, None] + squares[None, :, None] + squares[None, None, :]
    bounded = np.where(norm_sq > 0, norm_sq, 1.0)
    screened = np.where(
        norm_sq > 0,
        4.0 * math.pi / bounded * (1.0 - np.exp(-bounded / (4.0 * OMEGA * OMEGA))),
        math.pi / (OMEGA * OMEGA),
    )
    return (screened / NG**3).astype(np.float32)


def repeated(table):
    return np.kron(np.eye(STEP, dtype=np.float32), table.astype(np.float32)).astype(table.dtype)


def constants():
    table = cas_table()
    mixed = table[ORDER][:, ORDER]
    kernel = screened_kernel().transpose(1, 0, 2)[ORDER]
    return repeated(table), repeated(mixed), np.concatenate([kernel, kernel], axis=2)


def dot(left, right):
    return lax.dot_general(
        left, right, (((1,), (0,)), ((), ())), preferred_element_type=jnp.float32
    )


def pack_body(flat_ref, tiles_ref):
    def part(step, carry):
        columns = pl.ds(pl.multiple_of(step * 16384, 16384), 16384)
        rows = pl.ds(pl.multiple_of(step * 128, 128), 128)
        tiles_ref[rows, :] = flat_ref[0:1, columns].reshape(128, 128)
        return carry

    lax.fori_loop(0, 16, part, 0)


def pack_flagged_body(flat_ref, flag_ref, tiles_ref):
    pack_body(flat_ref, tiles_ref)
    flag = jnp.full((16, 128), flag_ref[0], jnp.int32)
    tiles_ref[pl.ds(ROWS, 16), :] = flag.astype(jnp.float32).astype(jnp.bfloat16)


def pack_after_body(flat_ref, earlier_ref, tiles_ref):
    pack_body(flat_ref, tiles_ref)


def packed_after(flat, earlier):
    return pl.pallas_call(
        pack_after_body,
        out_shape=jax.ShapeDtypeStruct((ROWS, 128), jnp.bfloat16),
        in_specs=[VMEM, pl.BlockSpec(memory_space=pl.ANY)],
        out_specs=VMEM,
        compiler_params=pltpu.CompilerParams(vmem_limit_bytes=16 * 1024 * 1024),
        name="pack",
    )(flat, earlier)


def packed_with_flag(flat, flag):
    return pl.pallas_call(
        pack_flagged_body,
        out_shape=jax.ShapeDtypeStruct((ROWS + 16, 128), jnp.bfloat16),
        in_specs=[VMEM, SMEM],
        out_specs=VMEM,
        compiler_params=pltpu.CompilerParams(vmem_limit_bytes=16 * 1024 * 1024),
        name="pack_flagged",
    )(flat, flag)


def plane_rows(plane, height):
    return pl.ds(pl.multiple_of(plane * height, height), height)


def passes_there(density_of, table_ref, mixed_ref, kernel_ref, grid):
    bf16 = jnp.bfloat16

    def pitched(plane):
        return pl.ds(pl.multiple_of(plane * PITCH, 8), NG)

    def beside(parts):
        return jnp.concatenate(
            [jnp.concatenate(parts[:STEP], axis=0), jnp.concatenate(parts[STEP:], axis=0)], axis=1
        )

    def part_of(values, part):
        rows = slice(part % STEP * NG, part % STEP * NG + NG)
        return values[rows, :128] if part < STEP else values[rows, 128:]

    def forward(step, carry):
        planes = [step * SPAN + part for part in range(SPAN)]
        values = beside([density_of(plane) for plane in planes])
        values = dot(values, table_ref[...]).astype(bf16)
        values = dot(mixed_ref[...], values)
        for part, plane in enumerate(planes):
            grid[pitched(plane), :] = part_of(values, part)
        return carry

    lax.fori_loop(0, NG // SPAN, forward, 0, unroll=True)

    def across(step, carry):
        lines = [step * SPAN + part for part in range(SPAN)]
        rows = [pl.ds(line, NG, stride=PITCH) for line in lines]
        values = beside([grid[row, :].astype(bf16) for row in rows])
        values = dot(table_ref[...], values)
        values = (values * beside([kernel_ref[line] for line in lines])).astype(bf16)
        values = dot(table_ref[...], values)
        for part, row in enumerate(rows):
            grid[row, :] = part_of(values, part)
        return carry

    lax.fori_loop(0, NG // SPAN, across, 0, unroll=True)

    def potentials(step):
        planes = [step * SPAN + part for part in range(SPAN)]
        values = beside([grid[pitched(plane), :].astype(bf16) for plane in planes])
        values = dot(mixed_ref[...], values).astype(bf16)
        values = dot(values, table_ref[...])
        return [(plane, part_of(values, part)) for part, plane in enumerate(planes)]

    return potentials


def fill_of(ref):
    return ref[pl.ds(ROWS, 16), :].astype(jnp.float32)[:1] * -FRACTION


def both_halves(value, low):
    turned = pltpu.roll(value, 64, 1)
    return jnp.concatenate([jnp.where(low, value, turned), jnp.where(low, turned, value)], axis=0)


def low_lanes(height):
    return lax.broadcasted_iota(jnp.int32, (height, 128), 1) < 64


def own_body(own_ref, table_ref, mixed_ref, kernel_ref, owner_ref, term_ref, grid):
    f32, bf16 = jnp.float32, jnp.bfloat16
    low = low_lanes(NG // 2)

    def density_of(plane):
        mine = both_halves(own_ref[plane_rows(plane, 32), :].astype(f32), low)
        owner_ref[plane_rows(plane, 64), :] = mine.astype(bf16)
        return (mine * mine).astype(bf16)

    potentials = passes_there(density_of, table_ref, mixed_ref, kernel_ref, grid)
    fill = fill_of(own_ref)

    def backward(step, carry):
        for plane, potential in potentials(step):
            total = potential * (owner_ref[plane_rows(plane, 64), :].astype(f32) * fill)
            term_ref[plane_rows(plane, 32), :] = jnp.where(low, total[:32], total[32:])
        return carry

    lax.fori_loop(0, NG // SPAN, backward, 0, unroll=True)


def own_term(own, table, mixed, kernel):
    return pl.pallas_call(
        own_body,
        out_shape=(
            jax.ShapeDtypeStruct((NG * NG, 128), jnp.bfloat16),
            jax.ShapeDtypeStruct((ROWS, 128), jnp.float32),
        ),
        in_specs=[VMEM] * 4,
        out_specs=(VMEM, VMEM),
        scratch_shapes=[pltpu.VMEM((NG * PITCH, 128), jnp.float32)],
        compiler_params=pltpu.CompilerParams(vmem_limit_bytes=24 * 1024 * 1024),
        cost_estimate=pl.CostEstimate(
            flops=OWN_FLOPS, bytes_accessed=4 * 1024 * 1024, transcendentals=0
        ),
        name="own_term",
    )(own, table, mixed, kernel)


def exchange_body(
    prev_ref, next_ref, owner_ref, term_ref, trial_ref, table_ref, mixed_ref, kernel_ref,
    out_ref, visitors, grid,
):
    f32, bf16 = jnp.float32, jnp.bfloat16
    low = low_lanes(NG // 2)

    def density_of(plane):
        before, after = (ref[plane_rows(plane, 32), :].astype(f32) for ref in (prev_ref, next_ref))
        before_turned, after_turned = (pltpu.roll(value, 64, 1) for value in (before, after))
        pairs = jnp.concatenate(
            [jnp.where(low, before, after_turned), jnp.where(low, before_turned, after)], axis=0
        )
        wide = plane_rows(plane, 64)
        visitors[wide, :] = pairs.astype(bf16)
        return (pairs * owner_ref[wide, :].astype(f32)).astype(bf16)

    potentials = passes_there(density_of, table_ref, mixed_ref, kernel_ref, grid)
    fill = jnp.where(low_lanes(NG), fill_of(prev_ref), fill_of(next_ref))

    def backward(step, carry):
        for plane, potential in potentials(step):
            total = potential * (visitors[plane_rows(plane, 64), :].astype(f32) * fill)
            total = total + pltpu.roll(total, 64, 1)
            rows = plane_rows(plane, 32)
            value = (jnp.where(low, total[:32], total[32:]) + term_ref[rows, :]).astype(bf16)
            trial = trial_ref[rows, :]
            out_ref[plane_rows(plane, 64), :] = jnp.concatenate(
                [trial[:16], value[:16], trial[16:], value[16:]], axis=0
            )
        return carry

    lax.fori_loop(0, NG // SPAN, backward, 0, unroll=True)


def exchange_of(before, after, owner, term, trial, table, mixed, kernel):
    return pl.pallas_call(
        exchange_body,
        out_shape=jax.ShapeDtypeStruct((2 * ROWS, 128), jnp.bfloat16),
        in_specs=[VMEM] * 8,
        out_specs=VMEM,
        scratch_shapes=[
            pltpu.VMEM((NG * NG, 128), jnp.bfloat16),
            pltpu.VMEM((NG * PITCH, 128), jnp.float32),
        ],
        compiler_params=pltpu.CompilerParams(vmem_limit_bytes=24 * 1024 * 1024),
        name="exchange",
    )(before, after, owner, term, trial, table, mixed, kernel)


def unpack_body(tiles_ref, flat_ref, token_ref):
    def part(step, carry):
        columns = pl.ds(pl.multiple_of(step * 16384, 16384), 16384)
        tiles = [tiles_ref[pl.ds(step * 256 + peer * 32 + 16, 16), :] for peer in range(8)]
        value = jnp.concatenate(tiles, axis=0).astype(jnp.float32).reshape(1, 16384)
        flat_ref[0:1, columns] = value.astype(jnp.bfloat16)
        return carry

    lax.fori_loop(0, 16, part, 0)
    token_ref[...] = tiles_ref[pl.ds(0, 16), :]


def unpacked(tiles):
    return pl.pallas_call(
        unpack_body,
        out_shape=(
            jax.ShapeDtypeStruct((1, G), jnp.bfloat16),
            jax.ShapeDtypeStruct((16, 128), jnp.bfloat16),
        ),
        in_specs=[VMEM],
        out_specs=(VMEM, VMEM),
        compiler_params=pltpu.CompilerParams(vmem_limit_bytes=16 * 1024 * 1024),
        name="unpack",
    )(tiles)


def intersection_body(tiles_ref, token_ref, lines_ref, copies_ref, wide):
    bf16 = jnp.bfloat16
    wide[...] = tiles_ref[...].astype(jnp.float32)
    total = jnp.zeros((128, 128), jnp.float32)
    for line in range(16):
        trial = wide[pl.ds(line, 128, stride=32), :].astype(bf16)
        value = wide[pl.ds(line + 16, 128, stride=32), :].astype(bf16)
        lines_ref[pl.ds(line * 128, 128), :] = value
        total = total + lax.dot_general(
            trial, value, (((1,), (1,)), ((), ())), preferred_element_type=jnp.float32
        )
    total = (total * (1.0 / math.sqrt(G))).astype(bf16)
    for peer in range(8):
        copies_ref[pl.ds(peer * 128, 128), :] = total


def intersection_of(tiles, token):
    return pl.pallas_call(
        intersection_body,
        out_shape=(
            jax.ShapeDtypeStruct((ROWS, 128), jnp.bfloat16),
            jax.ShapeDtypeStruct((8 * 128, 128), jnp.bfloat16),
        ),
        in_specs=[VMEM, pl.BlockSpec(memory_space=pl.ANY)],
        out_specs=(VMEM, VMEM),
        scratch_shapes=[pltpu.VMEM((2 * ROWS, 128), jnp.float32)],
        compiler_params=pltpu.CompilerParams(vmem_limit_bytes=16 * 1024 * 1024),
        name="intersection",
    )(tiles, token)


def summed_copies_body(tiles_ref, copies_ref):
    total = tiles_ref[0].astype(jnp.float32)
    for peer in range(1, 16):
        total = total + tiles_ref[peer].astype(jnp.float32)
    total = total.astype(jnp.bfloat16)
    for peer in range(16):
        copies_ref[peer] = total


def summed_copies(tiles):
    return pl.pallas_call(
        summed_copies_body,
        out_shape=jax.ShapeDtypeStruct((16, 64, 128), jnp.bfloat16),
        in_specs=[VMEM],
        out_specs=VMEM,
        compiler_params=pltpu.CompilerParams(vmem_limit_bytes=16 * 1024 * 1024),
        name="summed_copies",
    )(tiles)


def projected_body(lines_ref, tiles_ref, out_ref):
    halves = []
    for core in range(2):
        total = tiles_ref[core].astype(jnp.float32)
        for peer in range(1, 8):
            total = total + tiles_ref[2 * peer + core].astype(jnp.float32)
        halves.append(total)
    table = jnp.concatenate(halves, axis=0).astype(jnp.bfloat16)
    for line in range(16):
        rows = pl.ds(line * 128, 128)
        value = dot(table, lines_ref[rows, :]) * (-1.0 / math.sqrt(128))
        out_ref[:, rows] = value.astype(jnp.bfloat16)


def projected_of(lines, tiles):
    return pl.pallas_call(
        projected_body,
        out_shape=jax.ShapeDtypeStruct((128, ROWS), jnp.bfloat16),
        in_specs=[VMEM, VMEM],
        out_specs=VMEM,
        compiler_params=pltpu.CompilerParams(vmem_limit_bytes=16 * 1024 * 1024),
        name="projected",
    )(lines, tiles)


def passed_along(value, steps):
    count = lax.axis_size(BAND)
    return lax.ppermute(value, BAND, [(i, (i + steps) % count) for i in range(count)])


def sent_around(tiles, axes):
    return lax.all_to_all(tiles, axes, 0, 0, tiled=True)


def local(orbitals, trial, occupations):
    tables = [jnp.asarray(value) for value in constants()]
    own = packed_with_flag(orbitals, occupations)
    before, after = passed_along(own, 1), passed_along(own, -1)
    trial_rows = packed_after(trial, own)
    owner, term = own_term(own, *tables)
    both = exchange_of(before, after, owner, term, trial_rows, *tables)
    tiles = sent_around(both.reshape(128, 32, 128), BAND).reshape(2 * ROWS, 128)
    flat, token = unpacked(both)
    lines, copies = intersection_of(tiles, token)
    parts = sent_around(copies.reshape(16, 64, 128), ("y", "x", "core"))
    parts = sent_around(summed_copies(parts), ("z", "core"))
    return flat, projected_of(lines, parts)


def solution(mesh):
    finer = Mesh(mesh.devices.reshape(mesh.shape["spin"], 4, 2, 8, 2), SPIN_BAND)
    return jax.shard_map(
        local,
        mesh=finer,
        in_specs=(P(SPIN_BAND, None), P(SPIN_BAND, None), P(SPIN_BAND)),
        out_specs=(P(SPIN_BAND, None), P("spin", BAND)),
        check_vma=False,
    )
```

```python
import math

import jax
import jax.numpy as jnp
import ml_dtypes
import numpy as np
from jax import lax
from jax.experimental import pallas as pl
from jax.experimental.pallas import tpu as pltpu
from jax.sharding import Mesh
from jax.sharding import PartitionSpec as P

NG = 64
G = NG**3
ROWS = G // 128
FRACTION = 0.25
OMEGA = 1.0
BAND = ("y", "x", "z", "core")
SPIN_BAND = ("spin",) + BAND
ORDER = np.concatenate([np.arange(0, NG, 2), np.arange(1, NG, 2)])
STEP = 4
SPAN = 2 * STEP
PITCH = 72
PARTS = 8
EXCHANGE_FLOPS = 10**11
VMEM = pl.BlockSpec(memory_space=pltpu.VMEM)
SMEM = pl.BlockSpec(memory_space=pltpu.SMEM)


def cas_table():
    indices = np.arange(NG)
    phases = (indices[:, None] * indices[None, :] % NG) * (2.0 * math.pi / NG)
    return (np.cos(phases) + np.sin(phases)).astype(np.float32).astype(ml_dtypes.bfloat16)


def screened_kernel():
    modes = np.arange(NG)
    modes = np.where(2 * modes < NG, modes, modes - NG)
    squares = (modes * (2.0 * math.pi / NG)) ** 2
    norm_sq = squares[:, None, None] + squares[None, :, None] + squares[None, None, :]
    bounded = np.where(norm_sq > 0, norm_sq, 1.0)
    screened = np.where(
        norm_sq > 0,
        4.0 * math.pi / bounded * (1.0 - np.exp(-bounded / (4.0 * OMEGA * OMEGA))),
        math.pi / (OMEGA * OMEGA),
    )
    return (screened / NG**3).astype(np.float32)


def repeated(table):
    return np.kron(np.eye(STEP, dtype=np.float32), table.astype(np.float32)).astype(table.dtype)


def constants():
    table = cas_table()
    mixed = table[ORDER][:, ORDER]
    kernel = screened_kernel().transpose(1, 0, 2)[ORDER]
    return repeated(table), repeated(mixed), np.concatenate([kernel, kernel], axis=2)


def dot(left, right):
    return lax.dot_general(
        left, right, (((1,), (0,)), ((), ())), preferred_element_type=jnp.float32
    )


def pack_body(
    own_hbm, trial_hbm, flag_ref, own_out, trial_out,
    own_flat, trial_flat, own_tiles, trial_tiles, arrived, left, flag_left,
):
    width, height = G // PARTS, ROWS // PARTS

    def copy_in(source, flat, which, part):
        columns = pl.ds(part * width, width)
        return pltpu.make_async_copy(
            source.at[:, columns], flat.at[:, columns], arrived.at[which, part]
        )

    def copy_out(tiles, target, which, part):
        rows = pl.ds(part * height, height)
        return pltpu.make_async_copy(tiles.at[rows, :], target.at[rows, :], left.at[which, part])

    arrays = (
        (own_hbm, own_flat, own_tiles, own_out),
        (trial_hbm, trial_flat, trial_tiles, trial_out),
    )
    for which, (source, flat, _, _) in enumerate(arrays):
        for part in range(PARTS):
            copy_in(source, flat, which, part).start()
    flag = jnp.full((16, 128), flag_ref[0], jnp.int32)
    last = pl.ds(ROWS, 16)
    own_tiles[last, :] = flag.astype(jnp.float32).astype(jnp.bfloat16)
    flag_copy = pltpu.make_async_copy(own_tiles.at[last, :], own_out.at[last, :], flag_left)
    flag_copy.start()
    for which, (source, flat, tiles, target) in enumerate(arrays):
        for part in range(PARTS):
            copy_in(source, flat, which, part).wait()
            value = flat[0:1, pl.ds(part * width, width)].reshape(height, 128)
            tiles[pl.ds(part * height, height), :] = value
            copy_out(tiles, target, which, part).start()
    flag_copy.wait()
    for which, (_, _, tiles, target) in enumerate(arrays):
        for part in range(PARTS):
            copy_out(tiles, target, which, part).wait()


def packed(orbitals, trial, occupations):
    anywhere = pl.BlockSpec(memory_space=pltpu.HBM)
    own = jax.ShapeDtypeStruct((ROWS + 16, 128), jnp.bfloat16)
    other = jax.ShapeDtypeStruct((ROWS, 128), jnp.bfloat16)
    return pl.pallas_call(
        pack_body,
        out_shape=(own, other),
        in_specs=[anywhere, anywhere, SMEM],
        out_specs=(anywhere, anywhere),
        scratch_shapes=[
            pltpu.VMEM((1, G), jnp.bfloat16),
            pltpu.VMEM((1, G), jnp.bfloat16),
            pltpu.VMEM(own.shape, jnp.bfloat16),
            pltpu.VMEM(other.shape, jnp.bfloat16),
            pltpu.SemaphoreType.DMA((2, PARTS)),
            pltpu.SemaphoreType.DMA((2, PARTS)),
            pltpu.SemaphoreType.DMA,
        ],
        compiler_params=pltpu.CompilerParams(vmem_limit_bytes=58 * 1024 * 1024),
        name="pack",
    )(orbitals, trial, occupations)


def plane_rows(plane, height):
    return pl.ds(pl.multiple_of(plane * height, height), height)


def passes_there(density_of, table_ref, mixed_ref, kernel_ref, grid):
    bf16 = jnp.bfloat16

    def pitched(plane):
        return pl.ds(pl.multiple_of(plane * PITCH, 8), NG)

    def beside(parts):
        return jnp.concatenate(
            [jnp.concatenate(parts[:STEP], axis=0), jnp.concatenate(parts[STEP:], axis=0)], axis=1
        )

    def part_of(values, part):
        rows = slice(part % STEP * NG, part % STEP * NG + NG)
        return values[rows, :128] if part < STEP else values[rows, 128:]

    def forward(step, carry):
        planes = [step * SPAN + part for part in range(SPAN)]
        values = beside([density_of(plane) for plane in planes])
        values = dot(values, table_ref[...]).astype(bf16)
        values = dot(mixed_ref[...], values)
        for part, plane in enumerate(planes):
            grid[pitched(plane), :] = part_of(values, part)
        return carry

    lax.fori_loop(0, NG // SPAN, forward, 0, unroll=True)

    def across(step, carry):
        lines = [step * SPAN + part for part in range(SPAN)]
        rows = [pl.ds(line, NG, stride=PITCH) for line in lines]
        values = beside([grid[row, :].astype(bf16) for row in rows])
        values = dot(table_ref[...], values)
        values = (values * beside([kernel_ref[line] for line in lines])).astype(bf16)
        values = dot(table_ref[...], values)
        for part, row in enumerate(rows):
            grid[row, :] = part_of(values, part)
        return carry

    lax.fori_loop(0, NG // SPAN, across, 0, unroll=True)

    def potentials(step):
        planes = [step * SPAN + part for part in range(SPAN)]
        values = beside([grid[pitched(plane), :].astype(bf16) for plane in planes])
        values = dot(mixed_ref[...], values).astype(bf16)
        values = dot(values, table_ref[...])
        return [(plane, part_of(values, part)) for part, plane in enumerate(planes)]

    return potentials


def fill_of(ref):
    return ref[pl.ds(ROWS, 16), :].astype(jnp.float32)[:1] * -FRACTION


def both_halves(value, low):
    turned = pltpu.roll(value, 64, 1)
    return jnp.concatenate([jnp.where(low, value, turned), jnp.where(low, turned, value)], axis=0)


def low_lanes(height):
    return lax.broadcasted_iota(jnp.int32, (height, 128), 1) < 64


def own_body(own_ref, table_ref, mixed_ref, kernel_ref, owner_ref, term_ref, grid):
    f32, bf16 = jnp.float32, jnp.bfloat16
    low = low_lanes(NG // 2)

    def density_of(plane):
        mine = both_halves(own_ref[plane_rows(plane, 32), :].astype(f32), low)
        owner_ref[plane_rows(plane, 64), :] = mine.astype(bf16)
        return (mine * mine).astype(bf16)

    potentials = passes_there(density_of, table_ref, mixed_ref, kernel_ref, grid)
    fill = fill_of(own_ref)

    def backward(step, carry):
        for plane, potential in potentials(step):
            total = potential * (owner_ref[plane_rows(plane, 64), :].astype(f32) * fill)
            term_ref[plane_rows(plane, 32), :] = jnp.where(low, total[:32], total[32:])
        return carry

    lax.fori_loop(0, NG // SPAN, backward, 0, unroll=True)


def own_term(own, table, mixed, kernel):
    return pl.pallas_call(
        own_body,
        out_shape=(
            jax.ShapeDtypeStruct((NG * NG, 128), jnp.bfloat16),
            jax.ShapeDtypeStruct((ROWS, 128), jnp.float32),
        ),
        in_specs=[VMEM] * 4,
        out_specs=(VMEM, VMEM),
        scratch_shapes=[pltpu.VMEM((NG * PITCH, 128), jnp.float32)],
        compiler_params=pltpu.CompilerParams(vmem_limit_bytes=24 * 1024 * 1024),
        cost_estimate=pl.CostEstimate(
            flops=EXCHANGE_FLOPS, bytes_accessed=4 * 1024 * 1024, transcendentals=0
        ),
        name="own_term",
    )(own, table, mixed, kernel)


def exchange_body(
    prev_ref, next_ref, owner_ref, term_ref, table_ref, mixed_ref, kernel_ref,
    out_ref, visitors, grid,
):
    f32, bf16 = jnp.float32, jnp.bfloat16
    low = low_lanes(NG // 2)

    def density_of(plane):
        before, after = (ref[plane_rows(plane, 32), :].astype(f32) for ref in (prev_ref, next_ref))
        before_turned, after_turned = (pltpu.roll(value, 64, 1) for value in (before, after))
        pairs = jnp.concatenate(
            [jnp.where(low, before, after_turned), jnp.where(low, before_turned, after)], axis=0
        )
        wide = plane_rows(plane, 64)
        visitors[wide, :] = pairs.astype(bf16)
        return (pairs * owner_ref[wide, :].astype(f32)).astype(bf16)

    potentials = passes_there(density_of, table_ref, mixed_ref, kernel_ref, grid)
    fill = jnp.where(low_lanes(NG), fill_of(prev_ref), fill_of(next_ref))

    def backward(step, carry):
        for plane, potential in potentials(step):
            total = potential * (visitors[plane_rows(plane, 64), :].astype(f32) * fill)
            total = total + pltpu.roll(total, 64, 1)
            rows = plane_rows(plane, 32)
            value = (jnp.where(low, total[:32], total[32:]) + term_ref[rows, :]).astype(bf16)
            out_ref[rows, :] = value
        return carry

    lax.fori_loop(0, NG // SPAN, backward, 0, unroll=True)


def exchange_of(before, after, owner, term, table, mixed, kernel):
    return pl.pallas_call(
        exchange_body,
        out_shape=jax.ShapeDtypeStruct((ROWS, 128), jnp.bfloat16),
        in_specs=[VMEM] * 7,
        out_specs=VMEM,
        scratch_shapes=[
            pltpu.VMEM((NG * NG, 128), jnp.bfloat16),
            pltpu.VMEM((NG * PITCH, 128), jnp.float32),
        ],
        compiler_params=pltpu.CompilerParams(vmem_limit_bytes=24 * 1024 * 1024),
        cost_estimate=pl.CostEstimate(
            flops=EXCHANGE_FLOPS, bytes_accessed=4 * 1024 * 1024, transcendentals=0
        ),
        name="exchange",
    )(before, after, owner, term, table, mixed, kernel)


def unpack_body(tiles_ref, flat_ref):
    def part(step, carry):
        columns = pl.ds(pl.multiple_of(step * 16384, 16384), 16384)
        rows = pl.ds(pl.multiple_of(step * 128, 128), 128)
        value = tiles_ref[rows, :].astype(jnp.float32).reshape(1, 16384)
        flat_ref[0:1, columns] = value.astype(jnp.bfloat16)
        return carry

    lax.fori_loop(0, 16, part, 0)


def by_line_body(tiles_ref, out_ref, wide):
    wide[...] = tiles_ref[...].astype(jnp.float32)
    for line in range(16):
        rows = wide[pl.ds(line, 128, stride=16), :]
        out_ref[pl.ds(line * 128, 128), :] = rows.astype(jnp.bfloat16)


def aside_body(tiles_ref, exchange_ref, lines_ref, flat_ref, wide):
    by_line_body(tiles_ref, lines_ref, wide)
    unpack_body(exchange_ref, flat_ref)


def beside_slabs(tiles, exchange):
    return pl.pallas_call(
        aside_body,
        out_shape=(
            jax.ShapeDtypeStruct((ROWS, 128), jnp.bfloat16),
            jax.ShapeDtypeStruct((1, G), jnp.bfloat16),
        ),
        in_specs=[VMEM, VMEM],
        out_specs=(VMEM, VMEM),
        scratch_shapes=[pltpu.VMEM((ROWS, 128), jnp.float32)],
        compiler_params=pltpu.CompilerParams(vmem_limit_bytes=16 * 1024 * 1024),
        name="beside_slabs",
    )(tiles.reshape(ROWS, 128), exchange)


def intersection_body(tiles_ref, trial_ref, core_ref, lines_ref, mine_ref, other_ref, wide):
    by_line_body(tiles_ref, lines_ref, wide)
    total = jnp.zeros((128, 128), jnp.float32)
    for line in range(16):
        rows = pl.ds(line * 128, 128)
        total = total + lax.dot_general(
            trial_ref[rows, :], lines_ref[rows, :], (((1,), (1,)), ((), ())),
            preferred_element_type=jnp.float32,
        )
    total = total * (1.0 / math.sqrt(G))
    first = core_ref[0] == 0
    mine_ref[...] = jnp.where(first, total[:64], total[64:])
    other_ref[...] = jnp.where(first, total[64:], total[:64])


def intersection_of(tiles, trial_lines, core):
    half = jax.ShapeDtypeStruct((64, 128), jnp.float32)
    return pl.pallas_call(
        intersection_body,
        out_shape=(jax.ShapeDtypeStruct((ROWS, 128), jnp.bfloat16), half, half),
        in_specs=[VMEM, VMEM, SMEM],
        out_specs=(VMEM, VMEM, VMEM),
        scratch_shapes=[pltpu.VMEM((ROWS, 128), jnp.float32)],
        compiler_params=pltpu.CompilerParams(vmem_limit_bytes=16 * 1024 * 1024),
        name="intersection",
    )(tiles.reshape(ROWS, 128), trial_lines, core)


def projected_body(lines_ref, mine_ref, other_ref, core_ref, out_ref):
    first = core_ref[0] == 0
    mine, other = mine_ref[...].astype(jnp.float32), other_ref[...].astype(jnp.float32)
    table = jnp.concatenate(
        [jnp.where(first, mine, other), jnp.where(first, other, mine)], axis=0
    ).astype(jnp.bfloat16)
    for line in range(16):
        rows = pl.ds(line * 128, 128)
        value = dot(table, lines_ref[rows, :]) * (-1.0 / math.sqrt(128))
        out_ref[:, rows] = value.astype(jnp.bfloat16)


def projected_of(lines, mine, other, core):
    return pl.pallas_call(
        projected_body,
        out_shape=jax.ShapeDtypeStruct((128, ROWS), jnp.bfloat16),
        in_specs=[VMEM, VMEM, VMEM, SMEM],
        out_specs=VMEM,
        compiler_params=pltpu.CompilerParams(vmem_limit_bytes=16 * 1024 * 1024),
        name="projected",
    )(lines, mine, other, core)


def passed_along(value, steps):
    count = lax.axis_size(BAND)
    return lax.ppermute(value, BAND, [(i, (i + steps) % count) for i in range(count)])


def swapped(value):
    return lax.ppermute(value, "core", [(0, 1), (1, 0)])


def summed_over(value, axes):
    peers = lax.axis_size(axes)
    copies = jnp.broadcast_to(value[None], (peers,) + value.shape)
    tiles = lax.all_to_all(copies, axes, 0, 0, tiled=True)
    return jnp.sum(tiles.astype(jnp.float32), axis=0).astype(jnp.bfloat16)


def to_slabs(rows):
    return lax.all_to_all(rows.reshape(128, 16, 128), BAND, 0, 0, tiled=True)


def local(orbitals, trial, occupations):
    tables = [jnp.asarray(value) for value in constants()]
    own, trial_rows = packed(orbitals, trial, occupations)
    before, after = passed_along(own, 1), passed_along(own, -1)
    trial_tiles = to_slabs(trial_rows)
    exchange = exchange_of(before, after, *own_term(own, *tables), *tables)
    exchange_tiles = to_slabs(exchange)
    trial_lines, flat = beside_slabs(trial_tiles, exchange)
    core = lax.axis_index("core").astype(jnp.int32).reshape(1)
    lines, mine, other = intersection_of(exchange_tiles, trial_lines, core)
    half = (mine + swapped(other)).astype(jnp.bfloat16)
    half = summed_over(half, ("y", "x"))
    half = summed_over(half, "z")
    return flat, projected_of(lines, half, swapped(half), core)


def solution(mesh):
    finer = Mesh(mesh.devices.reshape(mesh.shape["spin"], 4, 2, 8, 2), SPIN_BAND)
    return jax.shard_map(
        local,
        mesh=finer,
        in_specs=(P(SPIN_BAND, None), P(SPIN_BAND, None), P(SPIN_BAND)),
        out_specs=(P(SPIN_BAND, None), P("spin", BAND)),
        check_vma=False,
    )
```

```python
import math

import jax
import jax.numpy as jnp
import ml_dtypes
import numpy as np
from jax import lax
from jax.experimental import pallas as pl
from jax.experimental.pallas import tpu as pltpu
from jax.sharding import Mesh
from jax.sharding import PartitionSpec as P

NG = 64
G = NG**3
ROWS = G // 128
FRACTION = 0.25
OMEGA = 1.0
BAND = ("y", "x", "z", "core")
SPIN_BAND = ("spin",) + BAND
ORDER = np.concatenate([np.arange(0, NG, 2), np.arange(1, NG, 2)])
STEP = 4
SPAN = 2 * STEP
PITCH = 72
WIDE = 40
NEAR_FLOPS = 10**10
VMEM = pl.BlockSpec(memory_space=pltpu.VMEM)
SMEM = pl.BlockSpec(memory_space=pltpu.SMEM)


def cas_table():
    indices = np.arange(NG)
    phases = (indices[:, None] * indices[None, :] % NG) * (2.0 * math.pi / NG)
    return (np.cos(phases) + np.sin(phases)).astype(np.float32).astype(ml_dtypes.bfloat16)


def screened_kernel():
    modes = np.arange(NG)
    modes = np.where(2 * modes < NG, modes, modes - NG)
    squares = (modes * (2.0 * math.pi / NG)) ** 2
    norm_sq = squares[:, None, None] + squares[None, :, None] + squares[None, None, :]
    bounded = np.where(norm_sq > 0, norm_sq, 1.0)
    screened = np.where(
        norm_sq > 0,
        4.0 * math.pi / bounded * (1.0 - np.exp(-bounded / (4.0 * OMEGA * OMEGA))),
        math.pi / (OMEGA * OMEGA),
    )
    return (screened / NG**3).astype(np.float32)


def repeated(table):
    return np.kron(np.eye(STEP, dtype=np.float32), table.astype(np.float32)).astype(table.dtype)


def constants():
    table = cas_table()
    mixed = table[ORDER][:, ORDER]
    kernel = screened_kernel().transpose(1, 0, 2)[ORDER]
    return repeated(table), repeated(mixed), np.concatenate([kernel, kernel], axis=2)


def dot(left, right):
    return lax.dot_general(
        left, right, (((1,), (0,)), ((), ())), preferred_element_type=jnp.float32
    )


def pack_body(flat_ref, tiles_ref):
    def part(step, carry):
        columns = pl.ds(pl.multiple_of(step * 16384, 16384), 16384)
        rows = pl.ds(pl.multiple_of(step * 128, 128), 128)
        tiles_ref[rows, :] = flat_ref[0:1, columns].reshape(128, 128)
        return carry

    lax.fori_loop(0, 16, part, 0)


def pack_flagged_body(flat_ref, flag_ref, tiles_ref):
    pack_body(flat_ref, tiles_ref)
    flag = jnp.full((16, 128), flag_ref[0], jnp.int32)
    tiles_ref[pl.ds(ROWS, 16), :] = flag.astype(jnp.float32).astype(jnp.bfloat16)


def pack_after_body(flat_ref, earlier_ref, tiles_ref):
    pack_body(flat_ref, tiles_ref)


def packed_after(flat, earlier):
    return pl.pallas_call(
        pack_after_body,
        out_shape=jax.ShapeDtypeStruct((ROWS, 128), jnp.bfloat16),
        in_specs=[VMEM, pl.BlockSpec(memory_space=pl.ANY)],
        out_specs=VMEM,
        compiler_params=pltpu.CompilerParams(vmem_limit_bytes=16 * 1024 * 1024),
        name="pack",
    )(flat, earlier)


def packed_with_flag(flat, flag):
    return pl.pallas_call(
        pack_flagged_body,
        out_shape=jax.ShapeDtypeStruct((ROWS + 16, 128), jnp.bfloat16),
        in_specs=[VMEM, SMEM],
        out_specs=VMEM,
        compiler_params=pltpu.CompilerParams(vmem_limit_bytes=16 * 1024 * 1024),
        name="pack_flagged",
    )(flat, flag)


def plane_rows(plane, height):
    return pl.ds(pl.multiple_of(plane * height, height), height)


def passes_there(density_of, table_ref, mixed_ref, kernel_ref, grid):
    bf16 = jnp.bfloat16

    def pitched(plane):
        return pl.ds(pl.multiple_of(plane * PITCH, 8), NG)

    def beside(parts):
        return jnp.concatenate(
            [jnp.concatenate(parts[:STEP], axis=0), jnp.concatenate(parts[STEP:], axis=0)], axis=1
        )

    def part_of(values, part):
        rows = slice(part % STEP * NG, part % STEP * NG + NG)
        return values[rows, :128] if part < STEP else values[rows, 128:]

    def forward(step, carry):
        planes = [step * SPAN + part for part in range(SPAN)]
        values = beside([density_of(plane) for plane in planes])
        values = dot(values, table_ref[...]).astype(bf16)
        values = dot(mixed_ref[...], values)
        for part, plane in enumerate(planes):
            grid[pitched(plane), :] = part_of(values, part)
        return carry

    lax.fori_loop(0, NG // SPAN, forward, 0, unroll=True)

    def across(step, carry):
        lines = [step * SPAN + part for part in range(SPAN)]
        rows = [pl.ds(line, NG, stride=PITCH) for line in lines]
        values = beside([grid[row, :].astype(bf16) for row in rows])
        values = dot(table_ref[...], values)
        values = (values * beside([kernel_ref[line] for line in lines])).astype(bf16)
        values = dot(table_ref[...], values)
        for part, row in enumerate(rows):
            grid[row, :] = part_of(values, part)
        return carry

    lax.fori_loop(0, NG // SPAN, across, 0, unroll=True)

    def potentials(step):
        planes = [step * SPAN + part for part in range(SPAN)]
        values = beside([grid[pitched(plane), :].astype(bf16) for plane in planes])
        values = dot(mixed_ref[...], values).astype(bf16)
        values = dot(values, table_ref[...])
        return [(plane, part_of(values, part)) for part, plane in enumerate(planes)]

    return potentials


def fill_of(ref):
    return ref[pl.ds(ROWS, 16), :].astype(jnp.float32)[:1] * -FRACTION


def both_halves(value, low):
    turned = pltpu.roll(value, 64, 1)
    return jnp.concatenate([jnp.where(low, value, turned), jnp.where(low, turned, value)], axis=0)


def low_lanes(height):
    return lax.broadcasted_iota(jnp.int32, (height, 128), 1) < 64


def near_body(
    own_ref, near_ref, table_ref, mixed_ref, kernel_ref, owner_ref, term_ref, visitors, grid
):
    f32, bf16 = jnp.float32, jnp.bfloat16
    low = low_lanes(NG // 2)

    def density_of(plane):
        own, near = (ref[plane_rows(plane, 32), :].astype(f32) for ref in (own_ref, near_ref))
        own_turned, near_turned = (pltpu.roll(value, 64, 1) for value in (own, near))
        mine = jnp.concatenate(
            [jnp.where(low, own, own_turned), jnp.where(low, own_turned, own)], axis=0
        )
        pairs = jnp.concatenate(
            [jnp.where(low, own, near_turned), jnp.where(low, own_turned, near)], axis=0
        )
        wide = plane_rows(plane, 64)
        owner_ref[wide, :] = mine.astype(bf16)
        visitors[wide, :] = pairs.astype(bf16)
        return (mine * pairs).astype(bf16)

    potentials = passes_there(density_of, table_ref, mixed_ref, kernel_ref, grid)
    fill = jnp.where(low_lanes(NG), fill_of(own_ref), fill_of(near_ref))

    def backward(step, carry):
        for plane, potential in potentials(step):
            total = potential * (visitors[plane_rows(plane, 64), :].astype(f32) * fill)
            total = total + pltpu.roll(total, 64, 1)
            term_ref[plane_rows(plane, 32), :] = jnp.where(low, total[:32], total[32:])
        return carry

    lax.fori_loop(0, NG // SPAN, backward, 0, unroll=True)


def near_term(own, near, table, mixed, kernel):
    return pl.pallas_call(
        near_body,
        out_shape=(
            jax.ShapeDtypeStruct((NG * NG, 128), jnp.bfloat16),
            jax.ShapeDtypeStruct((ROWS, 128), jnp.float32),
        ),
        in_specs=[VMEM] * 5,
        out_specs=(VMEM, VMEM),
        scratch_shapes=[
            pltpu.VMEM((NG * NG, 128), jnp.bfloat16),
            pltpu.VMEM((NG * PITCH, 128), jnp.float32),
        ],
        compiler_params=pltpu.CompilerParams(vmem_limit_bytes=24 * 1024 * 1024),
        cost_estimate=pl.CostEstimate(
            flops=NEAR_FLOPS, bytes_accessed=4 * 1024 * 1024, transcendentals=0
        ),
        name="near_term",
    )(own, near, table, mixed, kernel)


def exchange_body(
    far_ref, owner_ref, term_ref, trial_ref, table_ref, mixed_ref, kernel_ref,
    out_ref, visitors, grid,
):
    f32, bf16 = jnp.float32, jnp.bfloat16
    low = low_lanes(NG // 2)

    def density_of(plane):
        far = both_halves(far_ref[plane_rows(plane, 32), :].astype(f32), low)
        wide = plane_rows(plane, 64)
        visitors[wide, :] = far.astype(bf16)
        return (far * owner_ref[wide, :].astype(f32)).astype(bf16)

    potentials = passes_there(density_of, table_ref, mixed_ref, kernel_ref, grid)
    fill = fill_of(far_ref)

    def backward(step, carry):
        for plane, potential in potentials(step):
            total = potential * (visitors[plane_rows(plane, 64), :].astype(f32) * fill)
            rows = plane_rows(plane, 32)
            value = (jnp.where(low, total[:32], total[32:]) + term_ref[rows, :]).astype(bf16)
            trial = trial_ref[rows, :]
            out_ref[plane_rows(plane, 64), :] = jnp.concatenate(
                [trial[:16], value[:16], trial[16:], value[16:]], axis=0
            )
        return carry

    lax.fori_loop(0, NG // SPAN, backward, 0, unroll=True)


def exchange_of(far, owner, term, trial, table, mixed, kernel):
    return pl.pallas_call(
        exchange_body,
        out_shape=jax.ShapeDtypeStruct((2 * ROWS, 128), jnp.bfloat16),
        in_specs=[VMEM] * 7,
        out_specs=VMEM,
        scratch_shapes=[
            pltpu.VMEM((NG * NG, 128), jnp.bfloat16),
            pltpu.VMEM((NG * PITCH, 128), jnp.float32),
        ],
        compiler_params=pltpu.CompilerParams(vmem_limit_bytes=24 * 1024 * 1024),
        name="exchange",
    )(far, owner, term, trial, table, mixed, kernel)


def unpack_body(tiles_ref, flat_ref, token_ref):
    def part(step, carry):
        columns = pl.ds(pl.multiple_of(step * 16384, 16384), 16384)
        tiles = [tiles_ref[pl.ds(step * 256 + peer * 32 + 16, 16), :] for peer in range(8)]
        value = jnp.concatenate(tiles, axis=0).astype(jnp.float32).reshape(1, 16384)
        flat_ref[0:1, columns] = value.astype(jnp.bfloat16)
        return carry

    lax.fori_loop(0, 16, part, 0)
    token_ref[...] = tiles_ref[pl.ds(0, 16), :]


def unpacked(tiles):
    return pl.pallas_call(
        unpack_body,
        out_shape=(
            jax.ShapeDtypeStruct((1, G), jnp.bfloat16),
            jax.ShapeDtypeStruct((16, 128), jnp.bfloat16),
        ),
        in_specs=[VMEM],
        out_specs=(VMEM, VMEM),
        compiler_params=pltpu.CompilerParams(vmem_limit_bytes=16 * 1024 * 1024),
        name="unpack",
    )(tiles)


def intersection_body(tiles_ref, token_ref, core_ref, lines_ref, mine_ref, other_ref, wide):
    bf16 = jnp.bfloat16
    for peer in range(128):
        wide[pl.ds(peer * WIDE, 32), :] = tiles_ref[pl.ds(peer * 32, 32), :].astype(jnp.float32)
    total = jnp.zeros((128, 128), jnp.float32)
    for line in range(16):
        trial = wide[pl.ds(line, 128, stride=WIDE), :].astype(bf16)
        value = wide[pl.ds(line + 16, 128, stride=WIDE), :].astype(bf16)
        lines_ref[pl.ds(line * 128, 128), :] = value
        total = total + lax.dot_general(
            trial, value, (((1,), (1,)), ((), ())), preferred_element_type=jnp.float32
        )
    total = total * (1.0 / math.sqrt(G))
    first = core_ref[0] == 0
    mine_ref[...] = jnp.where(first, total[:64], total[64:])
    other_ref[...] = jnp.where(first, total[64:], total[:64])


def intersection_of(tiles, token, core):
    half = jax.ShapeDtypeStruct((64, 128), jnp.float32)
    return pl.pallas_call(
        intersection_body,
        out_shape=(jax.ShapeDtypeStruct((ROWS, 128), jnp.bfloat16), half, half),
        in_specs=[VMEM, pl.BlockSpec(memory_space=pl.ANY), SMEM],
        out_specs=(VMEM, VMEM, VMEM),
        scratch_shapes=[pltpu.VMEM((128 * WIDE, 128), jnp.float32)],
        compiler_params=pltpu.CompilerParams(vmem_limit_bytes=16 * 1024 * 1024),
        name="intersection",
    )(tiles, token, core)


def projected_body(lines_ref, mine_ref, other_ref, core_ref, out_ref):
    first = core_ref[0] == 0
    mine, other = mine_ref[...].astype(jnp.float32), other_ref[...].astype(jnp.float32)
    table = jnp.concatenate(
        [jnp.where(first, mine, other), jnp.where(first, other, mine)], axis=0
    ).astype(jnp.bfloat16)
    for line in range(16):
        rows = pl.ds(line * 128, 128)
        value = dot(table, lines_ref[rows, :]) * (-1.0 / math.sqrt(128))
        out_ref[:, rows] = value.astype(jnp.bfloat16)


def projected_of(lines, mine, other, core):
    return pl.pallas_call(
        projected_body,
        out_shape=jax.ShapeDtypeStruct((128, ROWS), jnp.bfloat16),
        in_specs=[VMEM, VMEM, VMEM, SMEM],
        out_specs=VMEM,
        compiler_params=pltpu.CompilerParams(vmem_limit_bytes=16 * 1024 * 1024),
        name="projected",
    )(lines, mine, other, core)


def from_far(value):
    count = lax.axis_size(BAND)
    pairs = [(i, (i - 1 if i % 2 == 0 else i + 1) % count) for i in range(count)]
    return lax.ppermute(value, BAND, pairs)


def swapped(value):
    return lax.ppermute(value, "core", [(0, 1), (1, 0)])


def summed_over(value, axes):
    peers = lax.axis_size(axes)
    copies = jnp.broadcast_to(value[None], (peers,) + value.shape)
    tiles = lax.all_to_all(copies, axes, 0, 0, tiled=True)
    return jnp.sum(tiles.astype(jnp.float32), axis=0).astype(jnp.bfloat16)


def local(orbitals, trial, occupations):
    tables = [jnp.asarray(value) for value in constants()]
    own = packed_with_flag(orbitals, occupations)
    far, near = from_far(own), swapped(own)
    trial_rows = packed_after(trial, own)
    owner, term = near_term(own, near, *tables)
    both = exchange_of(far, owner, term, trial_rows, *tables)
    tiles = lax.all_to_all(both.reshape(128, 32, 128), BAND, 0, 0, tiled=True)
    flat, token = unpacked(both)
    core = lax.axis_index("core").astype(jnp.int32).reshape(1)
    lines, mine, other = intersection_of(tiles.reshape(2 * ROWS, 128), token, core)
    half = (mine + swapped(other)).astype(jnp.bfloat16)
    half = summed_over(half, ("y", "x"))
    half = summed_over(half, "z")
    return flat, projected_of(lines, half, swapped(half), core)


def solution(mesh):
    finer = Mesh(mesh.devices.reshape(mesh.shape["spin"], 4, 2, 8, 2), SPIN_BAND)
    return jax.shard_map(
        local,
        mesh=finer,
        in_specs=(P(SPIN_BAND, None), P(SPIN_BAND, None), P(SPIN_BAND)),
        out_specs=(P(SPIN_BAND, None), P("spin", BAND)),
        check_vma=False,
    )
```

```python
import math

import jax
import jax.numpy as jnp
import ml_dtypes
import numpy as np
from jax import lax
from jax.experimental import pallas as pl
from jax.experimental.pallas import tpu as pltpu
from jax.sharding import Mesh
from jax.sharding import PartitionSpec as P

NG = 64
G = NG**3
ROWS = G // 128
FRACTION = 0.25
OMEGA = 1.0
BAND = ("y", "x", "z", "core")
SPIN_BAND = ("spin",) + BAND
ORDER = np.concatenate([np.arange(0, NG, 2), np.arange(1, NG, 2)])
STEP = 4
SPAN = 2 * STEP
PITCH = 72
WIDE = 40
NEAR_FLOPS = 10**10
VMEM = pl.BlockSpec(memory_space=pltpu.VMEM)
SMEM = pl.BlockSpec(memory_space=pltpu.SMEM)


def cas_table():
    indices = np.arange(NG)
    phases = (indices[:, None] * indices[None, :] % NG) * (2.0 * math.pi / NG)
    return (np.cos(phases) + np.sin(phases)).astype(np.float32).astype(ml_dtypes.bfloat16)


def squared_modes(index):
    modes = jnp.where(2 * index < NG, index, index - NG)
    wavenum = modes.astype(jnp.float32) * (2.0 * math.pi / NG)
    return wavenum * wavenum


def screened_body(earlier_ref, kernel_ref):
    first = squared_modes(lax.broadcasted_iota(jnp.int32, (NG, 128), 0))
    third = squared_modes(lax.rem(lax.broadcasted_iota(jnp.int32, (NG, 128), 1), NG))

    def one_line(line, carry):
        second = 2 * lax.rem(line, NG // 2) + lax.div(line, NG // 2)
        norm_sq = first + squared_modes(jnp.full((NG, 128), second, jnp.int32)) + third
        bounded = jnp.where(norm_sq > 0, norm_sq, 1.0)
        screened = jnp.where(
            norm_sq > 0,
            4.0 * math.pi / bounded * (1.0 - jnp.exp(-bounded / (4.0 * OMEGA * OMEGA))),
            math.pi / (OMEGA * OMEGA),
        )
        kernel_ref[line] = screened * (1.0 / G)
        return carry

    lax.fori_loop(0, NG, one_line, 0, unroll=2)


def screened_kernel(earlier):
    return pl.pallas_call(
        screened_body,
        out_shape=jax.ShapeDtypeStruct((NG, NG, 128), jnp.float32),
        in_specs=[pl.BlockSpec(memory_space=pl.ANY)],
        out_specs=VMEM,
        compiler_params=pltpu.CompilerParams(vmem_limit_bytes=16 * 1024 * 1024),
        cost_estimate=pl.CostEstimate(
            flops=NEAR_FLOPS, bytes_accessed=2 * 1024 * 1024, transcendentals=0
        ),
        name="screened_kernel",
    )(earlier)


def repeated(table):
    return np.kron(np.eye(STEP, dtype=np.float32), table.astype(np.float32)).astype(table.dtype)


def constants():
    table = cas_table()
    mixed = table[ORDER][:, ORDER]
    return repeated(table), repeated(mixed)


def dot(left, right):
    return lax.dot_general(
        left, right, (((1,), (0,)), ((), ())), preferred_element_type=jnp.float32
    )


def pack_body(flat_ref, tiles_ref):
    def part(step, carry):
        columns = pl.ds(pl.multiple_of(step * 16384, 16384), 16384)
        rows = pl.ds(pl.multiple_of(step * 128, 128), 128)
        tiles_ref[rows, :] = flat_ref[0:1, columns].reshape(128, 128)
        return carry

    lax.fori_loop(0, 16, part, 0)


def pack_flagged_body(flat_ref, flag_ref, tiles_ref):
    pack_body(flat_ref, tiles_ref)
    flag = jnp.full((16, 128), flag_ref[0], jnp.int32)
    tiles_ref[pl.ds(ROWS, 16), :] = flag.astype(jnp.float32).astype(jnp.bfloat16)


def pack_after_body(flat_ref, earlier_ref, tiles_ref):
    pack_body(flat_ref, tiles_ref)


def packed_after(flat, earlier):
    return pl.pallas_call(
        pack_after_body,
        out_shape=jax.ShapeDtypeStruct((ROWS, 128), jnp.bfloat16),
        in_specs=[VMEM, pl.BlockSpec(memory_space=pl.ANY)],
        out_specs=VMEM,
        compiler_params=pltpu.CompilerParams(vmem_limit_bytes=16 * 1024 * 1024),
        name="pack",
    )(flat, earlier)


def packed_with_flag(flat, flag):
    return pl.pallas_call(
        pack_flagged_body,
        out_shape=jax.ShapeDtypeStruct((ROWS + 16, 128), jnp.bfloat16),
        in_specs=[VMEM, SMEM],
        out_specs=VMEM,
        compiler_params=pltpu.CompilerParams(vmem_limit_bytes=16 * 1024 * 1024),
        name="pack_flagged",
    )(flat, flag)


def plane_rows(plane, height):
    if isinstance(plane, int):
        return pl.ds(plane * height, height)
    return pl.ds(pl.multiple_of(plane * height, height), height)


def passes_there(density_of, table_ref, mixed_ref, kernel_ref, grid):
    bf16 = jnp.bfloat16

    def pitched(plane):
        if isinstance(plane, int):
            return pl.ds(plane * PITCH, NG)
        return pl.ds(pl.multiple_of(plane * PITCH, 8), NG)

    def beside(parts):
        return jnp.concatenate(
            [jnp.concatenate(parts[:STEP], axis=0), jnp.concatenate(parts[STEP:], axis=0)], axis=1
        )

    def part_of(values, part):
        rows = slice(part % STEP * NG, part % STEP * NG + NG)
        return values[rows, :128] if part < STEP else values[rows, 128:]

    def forward(step, carry):
        planes = [step * SPAN + part for part in range(SPAN)]
        values = beside([density_of(plane) for plane in planes])
        values = dot(values, table_ref[...]).astype(bf16)
        values = dot(mixed_ref[...], values)
        for part, plane in enumerate(planes):
            grid[pitched(plane), :] = part_of(values, part)
        return carry

    lax.fori_loop(0, NG // SPAN, forward, 0, unroll=True)

    def across(step, carry):
        lines = [step * SPAN + part for part in range(SPAN)]
        rows = [pl.ds(line, NG, stride=PITCH) for line in lines]
        values = beside([grid[row, :].astype(bf16) for row in rows])
        values = dot(table_ref[...], values)
        values = (values * beside([kernel_ref[line] for line in lines])).astype(bf16)
        values = dot(table_ref[...], values)
        for part, row in enumerate(rows):
            grid[row, :] = part_of(values, part)
        return carry

    lax.fori_loop(0, NG // SPAN, across, 0, unroll=True)

    def potentials(step):
        planes = [step * SPAN + part for part in range(SPAN)]
        values = beside([grid[pitched(plane), :].astype(bf16) for plane in planes])
        values = dot(mixed_ref[...], values).astype(bf16)
        values = dot(values, table_ref[...])
        return [(plane, part_of(values, part)) for part, plane in enumerate(planes)]

    return potentials


def fill_of(ref):
    return ref[pl.ds(ROWS, 16), :].astype(jnp.float32)[:1] * -FRACTION


def both_halves(value, low):
    turned = pltpu.roll(value, 64, 1)
    return jnp.concatenate([jnp.where(low, value, turned), jnp.where(low, turned, value)], axis=0)


def low_lanes(height):
    return lax.broadcasted_iota(jnp.int32, (height, 128), 1) < 64


def near_body(
    own_ref, near_ref, table_ref, mixed_ref, kernel_ref, owner_ref, term_ref, visitors, grid
):
    f32, bf16 = jnp.float32, jnp.bfloat16
    low = low_lanes(NG // 2)

    def density_of(plane):
        own, near = (ref[plane_rows(plane, 32), :].astype(f32) for ref in (own_ref, near_ref))
        own_turned, near_turned = (pltpu.roll(value, 64, 1) for value in (own, near))
        mine = jnp.concatenate(
            [jnp.where(low, own, own_turned), jnp.where(low, own_turned, own)], axis=0
        )
        pairs = jnp.concatenate(
            [jnp.where(low, own, near_turned), jnp.where(low, own_turned, near)], axis=0
        )
        wide = plane_rows(plane, 64)
        owner_ref[wide, :] = mine.astype(bf16)
        visitors[wide, :] = pairs.astype(bf16)
        return (mine * pairs).astype(bf16)

    potentials = passes_there(density_of, table_ref, mixed_ref, kernel_ref, grid)
    fill = jnp.where(low_lanes(NG), fill_of(own_ref), fill_of(near_ref))

    def backward(step, carry):
        for plane, potential in potentials(step):
            total = potential * (visitors[plane_rows(plane, 64), :].astype(f32) * fill)
            total = total + pltpu.roll(total, 64, 1)
            term_ref[plane_rows(plane, 32), :] = jnp.where(low, total[:32], total[32:])
        return carry

    lax.fori_loop(0, NG // SPAN, backward, 0, unroll=True)


def near_term(own, near, table, mixed, kernel):
    return pl.pallas_call(
        near_body,
        out_shape=(
            jax.ShapeDtypeStruct((NG * NG, 128), jnp.bfloat16),
            jax.ShapeDtypeStruct((ROWS, 128), jnp.float32),
        ),
        in_specs=[VMEM] * 5,
        out_specs=(VMEM, VMEM),
        scratch_shapes=[
            pltpu.VMEM((NG * NG, 128), jnp.bfloat16),
            pltpu.VMEM((NG * PITCH, 128), jnp.float32),
        ],
        compiler_params=pltpu.CompilerParams(vmem_limit_bytes=24 * 1024 * 1024),
        cost_estimate=pl.CostEstimate(
            flops=NEAR_FLOPS, bytes_accessed=4 * 1024 * 1024, transcendentals=0
        ),
        name="near_term",
    )(own, near, table, mixed, kernel)


def exchange_body(
    far_ref, owner_ref, term_ref, trial_ref, table_ref, mixed_ref, kernel_ref,
    out_ref, visitors, grid, tiles, trial_left, left,
):
    f32, bf16 = jnp.float32, jnp.bfloat16
    low = low_lanes(NG // 2)
    trial_copy = pltpu.make_async_copy(trial_ref, out_ref.at[:, pl.ds(0, 16), :], trial_left)
    trial_copy.start()

    def density_of(plane):
        far = both_halves(far_ref[plane_rows(plane, 32), :].astype(f32), low)
        wide = plane_rows(plane, 64)
        visitors[wide, :] = far.astype(bf16)
        return (far * owner_ref[wide, :].astype(f32)).astype(bf16)

    potentials = passes_there(density_of, table_ref, mixed_ref, kernel_ref, grid)
    fill = fill_of(far_ref)

    def tile_copy(step):
        peers = pl.ds(step * 2 * SPAN, 2 * SPAN)
        return pltpu.make_async_copy(
            tiles.at[peers], out_ref.at[peers, pl.ds(16, 16), :], left.at[step]
        )

    for step in range(NG // SPAN):
        for plane, potential in potentials(step):
            total = potential * (visitors[plane_rows(plane, 64), :].astype(f32) * fill)
            value = jnp.where(low, total[:32], total[32:]) + term_ref[plane_rows(plane, 32), :]
            tiles[pl.ds(2 * plane, 2)] = value.astype(bf16).reshape(2, 16, 128)
        tile_copy(step).start()
    trial_copy.wait()
    for step in range(NG // SPAN):
        tile_copy(step).wait()


def exchange_of(far, owner, term, trial, table, mixed, kernel):
    return pl.pallas_call(
        exchange_body,
        out_shape=jax.ShapeDtypeStruct((128, 32, 128), jnp.bfloat16),
        in_specs=[VMEM] * 7,
        out_specs=pl.BlockSpec(memory_space=pltpu.HBM),
        scratch_shapes=[
            pltpu.VMEM((NG * NG, 128), jnp.bfloat16),
            pltpu.VMEM((NG * PITCH, 128), jnp.float32),
            pltpu.VMEM((128, 16, 128), jnp.bfloat16),
            pltpu.SemaphoreType.DMA,
            pltpu.SemaphoreType.DMA((NG // SPAN,)),
        ],
        compiler_params=pltpu.CompilerParams(vmem_limit_bytes=24 * 1024 * 1024),
        name="exchange",
    )(far, owner, term, trial, table, mixed, kernel)


def unpack_body(tiles_ref, flat_ref, token_ref):
    def part(step, carry):
        columns = pl.ds(pl.multiple_of(step * 16384, 16384), 16384)
        tiles = [tiles_ref[pl.ds(step * 256 + peer * 32 + 16, 16), :] for peer in range(8)]
        value = jnp.concatenate(tiles, axis=0).astype(jnp.float32).reshape(1, 16384)
        flat_ref[0:1, columns] = value.astype(jnp.bfloat16)
        return carry

    lax.fori_loop(0, 16, part, 0)
    token_ref[...] = tiles_ref[pl.ds(0, 16), :]


def unpacked(tiles):
    return pl.pallas_call(
        unpack_body,
        out_shape=(
            jax.ShapeDtypeStruct((1, G), jnp.bfloat16),
            jax.ShapeDtypeStruct((16, 128), jnp.bfloat16),
        ),
        in_specs=[VMEM],
        out_specs=(VMEM, VMEM),
        compiler_params=pltpu.CompilerParams(vmem_limit_bytes=16 * 1024 * 1024),
        name="unpack",
    )(tiles)


def intersection_body(tiles_ref, token_ref, core_ref, lines_ref, mine_ref, other_ref, wide):
    bf16 = jnp.bfloat16
    for peer in range(128):
        wide[pl.ds(peer * WIDE, 32), :] = tiles_ref[pl.ds(peer * 32, 32), :].astype(jnp.float32)
    total = jnp.zeros((128, 128), jnp.float32)
    for line in range(16):
        trial = wide[pl.ds(line, 128, stride=WIDE), :].astype(bf16)
        value = wide[pl.ds(line + 16, 128, stride=WIDE), :].astype(bf16)
        lines_ref[pl.ds(line * 128, 128), :] = value
        total = total + lax.dot_general(
            trial, value, (((1,), (1,)), ((), ())), preferred_element_type=jnp.float32
        )
    total = total * (1.0 / math.sqrt(G))
    first = core_ref[0] == 0
    mine_ref[...] = jnp.where(first, total[:64], total[64:])
    other_ref[...] = jnp.where(first, total[64:], total[:64])


def intersection_of(tiles, token, core):
    half = jax.ShapeDtypeStruct((64, 128), jnp.float32)
    return pl.pallas_call(
        intersection_body,
        out_shape=(jax.ShapeDtypeStruct((ROWS, 128), jnp.bfloat16), half, half),
        in_specs=[VMEM, pl.BlockSpec(memory_space=pl.ANY), SMEM],
        out_specs=(VMEM, VMEM, VMEM),
        scratch_shapes=[pltpu.VMEM((128 * WIDE, 128), jnp.float32)],
        compiler_params=pltpu.CompilerParams(vmem_limit_bytes=16 * 1024 * 1024),
        name="intersection",
    )(tiles, token, core)


def projected_body(lines_ref, mine_ref, other_ref, core_ref, out_ref, result, left):
    first = core_ref[0] == 0
    mine, other = mine_ref[...].astype(jnp.float32), other_ref[...].astype(jnp.float32)
    table = jnp.concatenate(
        [jnp.where(first, mine, other), jnp.where(first, other, mine)], axis=0
    ).astype(jnp.bfloat16)

    def copy(part):
        columns = pl.ds(part * 512, 512)
        return pltpu.make_async_copy(result.at[:, columns], out_ref.at[:, columns], left.at[part])

    for part in range(4):
        for line in range(part * 4, part * 4 + 4):
            rows = pl.ds(line * 128, 128)
            value = dot(table, lines_ref[rows, :]) * (-1.0 / math.sqrt(128))
            result[:, rows] = value.astype(jnp.bfloat16)
        copy(part).start()
    for part in range(4):
        copy(part).wait()


def projected_of(lines, mine, other, core):
    return pl.pallas_call(
        projected_body,
        out_shape=jax.ShapeDtypeStruct((128, ROWS), jnp.bfloat16),
        in_specs=[VMEM, VMEM, VMEM, SMEM],
        out_specs=pl.BlockSpec(memory_space=pltpu.HBM),
        scratch_shapes=[
            pltpu.VMEM((128, ROWS), jnp.bfloat16),
            pltpu.SemaphoreType.DMA((4,)),
        ],
        compiler_params=pltpu.CompilerParams(vmem_limit_bytes=16 * 1024 * 1024),
        name="projected",
    )(lines, mine, other, core)


def from_far(value):
    count = lax.axis_size(BAND)
    pairs = [(i, (i - 1 if i % 2 == 0 else i + 1) % count) for i in range(count)]
    return lax.ppermute(value, BAND, pairs)


def swapped(value):
    return lax.ppermute(value, "core", [(0, 1), (1, 0)])


def summed_over(value, axes):
    peers = lax.axis_size(axes)
    copies = jnp.broadcast_to(value[None], (peers,) + value.shape)
    tiles = lax.all_to_all(copies, axes, 0, 0, tiled=True)
    return jnp.sum(tiles.astype(jnp.float32), axis=0).astype(jnp.bfloat16)


def local(orbitals, trial, occupations):
    own = packed_with_flag(orbitals, occupations)
    tables = [jnp.asarray(value) for value in constants()] + [screened_kernel(own)]
    far, near = from_far(own), swapped(own)
    trial_rows = packed_after(trial, own)
    owner, term = near_term(own, near, *tables)
    both = exchange_of(far, owner, term, trial_rows.reshape(128, 16, 128), *tables)
    tiles = lax.all_to_all(both, BAND, 0, 0, tiled=True)
    flat, token = unpacked(both.reshape(2 * ROWS, 128))
    core = lax.axis_index("core").astype(jnp.int32).reshape(1)
    lines, mine, other = intersection_of(tiles.reshape(2 * ROWS, 128), token, core)
    half = (mine + swapped(other)).astype(jnp.bfloat16)
    half = summed_over(half, ("y", "x"))
    half = summed_over(half, "z")
    return flat, projected_of(lines, half, swapped(half), core)


def solution(mesh):
    finer = Mesh(mesh.devices.reshape(mesh.shape["spin"], 4, 2, 8, 2), SPIN_BAND)
    return jax.shard_map(
        local,
        mesh=finer,
        in_specs=(P(SPIN_BAND, None), P(SPIN_BAND, None), P(SPIN_BAND)),
        out_specs=(P(SPIN_BAND, None), P("spin", BAND)),
        check_vma=False,
    )
```

```python
import math

import jax
import jax.numpy as jnp
import ml_dtypes
import numpy as np
from jax import lax
from jax.experimental import pallas as pl
from jax.experimental.pallas import tpu as pltpu
from jax.sharding import Mesh
from jax.sharding import PartitionSpec as P

NG = 64
G = NG**3
ROWS = G // 128
FRACTION = 0.25
OMEGA = 1.0
BAND = ("y", "x", "z", "core")
SPIN_BAND = ("spin",) + BAND
ORDER = np.concatenate([np.arange(0, NG, 2), np.arange(1, NG, 2)])
STEP = 4
SPAN = 2 * STEP
PITCH = 72
WIDE = 40
HALF = NG // 2
NEAR_FLOPS = 10**10
VMEM = pl.BlockSpec(memory_space=pltpu.VMEM)
SMEM = pl.BlockSpec(memory_space=pltpu.SMEM)


def cas_table():
    indices = np.arange(NG)
    phases = (indices[:, None] * indices[None, :] % NG) * (2.0 * math.pi / NG)
    return (np.cos(phases) + np.sin(phases)).astype(np.float32).astype(ml_dtypes.bfloat16)


def squared_modes(index):
    modes = jnp.where(2 * index < NG, index, index - NG)
    wavenum = modes.astype(jnp.float32) * (2.0 * math.pi / NG)
    return wavenum * wavenum


def screened_body(earlier_ref, kernel_ref):
    first = squared_modes(lax.broadcasted_iota(jnp.int32, (NG, 128), 0))
    third = squared_modes(lax.rem(lax.broadcasted_iota(jnp.int32, (NG, 128), 1), NG))

    def one_line(line, carry):
        second = 2 * lax.rem(line, NG // 2) + lax.div(line, NG // 2)
        norm_sq = first + squared_modes(jnp.full((NG, 128), second, jnp.int32)) + third
        bounded = jnp.where(norm_sq > 0, norm_sq, 1.0)
        screened = jnp.where(
            norm_sq > 0,
            4.0 * math.pi / bounded * (1.0 - jnp.exp(-bounded / (4.0 * OMEGA * OMEGA))),
            math.pi / (OMEGA * OMEGA),
        )
        kernel_ref[line] = screened * (1.0 / G)
        return carry

    lax.fori_loop(0, NG, one_line, 0, unroll=2)


def screened_kernel(earlier):
    return pl.pallas_call(
        screened_body,
        out_shape=jax.ShapeDtypeStruct((NG, NG, 128), jnp.float32),
        in_specs=[pl.BlockSpec(memory_space=pl.ANY)],
        out_specs=VMEM,
        compiler_params=pltpu.CompilerParams(vmem_limit_bytes=16 * 1024 * 1024),
        cost_estimate=pl.CostEstimate(
            flops=NEAR_FLOPS, bytes_accessed=2 * 1024 * 1024, transcendentals=0
        ),
        name="screened_kernel",
    )(earlier)


def repeated(table):
    return np.kron(np.eye(STEP, dtype=np.float32), table.astype(np.float32)).astype(table.dtype)


def constants():
    table = cas_table()
    mixed = table[ORDER][:, ORDER]
    crossed = np.concatenate([table[HALF:, HALF:], table[HALF:, :HALF]], axis=1)
    halves = np.concatenate([table[:HALF], crossed], axis=0)
    return repeated(table), repeated(mixed), repeated(halves)


def dot(left, right):
    return lax.dot_general(
        left, right, (((1,), (0,)), ((), ())), preferred_element_type=jnp.float32
    )


def pack_body(flat_ref, tiles_ref):
    def part(step, carry):
        columns = pl.ds(pl.multiple_of(step * 16384, 16384), 16384)
        rows = pl.ds(pl.multiple_of(step * 128, 128), 128)
        tiles_ref[rows, :] = flat_ref[0:1, columns].reshape(128, 128)
        return carry

    lax.fori_loop(0, 16, part, 0)


def pack_flagged_body(flat_ref, flag_ref, tiles_ref):
    pack_body(flat_ref, tiles_ref)
    flag = jnp.broadcast_to(flag_ref[...], (16, 128))
    tiles_ref[pl.ds(ROWS, 16), :] = flag.astype(jnp.float32).astype(jnp.bfloat16)


def pack_after_body(flat_ref, earlier_ref, tiles_ref):
    pack_body(flat_ref, tiles_ref)


def packed_after(flat, earlier):
    return pl.pallas_call(
        pack_after_body,
        out_shape=jax.ShapeDtypeStruct((ROWS, 128), jnp.bfloat16),
        in_specs=[VMEM, pl.BlockSpec(memory_space=pl.ANY)],
        out_specs=VMEM,
        compiler_params=pltpu.CompilerParams(vmem_limit_bytes=16 * 1024 * 1024),
        name="pack",
    )(flat, earlier)


def packed_with_flag(flat, flag):
    return pl.pallas_call(
        pack_flagged_body,
        out_shape=jax.ShapeDtypeStruct((ROWS + 16, 128), jnp.bfloat16),
        in_specs=[VMEM, VMEM],
        out_specs=VMEM,
        compiler_params=pltpu.CompilerParams(vmem_limit_bytes=16 * 1024 * 1024),
        name="pack_flagged",
    )(flat, flag.reshape(1, 1))


def plane_rows(plane, height):
    if isinstance(plane, int):
        return pl.ds(plane * height, height)
    return pl.ds(pl.multiple_of(plane * height, height), height)


def pitched(plane):
    if isinstance(plane, int):
        return pl.ds(plane * PITCH, NG)
    return pl.ds(pl.multiple_of(plane * PITCH, 8), NG)


def beside(parts):
    return jnp.concatenate(
        [jnp.concatenate(parts[:STEP], axis=0), jnp.concatenate(parts[STEP:], axis=0)], axis=1
    )


def part_of(values, part):
    rows = slice(part % STEP * NG, part % STEP * NG + NG)
    return values[rows, :128] if part < STEP else values[rows, 128:]


def passes_there(density_of, table_ref, mixed_ref, kernel_ref, grid):
    bf16 = jnp.bfloat16

    def forward(step, carry):
        planes = [step * SPAN + part for part in range(SPAN)]
        values = beside([density_of(plane) for plane in planes])
        values = dot(values, table_ref[...]).astype(bf16)
        values = dot(mixed_ref[...], values)
        for part, plane in enumerate(planes):
            grid[pitched(plane), :] = part_of(values, part)
        return carry

    lax.fori_loop(0, NG // SPAN, forward, 0, unroll=True)

    def across(step, carry):
        lines = [step * SPAN + part for part in range(SPAN)]
        rows = [pl.ds(line, NG, stride=PITCH) for line in lines]
        values = beside([grid[row, :].astype(bf16) for row in rows])
        values = dot(table_ref[...], values)
        values = (values * beside([kernel_ref[line] for line in lines])).astype(bf16)
        values = dot(table_ref[...], values)
        for part, row in enumerate(rows):
            grid[row, :] = part_of(values, part)
        return carry

    lax.fori_loop(0, NG // SPAN, across, 0, unroll=True)

    def potentials(step):
        planes = [step * SPAN + part for part in range(SPAN)]
        values = beside([grid[pitched(plane), :].astype(bf16) for plane in planes])
        values = dot(mixed_ref[...], values).astype(bf16)
        values = dot(values, table_ref[...])
        return [(plane, part_of(values, part)) for part, plane in enumerate(planes)]

    return potentials


def fill_of(ref):
    return ref[pl.ds(ROWS, 16), :].astype(jnp.float32)[:1] * -FRACTION


def two_planes(ref, plane, low):
    first, second = (
        ref[plane_rows(index, 32), :].astype(jnp.float32) for index in (plane, plane + HALF)
    )
    first_turned, second_turned = (pltpu.roll(value, 64, 1) for value in (first, second))
    return jnp.concatenate(
        [jnp.where(low, first, second_turned), jnp.where(low, first_turned, second)], axis=0
    )


def low_lanes(height):
    return lax.broadcasted_iota(jnp.int32, (height, 128), 1) < 64


def near_body(
    own_ref, near_ref, table_ref, mixed_ref, kernel_ref, owner_ref, term_ref, visitors, grid
):
    f32, bf16 = jnp.float32, jnp.bfloat16
    low = low_lanes(NG // 2)

    def density_of(plane):
        own, near = (ref[plane_rows(plane, 32), :].astype(f32) for ref in (own_ref, near_ref))
        own_turned, near_turned = (pltpu.roll(value, 64, 1) for value in (own, near))
        mine = jnp.concatenate(
            [jnp.where(low, own, own_turned), jnp.where(low, own_turned, own)], axis=0
        )
        pairs = jnp.concatenate(
            [jnp.where(low, own, near_turned), jnp.where(low, own_turned, near)], axis=0
        )
        wide = plane_rows(plane, 64)
        visitors[wide, :] = pairs.astype(bf16)
        return (mine * pairs).astype(bf16)

    potentials = passes_there(density_of, table_ref, mixed_ref, kernel_ref, grid)
    fill = jnp.where(low_lanes(NG), fill_of(own_ref), fill_of(near_ref))
    for plane in range(HALF):
        owner_ref[plane_rows(plane, 64), :] = two_planes(own_ref, plane, low).astype(bf16)

    def backward(step, carry):
        for plane, potential in potentials(step):
            total = potential * (visitors[plane_rows(plane, 64), :].astype(f32) * fill)
            total = total + pltpu.roll(total, 64, 1)
            term_ref[plane_rows(plane, 32), :] = jnp.where(low, total[:32], total[32:])
        return carry

    lax.fori_loop(0, NG // SPAN, backward, 0, unroll=True)


def near_term(own, near, table, mixed, kernel):
    return pl.pallas_call(
        near_body,
        out_shape=(
            jax.ShapeDtypeStruct((HALF * NG, 128), jnp.bfloat16),
            jax.ShapeDtypeStruct((ROWS, 128), jnp.float32),
        ),
        in_specs=[VMEM] * 5,
        out_specs=(VMEM, VMEM),
        scratch_shapes=[
            pltpu.VMEM((NG * NG, 128), jnp.bfloat16),
            pltpu.VMEM((NG * PITCH, 128), jnp.float32),
        ],
        compiler_params=pltpu.CompilerParams(vmem_limit_bytes=24 * 1024 * 1024),
        cost_estimate=pl.CostEstimate(
            flops=NEAR_FLOPS, bytes_accessed=4 * 1024 * 1024, transcendentals=0
        ),
        name="near_term",
    )(own, near, table, mixed, kernel)


def exchange_body(
    far_ref, owner_ref, term_ref, trial_ref, table_ref, mixed_ref, halves_ref, kernel_ref,
    out_ref, visitors, grid, tiles, trial_left, left,
):
    f32, bf16 = jnp.float32, jnp.bfloat16
    low = low_lanes(HALF)
    trial_copy = pltpu.make_async_copy(trial_ref, out_ref.at[:, pl.ds(0, 16), :], trial_left)
    trial_copy.start()

    for step in range(HALF // SPAN):
        planes = [step * SPAN + part for part in range(SPAN)]
        densities = []
        for plane in planes:
            far = two_planes(far_ref, plane, low)
            wide = plane_rows(plane, 64)
            visitors[wide, :] = far.astype(bf16)
            densities.append((far * owner_ref[wide, :].astype(f32)).astype(bf16))
        values = dot(beside(densities), table_ref[...]).astype(bf16)
        values = dot(mixed_ref[...], values)
        for part, plane in enumerate(planes):
            grid[pitched(plane), :] = part_of(values, part)

    def crossed(value):
        return jnp.concatenate([value, pltpu.roll(value, 64, 1)], axis=0).astype(bf16)

    def joined(value):
        return jnp.where(low, value[:HALF], value[HALF:])

    for step in range(NG // SPAN):
        lines = [step * SPAN + part for part in range(SPAN)]
        rows = [pl.ds(line, HALF, stride=PITCH) for line in lines]
        values = dot(halves_ref[...], beside([crossed(grid[row, :]) for row in rows]))
        values = beside(
            [
                crossed(joined(part_of(values, part)) * joined(kernel_ref[line]))
                for part, line in enumerate(lines)
            ]
        )
        values = dot(halves_ref[...], values)
        for part, row in enumerate(rows):
            grid[row, :] = joined(part_of(values, part))

    fill = fill_of(far_ref)

    def tile_copies(step):
        copies = []
        for half in range(2):
            peers = pl.ds(step * 2 * SPAN + half * NG, 2 * SPAN)
            copies.append(
                pltpu.make_async_copy(
                    tiles.at[peers], out_ref.at[peers, pl.ds(16, 16), :], left.at[half, step]
                )
            )
        return copies

    for step in range(HALF // SPAN):
        planes = [step * SPAN + part for part in range(SPAN)]
        values = beside([grid[pitched(plane), :].astype(bf16) for plane in planes])
        values = dot(mixed_ref[...], values).astype(bf16)
        values = dot(values, table_ref[...])
        for part, plane in enumerate(planes):
            weight = visitors[plane_rows(plane, 64), :].astype(f32) * fill
            total = part_of(values, part) * weight
            turned = pltpu.roll(total, 64, 1)
            first = jnp.where(low, total[:HALF], turned[HALF:])
            second = jnp.where(low, turned[:HALF], total[HALF:])
            for index, value in ((plane, first), (plane + HALF, second)):
                value = value + term_ref[plane_rows(index, 32), :]
                tiles[pl.ds(2 * index, 2)] = value.astype(bf16).reshape(2, 16, 128)
        for copy in tile_copies(step):
            copy.start()
    trial_copy.wait()
    for step in range(HALF // SPAN):
        for copy in tile_copies(step):
            copy.wait()


def exchange_of(far, owner, term, trial, table, mixed, halves, kernel):
    return pl.pallas_call(
        exchange_body,
        out_shape=jax.ShapeDtypeStruct((128, 32, 128), jnp.bfloat16),
        in_specs=[VMEM] * 8,
        out_specs=pl.BlockSpec(memory_space=pltpu.HBM),
        scratch_shapes=[
            pltpu.VMEM((HALF * NG, 128), jnp.bfloat16),
            pltpu.VMEM((HALF * PITCH, 128), jnp.float32),
            pltpu.VMEM((128, 16, 128), jnp.bfloat16),
            pltpu.SemaphoreType.DMA,
            pltpu.SemaphoreType.DMA((2, HALF // SPAN)),
        ],
        compiler_params=pltpu.CompilerParams(vmem_limit_bytes=24 * 1024 * 1024),
        name="exchange",
    )(far, owner, term, trial, table, mixed, halves, kernel)


def unpack_body(tiles_ref, flat_ref, token_ref):
    def part(step, carry):
        columns = pl.ds(pl.multiple_of(step * 16384, 16384), 16384)
        tiles = [tiles_ref[pl.ds(step * 256 + peer * 32 + 16, 16), :] for peer in range(8)]
        value = jnp.concatenate(tiles, axis=0).astype(jnp.float32).reshape(1, 16384)
        flat_ref[0:1, columns] = value.astype(jnp.bfloat16)
        return carry

    lax.fori_loop(0, 16, part, 0)
    token_ref[...] = tiles_ref[pl.ds(0, 16), :]


def unpacked(tiles):
    return pl.pallas_call(
        unpack_body,
        out_shape=(
            jax.ShapeDtypeStruct((1, G), jnp.bfloat16),
            jax.ShapeDtypeStruct((16, 128), jnp.bfloat16),
        ),
        in_specs=[VMEM],
        out_specs=(VMEM, VMEM),
        compiler_params=pltpu.CompilerParams(vmem_limit_bytes=16 * 1024 * 1024),
        name="unpack",
    )(tiles)


def intersection_body(tiles_ref, token_ref, core_ref, lines_ref, mine_ref, other_ref, wide):
    bf16 = jnp.bfloat16
    for peer in range(128):
        wide[pl.ds(peer * WIDE, 32), :] = tiles_ref[pl.ds(peer * 32, 32), :].astype(jnp.float32)
    total = jnp.zeros((128, 128), jnp.float32)
    for line in range(16):
        trial = wide[pl.ds(line, 128, stride=WIDE), :].astype(bf16)
        value = wide[pl.ds(line + 16, 128, stride=WIDE), :].astype(bf16)
        lines_ref[pl.ds(line * 128, 128), :] = value
        total = total + lax.dot_general(
            trial, value, (((1,), (1,)), ((), ())), preferred_element_type=jnp.float32
        )
    total = total * (1.0 / math.sqrt(G))
    first = core_ref[0] == 0
    mine_ref[...] = jnp.where(first, total[:64], total[64:])
    other_ref[...] = jnp.where(first, total[64:], total[:64])


def intersection_of(tiles, token, core):
    half = jax.ShapeDtypeStruct((64, 128), jnp.float32)
    return pl.pallas_call(
        intersection_body,
        out_shape=(jax.ShapeDtypeStruct((ROWS, 128), jnp.bfloat16), half, half),
        in_specs=[VMEM, pl.BlockSpec(memory_space=pl.ANY), SMEM],
        out_specs=(VMEM, VMEM, VMEM),
        scratch_shapes=[pltpu.VMEM((128 * WIDE, 128), jnp.float32)],
        compiler_params=pltpu.CompilerParams(vmem_limit_bytes=16 * 1024 * 1024),
        name="intersection",
    )(tiles, token, core)


def projected_body(lines_ref, mine_ref, other_ref, core_ref, out_ref, result, left):
    first = core_ref[0] == 0
    mine, other = mine_ref[...].astype(jnp.float32), other_ref[...].astype(jnp.float32)
    table = jnp.concatenate(
        [jnp.where(first, mine, other), jnp.where(first, other, mine)], axis=0
    ).astype(jnp.bfloat16)

    def copy(part):
        columns = pl.ds(part * 512, 512)
        return pltpu.make_async_copy(result.at[:, columns], out_ref.at[:, columns], left.at[part])

    for part in range(4):
        for line in range(part * 4, part * 4 + 4):
            rows = pl.ds(line * 128, 128)
            value = dot(table, lines_ref[rows, :]) * (-1.0 / math.sqrt(128))
            result[:, rows] = value.astype(jnp.bfloat16)
        copy(part).start()
    for part in range(4):
        copy(part).wait()


def projected_of(lines, mine, other, core):
    return pl.pallas_call(
        projected_body,
        out_shape=jax.ShapeDtypeStruct((128, ROWS), jnp.bfloat16),
        in_specs=[VMEM, VMEM, VMEM, SMEM],
        out_specs=pl.BlockSpec(memory_space=pltpu.HBM),
        scratch_shapes=[
            pltpu.VMEM((128, ROWS), jnp.bfloat16),
            pltpu.SemaphoreType.DMA((4,)),
        ],
        compiler_params=pltpu.CompilerParams(vmem_limit_bytes=16 * 1024 * 1024),
        name="projected",
    )(lines, mine, other, core)


def from_far(value):
    count = lax.axis_size(BAND)
    pairs = [(i, (i - 1 if i % 2 == 0 else i + 1) % count) for i in range(count)]
    return lax.ppermute(value, BAND, pairs)


def swapped(value):
    return lax.ppermute(value, "core", [(0, 1), (1, 0)])


def summed_over(value, axes):
    peers = lax.axis_size(axes)
    copies = jnp.broadcast_to(value[None], (peers,) + value.shape)
    tiles = lax.all_to_all(copies, axes, 0, 0, tiled=True)
    return jnp.sum(tiles.astype(jnp.float32), axis=0).astype(jnp.bfloat16)


def local(orbitals, trial, occupations):
    own = packed_with_flag(orbitals, occupations)
    table, mixed, halves = (jnp.asarray(value) for value in constants())
    kernel = screened_kernel(own)
    far, near = from_far(own), swapped(own)
    trial_rows = packed_after(trial, own)
    owner, term = near_term(own, near, table, mixed, kernel)
    trial_tiles = trial_rows.reshape(128, 16, 128)
    both = exchange_of(far, owner, term, trial_tiles, table, mixed, halves, kernel)
    tiles = lax.all_to_all(both, BAND, 0, 0, tiled=True)
    flat, token = unpacked(both.reshape(2 * ROWS, 128))
    core = lax.axis_index("core").astype(jnp.int32).reshape(1)
    lines, mine, other = intersection_of(tiles.reshape(2 * ROWS, 128), token, core)
    half = (mine + swapped(other)).astype(jnp.bfloat16)
    half = summed_over(half, ("y", "x"))
    half = summed_over(half, "z")
    return flat, projected_of(lines, half, swapped(half), core)


def solution(mesh):
    finer = Mesh(mesh.devices.reshape(mesh.shape["spin"], 4, 2, 8, 2), SPIN_BAND)
    return jax.shard_map(
        local,
        mesh=finer,
        in_specs=(P(SPIN_BAND, None), P(SPIN_BAND, None), P(SPIN_BAND)),
        out_specs=(P(SPIN_BAND, None), P("spin", BAND)),
        check_vma=False,
    )
```

```python
import math

import jax
import jax.numpy as jnp
import ml_dtypes
import numpy as np
from jax import lax
from jax.experimental import pallas as pl
from jax.experimental.pallas import tpu as pltpu
from jax.sharding import Mesh
from jax.sharding import PartitionSpec as P

NG = 64
G = NG**3
ROWS = G // 128
FRACTION = 0.25
OMEGA = 1.0
BAND = ("y", "x", "z", "core")
SPIN_BAND = ("spin",) + BAND
SLABS = ("z", "y", "x", "core")
ORDER = np.concatenate([np.arange(0, NG, 2), np.arange(1, NG, 2)])
STEP = 4
SPAN = 2 * STEP
PITCH = 72
WIDE = 40
HALF = NG // 2
NEAR_FLOPS = 10**10
VMEM = pl.BlockSpec(memory_space=pltpu.VMEM)
SMEM = pl.BlockSpec(memory_space=pltpu.SMEM)


def cas_table():
    indices = np.arange(NG)
    phases = (indices[:, None] * indices[None, :] % NG) * (2.0 * math.pi / NG)
    return (np.cos(phases) + np.sin(phases)).astype(np.float32).astype(ml_dtypes.bfloat16)


def squared_modes(index):
    modes = jnp.where(2 * index < NG, index, index - NG)
    wavenum = modes.astype(jnp.float32) * (2.0 * math.pi / NG)
    return wavenum * wavenum


def screened_body(earlier_ref, kernel_ref):
    first = squared_modes(lax.broadcasted_iota(jnp.int32, (NG, 128), 0))
    third = squared_modes(lax.rem(lax.broadcasted_iota(jnp.int32, (NG, 128), 1), NG))

    def one_line(line, carry):
        second = 2 * lax.rem(line, NG // 2) + lax.div(line, NG // 2)
        norm_sq = first + squared_modes(jnp.full((NG, 128), second, jnp.int32)) + third
        bounded = jnp.where(norm_sq > 0, norm_sq, 1.0)
        screened = jnp.where(
            norm_sq > 0,
            4.0 * math.pi / bounded * (1.0 - jnp.exp(-bounded / (4.0 * OMEGA * OMEGA))),
            math.pi / (OMEGA * OMEGA),
        )
        kernel_ref[line] = screened * (1.0 / G)
        return carry

    lax.fori_loop(0, NG, one_line, 0, unroll=2)


def screened_kernel(earlier):
    return pl.pallas_call(
        screened_body,
        out_shape=jax.ShapeDtypeStruct((NG, NG, 128), jnp.float32),
        in_specs=[pl.BlockSpec(memory_space=pl.ANY)],
        out_specs=VMEM,
        compiler_params=pltpu.CompilerParams(vmem_limit_bytes=16 * 1024 * 1024),
        cost_estimate=pl.CostEstimate(
            flops=NEAR_FLOPS, bytes_accessed=2 * 1024 * 1024, transcendentals=0
        ),
        name="screened_kernel",
    )(earlier)


def repeated(table):
    return np.kron(np.eye(STEP, dtype=np.float32), table.astype(np.float32)).astype(table.dtype)


def constants():
    table = cas_table()
    mixed = table[ORDER][:, ORDER]
    crossed = np.concatenate([table[HALF:, HALF:], table[HALF:, :HALF]], axis=1)
    halves = np.concatenate([table[:HALF], crossed], axis=0)
    return repeated(table), repeated(mixed), repeated(halves)


def dot(left, right):
    return lax.dot_general(
        left, right, (((1,), (0,)), ((), ())), preferred_element_type=jnp.float32
    )


def pack_body(flat_ref, tiles_ref):
    def part(step, carry):
        columns = pl.ds(pl.multiple_of(step * 16384, 16384), 16384)
        rows = pl.ds(pl.multiple_of(step * 128, 128), 128)
        tiles_ref[rows, :] = flat_ref[0:1, columns].reshape(128, 128)
        return carry

    lax.fori_loop(0, 16, part, 0)


def pack_flagged_body(flat_ref, flag_ref, tiles_ref):
    pack_body(flat_ref, tiles_ref)
    flag = jnp.broadcast_to(flag_ref[...], (16, 128))
    tiles_ref[pl.ds(ROWS, 16), :] = flag.astype(jnp.float32).astype(jnp.bfloat16)


def pack_after_body(flat_ref, earlier_ref, tiles_ref):
    pack_body(flat_ref, tiles_ref)


def packed_after(flat, earlier):
    return pl.pallas_call(
        pack_after_body,
        out_shape=jax.ShapeDtypeStruct((ROWS, 128), jnp.bfloat16),
        in_specs=[VMEM, pl.BlockSpec(memory_space=pl.ANY)],
        out_specs=VMEM,
        compiler_params=pltpu.CompilerParams(vmem_limit_bytes=16 * 1024 * 1024),
        name="pack",
    )(flat, earlier)


def again_body(tiles_ref, again_ref):
    again_ref[...] = tiles_ref[...]


def copied(tiles):
    return pl.pallas_call(
        again_body,
        out_shape=jax.ShapeDtypeStruct(tiles.shape, tiles.dtype),
        in_specs=[VMEM],
        out_specs=VMEM,
        compiler_params=pltpu.CompilerParams(vmem_limit_bytes=16 * 1024 * 1024),
        name="again",
    )(tiles)


def packed_with_flag(flat, flag):
    return pl.pallas_call(
        pack_flagged_body,
        out_shape=jax.ShapeDtypeStruct((ROWS + 16, 128), jnp.bfloat16),
        in_specs=[VMEM, VMEM],
        out_specs=VMEM,
        compiler_params=pltpu.CompilerParams(vmem_limit_bytes=16 * 1024 * 1024),
        name="pack_flagged",
    )(flat, flag.reshape(1, 1))


def plane_rows(plane, height):
    if isinstance(plane, int):
        return pl.ds(plane * height, height)
    return pl.ds(pl.multiple_of(plane * height, height), height)


def pitched(plane):
    if isinstance(plane, int):
        return pl.ds(plane * PITCH, NG)
    return pl.ds(pl.multiple_of(plane * PITCH, 8), NG)


def beside(parts):
    return jnp.concatenate(
        [jnp.concatenate(parts[:STEP], axis=0), jnp.concatenate(parts[STEP:], axis=0)], axis=1
    )


def part_of(values, part):
    rows = slice(part % STEP * NG, part % STEP * NG + NG)
    return values[rows, :128] if part < STEP else values[rows, 128:]


def passes_there(density_of, table_ref, mixed_ref, kernel_ref, grid):
    bf16 = jnp.bfloat16

    def forward(step, carry):
        planes = [step * SPAN + part for part in range(SPAN)]
        values = beside([density_of(plane) for plane in planes])
        values = dot(values, table_ref[...]).astype(bf16)
        values = dot(mixed_ref[...], values)
        for part, plane in enumerate(planes):
            grid[pitched(plane), :] = part_of(values, part)
        return carry

    lax.fori_loop(0, NG // SPAN, forward, 0, unroll=True)

    def across(step, carry):
        lines = [step * SPAN + part for part in range(SPAN)]
        rows = [pl.ds(line, NG, stride=PITCH) for line in lines]
        values = beside([grid[row, :].astype(bf16) for row in rows])
        values = dot(table_ref[...], values)
        values = (values * beside([kernel_ref[line] for line in lines])).astype(bf16)
        values = dot(table_ref[...], values)
        for part, row in enumerate(rows):
            grid[row, :] = part_of(values, part)
        return carry

    lax.fori_loop(0, NG // SPAN, across, 0, unroll=True)

    def potentials(step):
        planes = [step * SPAN + part for part in range(SPAN)]
        values = beside([grid[pitched(plane), :].astype(bf16) for plane in planes])
        values = dot(mixed_ref[...], values).astype(bf16)
        values = dot(values, table_ref[...])
        return [(plane, part_of(values, part)) for part, plane in enumerate(planes)]

    return potentials


def fill_of(ref):
    return ref[pl.ds(ROWS, 16), :].astype(jnp.float32)[:1] * -FRACTION


def two_planes(ref, plane, low):
    first, second = (
        ref[plane_rows(index, 32), :].astype(jnp.float32) for index in (plane, plane + HALF)
    )
    first_turned, second_turned = (pltpu.roll(value, 64, 1) for value in (first, second))
    return jnp.concatenate(
        [jnp.where(low, first, second_turned), jnp.where(low, first_turned, second)], axis=0
    )


def low_lanes(height):
    return lax.broadcasted_iota(jnp.int32, (height, 128), 1) < 64


def near_body(
    own_ref, near_ref, table_ref, mixed_ref, kernel_ref, owner_ref, term_ref, visitors, grid
):
    f32, bf16 = jnp.float32, jnp.bfloat16
    low = low_lanes(NG // 2)

    def density_of(plane):
        own, near = (ref[plane_rows(plane, 32), :].astype(f32) for ref in (own_ref, near_ref))
        own_turned, near_turned = (pltpu.roll(value, 64, 1) for value in (own, near))
        mine = jnp.concatenate(
            [jnp.where(low, own, own_turned), jnp.where(low, own_turned, own)], axis=0
        )
        pairs = jnp.concatenate(
            [jnp.where(low, own, near_turned), jnp.where(low, own_turned, near)], axis=0
        )
        wide = plane_rows(plane, 64)
        visitors[wide, :] = pairs.astype(bf16)
        return (mine * pairs).astype(bf16)

    potentials = passes_there(density_of, table_ref, mixed_ref, kernel_ref, grid)
    fill = jnp.where(low_lanes(NG), fill_of(own_ref), fill_of(near_ref))
    for plane in range(HALF):
        owner_ref[plane_rows(plane, 64), :] = two_planes(own_ref, plane, low).astype(bf16)

    def backward(step, carry):
        for plane, potential in potentials(step):
            total = potential * (visitors[plane_rows(plane, 64), :].astype(f32) * fill)
            total = total + pltpu.roll(total, 64, 1)
            term_ref[plane_rows(plane, 32), :] = jnp.where(low, total[:32], total[32:])
        return carry

    lax.fori_loop(0, NG // SPAN, backward, 0, unroll=True)


def near_term(own, near, table, mixed, kernel):
    return pl.pallas_call(
        near_body,
        out_shape=(
            jax.ShapeDtypeStruct((HALF * NG, 128), jnp.bfloat16),
            jax.ShapeDtypeStruct((ROWS, 128), jnp.float32),
        ),
        in_specs=[VMEM] * 5,
        out_specs=(VMEM, VMEM),
        scratch_shapes=[
            pltpu.VMEM((NG * NG, 128), jnp.bfloat16),
            pltpu.VMEM((NG * PITCH, 128), jnp.float32),
        ],
        compiler_params=pltpu.CompilerParams(vmem_limit_bytes=24 * 1024 * 1024),
        cost_estimate=pl.CostEstimate(
            flops=NEAR_FLOPS, bytes_accessed=4 * 1024 * 1024, transcendentals=0
        ),
        name="near_term",
    )(own, near, table, mixed, kernel)


def exchange_body(
    far_ref, owner_ref, term_ref, trial_ref, table_ref, mixed_ref, halves_ref, kernel_ref,
    out_ref, visitors, grid, tiles, trial_left, left,
):
    f32, bf16 = jnp.float32, jnp.bfloat16
    low = low_lanes(HALF)
    trial_copies = [
        pltpu.make_async_copy(
            trial_ref.at[row], out_ref.at[:, row, :, pl.ds(0, 16), :], trial_left.at[row]
        )
        for row in range(8)
    ]
    for copy in trial_copies:
        copy.start()

    for step in range(HALF // SPAN):
        planes = [step * SPAN + part for part in range(SPAN)]
        densities = []
        for plane in planes:
            far = two_planes(far_ref, plane, low)
            wide = plane_rows(plane, 64)
            visitors[wide, :] = far.astype(bf16)
            densities.append((far * owner_ref[wide, :].astype(f32)).astype(bf16))
        values = dot(beside(densities), table_ref[...]).astype(bf16)
        values = dot(mixed_ref[...], values)
        for part, plane in enumerate(planes):
            grid[pitched(plane), :] = part_of(values, part)

    def crossed(value):
        return jnp.concatenate([value, pltpu.roll(value, 64, 1)], axis=0).astype(bf16)

    def joined(value):
        return jnp.where(low, value[:HALF], value[HALF:])

    for step in range(NG // SPAN):
        lines = [step * SPAN + part for part in range(SPAN)]
        rows = [pl.ds(line, HALF, stride=PITCH) for line in lines]
        values = dot(halves_ref[...], beside([crossed(grid[row, :]) for row in rows]))
        values = beside(
            [
                crossed(joined(part_of(values, part)) * joined(kernel_ref[line]))
                for part, line in enumerate(lines)
            ]
        )
        values = dot(halves_ref[...], values)
        for part, row in enumerate(rows):
            grid[row, :] = joined(part_of(values, part))

    fill = fill_of(far_ref)

    def tile_copies(step):
        return [
            pltpu.make_async_copy(
                tiles.at[:, row], out_ref.at[:, row, :, pl.ds(16, 16), :], left.at[row]
            )
            for row in (step, step + 4)
        ]

    for step in range(HALF // SPAN):
        planes = [step * SPAN + part for part in range(SPAN)]
        values = beside([grid[pitched(plane), :].astype(bf16) for plane in planes])
        values = dot(mixed_ref[...], values).astype(bf16)
        values = dot(values, table_ref[...])
        for part, plane in enumerate(planes):
            weight = visitors[plane_rows(plane, 64), :].astype(f32) * fill
            total = part_of(values, part) * weight
            turned = pltpu.roll(total, 64, 1)
            first = jnp.where(low, total[:HALF], turned[HALF:])
            second = jnp.where(low, turned[:HALF], total[HALF:])
            for index, value in ((plane, first), (plane + HALF, second)):
                value = value + term_ref[plane_rows(index, 32), :]
                tiles[index % 8, index // 8] = value.astype(bf16).reshape(2, 16, 128)
        for copy in tile_copies(step):
            copy.start()
    for copy in trial_copies:
        copy.wait()
    for step in range(HALF // SPAN):
        for copy in tile_copies(step):
            copy.wait()


def exchange_of(far, owner, term, trial, table, mixed, halves, kernel):
    return pl.pallas_call(
        exchange_body,
        out_shape=jax.ShapeDtypeStruct((8, 8, 2, 32, 128), jnp.bfloat16),
        in_specs=[VMEM] * 8,
        out_specs=pl.BlockSpec(memory_space=pltpu.HBM),
        scratch_shapes=[
            pltpu.VMEM((HALF * NG, 128), jnp.bfloat16),
            pltpu.VMEM((HALF * PITCH, 128), jnp.float32),
            pltpu.VMEM((8, 8, 2, 16, 128), jnp.bfloat16),
            pltpu.SemaphoreType.DMA((8,)),
            pltpu.SemaphoreType.DMA((8,)),
        ],
        compiler_params=pltpu.CompilerParams(vmem_limit_bytes=24 * 1024 * 1024),
        name="exchange",
    )(far, owner, term, trial, table, mixed, halves, kernel)


def unpack_body(tiles_ref, flat_ref, token_ref):
    def part(step, carry):
        columns = pl.ds(pl.multiple_of(step * 16384, 16384), 16384)
        row, first = lax.div(step, 2), 4 * lax.rem(step, 2)
        tiles = [
            tiles_ref[first + peer // 2, row, peer % 2, pl.ds(16, 16), :] for peer in range(8)
        ]
        value = jnp.concatenate(tiles, axis=0).astype(jnp.float32).reshape(1, 16384)
        flat_ref[0:1, columns] = value.astype(jnp.bfloat16)
        return carry

    lax.fori_loop(0, 16, part, 0)
    token_ref[...] = tiles_ref[0, 0, 0, pl.ds(0, 16), :]


def unpacked(tiles):
    return pl.pallas_call(
        unpack_body,
        out_shape=(
            jax.ShapeDtypeStruct((1, G), jnp.bfloat16),
            jax.ShapeDtypeStruct((16, 128), jnp.bfloat16),
        ),
        in_specs=[VMEM],
        out_specs=(VMEM, VMEM),
        compiler_params=pltpu.CompilerParams(vmem_limit_bytes=16 * 1024 * 1024),
        name="unpack",
    )(tiles)


def intersection_body(tiles_ref, token_ref, core_ref, lines_ref, mine_ref, other_ref, wide):
    bf16 = jnp.bfloat16
    for peer in range(128):
        orbital = (peer // 2 % 8 * 8 + peer // 16) * 2 + peer % 2
        rows = pl.ds(orbital * WIDE, 32)
        wide[rows, :] = tiles_ref[pl.ds(peer * 32, 32), :].astype(jnp.float32)
    total = jnp.zeros((128, 128), jnp.float32)
    for line in range(16):
        trial = wide[pl.ds(line, 128, stride=WIDE), :].astype(bf16)
        value = wide[pl.ds(line + 16, 128, stride=WIDE), :].astype(bf16)
        lines_ref[pl.ds(line * 128, 128), :] = value
        total = total + lax.dot_general(
            trial, value, (((1,), (1,)), ((), ())), preferred_element_type=jnp.float32
        )
    total = total * (1.0 / math.sqrt(G))
    first = core_ref[0] == 0
    mine_ref[...] = jnp.where(first, total[:64], total[64:])
    other_ref[...] = jnp.where(first, total[64:], total[:64])


def intersection_of(tiles, token, core):
    half = jax.ShapeDtypeStruct((64, 128), jnp.float32)
    return pl.pallas_call(
        intersection_body,
        out_shape=(jax.ShapeDtypeStruct((ROWS, 128), jnp.bfloat16), half, half),
        in_specs=[VMEM, pl.BlockSpec(memory_space=pl.ANY), SMEM],
        out_specs=(VMEM, VMEM, VMEM),
        scratch_shapes=[pltpu.VMEM((128 * WIDE, 128), jnp.float32)],
        compiler_params=pltpu.CompilerParams(vmem_limit_bytes=16 * 1024 * 1024),
        name="intersection",
    )(tiles, token, core)


def projected_body(lines_ref, mine_ref, other_ref, core_ref, out_ref, result, left):
    first = core_ref[0] == 0
    mine, other = mine_ref[...].astype(jnp.float32), other_ref[...].astype(jnp.float32)
    table = jnp.concatenate(
        [jnp.where(first, mine, other), jnp.where(first, other, mine)], axis=0
    ).astype(jnp.bfloat16)

    def copy(part):
        columns = pl.ds(part * 512, 512)
        return pltpu.make_async_copy(result.at[:, columns], out_ref.at[:, columns], left.at[part])

    for part in range(4):
        for line in range(part * 4, part * 4 + 4):
            rows = pl.ds(line * 128, 128)
            value = dot(table, lines_ref[rows, :]) * (-1.0 / math.sqrt(128))
            result[:, rows] = value.astype(jnp.bfloat16)
        copy(part).start()
    for part in range(4):
        copy(part).wait()


def projected_of(lines, mine, other, core):
    return pl.pallas_call(
        projected_body,
        out_shape=jax.ShapeDtypeStruct((128, ROWS), jnp.bfloat16),
        in_specs=[VMEM, VMEM, VMEM, SMEM],
        out_specs=pl.BlockSpec(memory_space=pltpu.HBM),
        scratch_shapes=[
            pltpu.VMEM((128, ROWS), jnp.bfloat16),
            pltpu.SemaphoreType.DMA((4,)),
        ],
        compiler_params=pltpu.CompilerParams(vmem_limit_bytes=16 * 1024 * 1024),
        name="projected",
    )(lines, mine, other, core)


def from_far(value):
    count = lax.axis_size(BAND)
    pairs = [(i, (i - 1 if i % 2 == 0 else i + 1) % count) for i in range(count)]
    return lax.ppermute(value, BAND, pairs)


def swapped(value):
    return lax.ppermute(value, "core", [(0, 1), (1, 0)])


def summed_over(value, axes):
    peers = lax.axis_size(axes)
    copies = jnp.broadcast_to(value[None], (peers,) + value.shape)
    tiles = lax.all_to_all(copies, axes, 0, 0, tiled=True)
    return jnp.sum(tiles.astype(jnp.float32), axis=0).astype(jnp.bfloat16)


def local(orbitals, trial, occupations):
    own = packed_with_flag(orbitals, occupations)
    far = from_far(own)
    again = copied(own)
    near = swapped(again)
    trial_rows = packed_after(trial, again)
    table, mixed, halves = (jnp.asarray(value) for value in constants())
    kernel = screened_kernel(again)
    owner, term = near_term(own, near, table, mixed, kernel)
    trial_tiles = trial_rows.reshape(8, 8, 2, 16, 128)
    both = exchange_of(far, owner, term, trial_tiles, table, mixed, halves, kernel)
    tiles = lax.all_to_all(both.reshape(128, 32, 128), SLABS, 0, 0, tiled=True)
    flat, token = unpacked(both)
    core = lax.axis_index("core").astype(jnp.int32).reshape(1)
    lines, mine, other = intersection_of(tiles.reshape(2 * ROWS, 128), token, core)
    half = (mine + swapped(other)).astype(jnp.bfloat16)
    half = summed_over(half, ("x", "y"))
    half = summed_over(half, "z")
    return flat, projected_of(lines, half, swapped(half), core)


def solution(mesh):
    finer = Mesh(mesh.devices.reshape(mesh.shape["spin"], 4, 2, 8, 2), SPIN_BAND)
    return jax.shard_map(
        local,
        mesh=finer,
        in_specs=(P(SPIN_BAND, None), P(SPIN_BAND, None), P(SPIN_BAND)),
        out_specs=(P(SPIN_BAND, None), P("spin", BAND)),
        check_vma=False,
    )
```

```python
import math

import jax
import jax.numpy as jnp
import ml_dtypes
import numpy as np
from jax import lax
from jax.experimental import pallas as pl
from jax.experimental.pallas import tpu as pltpu
from jax.sharding import Mesh
from jax.sharding import PartitionSpec as P

NG = 64
G = NG**3
ROWS = G // 128
FRACTION = 0.25
OMEGA = 1.0
BAND = ("y", "x", "z", "core")
SPIN_BAND = ("spin",) + BAND
ORDER = np.concatenate([np.arange(0, NG, 2), np.arange(1, NG, 2)])
STEP = 4
SPAN = 2 * STEP
PITCH = 72
WIDE = 40
HALF = NG // 2
NEAR_FLOPS = 10**10
VMEM = pl.BlockSpec(memory_space=pltpu.VMEM)
SMEM = pl.BlockSpec(memory_space=pltpu.SMEM)


def cas_table():
    indices = np.arange(NG)
    phases = (indices[:, None] * indices[None, :] % NG) * (2.0 * math.pi / NG)
    return (np.cos(phases) + np.sin(phases)).astype(np.float32).astype(ml_dtypes.bfloat16)


def squared_modes(index):
    modes = jnp.where(2 * index < NG, index, index - NG)
    wavenum = modes.astype(jnp.float32) * (2.0 * math.pi / NG)
    return wavenum * wavenum


def screened_body(earlier_ref, kernel_ref):
    first = squared_modes(lax.broadcasted_iota(jnp.int32, (NG, 128), 0))
    third = squared_modes(lax.rem(lax.broadcasted_iota(jnp.int32, (NG, 128), 1), NG))

    def one_line(line, carry):
        second = 2 * lax.rem(line, NG // 2) + lax.div(line, NG // 2)
        norm_sq = first + squared_modes(jnp.full((NG, 128), second, jnp.int32)) + third
        bounded = jnp.where(norm_sq > 0, norm_sq, 1.0)
        screened = jnp.where(
            norm_sq > 0,
            4.0 * math.pi / bounded * (1.0 - jnp.exp(-bounded / (4.0 * OMEGA * OMEGA))),
            math.pi / (OMEGA * OMEGA),
        )
        kernel_ref[line] = screened * (1.0 / G)
        return carry

    lax.fori_loop(0, NG, one_line, 0, unroll=2)


def screened_kernel(earlier):
    return pl.pallas_call(
        screened_body,
        out_shape=jax.ShapeDtypeStruct((NG, NG, 128), jnp.float32),
        in_specs=[pl.BlockSpec(memory_space=pl.ANY)],
        out_specs=VMEM,
        compiler_params=pltpu.CompilerParams(vmem_limit_bytes=16 * 1024 * 1024),
        cost_estimate=pl.CostEstimate(
            flops=NEAR_FLOPS, bytes_accessed=2 * 1024 * 1024, transcendentals=0
        ),
        name="screened_kernel",
    )(earlier)


def repeated(table):
    return np.kron(np.eye(STEP, dtype=np.float32), table.astype(np.float32)).astype(table.dtype)


def constants():
    table = cas_table()
    mixed = table[ORDER][:, ORDER]
    crossed = np.concatenate([table[HALF:, HALF:], table[HALF:, :HALF]], axis=1)
    halves = np.concatenate([table[:HALF], crossed], axis=0)
    return repeated(table), repeated(mixed), repeated(halves)


def dot(left, right):
    return lax.dot_general(
        left, right, (((1,), (0,)), ((), ())), preferred_element_type=jnp.float32
    )


def pack_body(flat_ref, tiles_ref):
    def part(step, carry):
        columns = pl.ds(pl.multiple_of(step * 16384, 16384), 16384)
        rows = pl.ds(pl.multiple_of(step * 128, 128), 128)
        tiles_ref[rows, :] = flat_ref[0:1, columns].reshape(128, 128)
        return carry

    lax.fori_loop(0, 16, part, 0)


def pack_flagged_body(flat_ref, flag_ref, tiles_ref):
    pack_body(flat_ref, tiles_ref)
    flag = jnp.broadcast_to(flag_ref[...], (16, 128))
    tiles_ref[pl.ds(ROWS, 16), :] = flag.astype(jnp.float32).astype(jnp.bfloat16)


def pack_after_body(flat_ref, earlier_ref, both_ref):
    both_ref[...] = flat_ref[...].reshape(256, 128).reshape(16, 16, 128)


def packed_after(flat, earlier):
    return pl.pallas_call(
        pack_after_body,
        grid=(8,),
        out_shape=jax.ShapeDtypeStruct((128, 32, 128), jnp.bfloat16),
        in_specs=[
            pl.BlockSpec((1, G // 8), lambda part: (0, part)),
            pl.BlockSpec(memory_space=pl.ANY),
        ],
        out_specs=pl.BlockSpec((16, 16, 128), lambda part: (part, 0, 0)),
        compiler_params=pltpu.CompilerParams(vmem_limit_bytes=16 * 1024 * 1024),
        name="pack",
    )(flat, earlier)


def again_body(tiles_ref, again_ref):
    again_ref[...] = tiles_ref[...]


def copied(tiles):
    return pl.pallas_call(
        again_body,
        out_shape=jax.ShapeDtypeStruct(tiles.shape, tiles.dtype),
        in_specs=[VMEM],
        out_specs=VMEM,
        compiler_params=pltpu.CompilerParams(vmem_limit_bytes=16 * 1024 * 1024),
        name="again",
    )(tiles)


def packed_with_flag(flat, flag):
    return pl.pallas_call(
        pack_flagged_body,
        out_shape=jax.ShapeDtypeStruct((ROWS + 16, 128), jnp.bfloat16),
        in_specs=[VMEM, VMEM],
        out_specs=VMEM,
        compiler_params=pltpu.CompilerParams(vmem_limit_bytes=16 * 1024 * 1024),
        name="pack_flagged",
    )(flat, flag.reshape(1, 1))


def plane_rows(plane, height):
    if isinstance(plane, int):
        return pl.ds(plane * height, height)
    return pl.ds(pl.multiple_of(plane * height, height), height)


def pitched(plane):
    if isinstance(plane, int):
        return pl.ds(plane * PITCH, NG)
    return pl.ds(pl.multiple_of(plane * PITCH, 8), NG)


def beside(parts):
    return jnp.concatenate(
        [jnp.concatenate(parts[:STEP], axis=0), jnp.concatenate(parts[STEP:], axis=0)], axis=1
    )


def part_of(values, part):
    rows = slice(part % STEP * NG, part % STEP * NG + NG)
    return values[rows, :128] if part < STEP else values[rows, 128:]


def passes_there(density_of, table_ref, mixed_ref, kernel_ref, grid):
    bf16 = jnp.bfloat16

    def forward(step, carry):
        planes = [step * SPAN + part for part in range(SPAN)]
        values = beside([density_of(plane) for plane in planes])
        values = dot(values, table_ref[...]).astype(bf16)
        values = dot(mixed_ref[...], values)
        for part, plane in enumerate(planes):
            grid[pitched(plane), :] = part_of(values, part)
        return carry

    lax.fori_loop(0, NG // SPAN, forward, 0, unroll=True)

    def across(step, carry):
        lines = [step * SPAN + part for part in range(SPAN)]
        rows = [pl.ds(line, NG, stride=PITCH) for line in lines]
        values = beside([grid[row, :].astype(bf16) for row in rows])
        values = dot(table_ref[...], values)
        values = (values * beside([kernel_ref[line] for line in lines])).astype(bf16)
        values = dot(table_ref[...], values)
        for part, row in enumerate(rows):
            grid[row, :] = part_of(values, part)
        return carry

    lax.fori_loop(0, NG // SPAN, across, 0, unroll=True)

    def potentials(step):
        planes = [step * SPAN + part for part in range(SPAN)]
        values = beside([grid[pitched(plane), :].astype(bf16) for plane in planes])
        values = dot(mixed_ref[...], values).astype(bf16)
        values = dot(values, table_ref[...])
        return [(plane, part_of(values, part)) for part, plane in enumerate(planes)]

    return potentials


def fill_of(ref):
    return ref[pl.ds(ROWS, 16), :].astype(jnp.float32)[:1] * -FRACTION


def two_planes(ref, plane, low):
    first, second = (
        ref[plane_rows(index, 32), :].astype(jnp.float32) for index in (plane, plane + HALF)
    )
    first_turned, second_turned = (pltpu.roll(value, 64, 1) for value in (first, second))
    return jnp.concatenate(
        [jnp.where(low, first, second_turned), jnp.where(low, first_turned, second)], axis=0
    )


def low_lanes(height):
    return lax.broadcasted_iota(jnp.int32, (height, 128), 1) < 64


def near_body(
    own_ref, near_ref, table_ref, mixed_ref, kernel_ref, owner_ref, term_ref, visitors, grid
):
    f32, bf16 = jnp.float32, jnp.bfloat16
    low = low_lanes(NG // 2)

    def density_of(plane):
        own, near = (ref[plane_rows(plane, 32), :].astype(f32) for ref in (own_ref, near_ref))
        own_turned, near_turned = (pltpu.roll(value, 64, 1) for value in (own, near))
        mine = jnp.concatenate(
            [jnp.where(low, own, own_turned), jnp.where(low, own_turned, own)], axis=0
        )
        pairs = jnp.concatenate(
            [jnp.where(low, own, near_turned), jnp.where(low, own_turned, near)], axis=0
        )
        wide = plane_rows(plane, 64)
        visitors[wide, :] = pairs.astype(bf16)
        return (mine * pairs).astype(bf16)

    potentials = passes_there(density_of, table_ref, mixed_ref, kernel_ref, grid)
    fill = jnp.where(low_lanes(NG), fill_of(own_ref), fill_of(near_ref))
    for plane in range(HALF):
        owner_ref[plane_rows(plane, 64), :] = two_planes(own_ref, plane, low).astype(bf16)

    def backward(step, carry):
        for plane, potential in potentials(step):
            total = potential * (visitors[plane_rows(plane, 64), :].astype(f32) * fill)
            total = total + pltpu.roll(total, 64, 1)
            term_ref[plane_rows(plane, 32), :] = jnp.where(low, total[:32], total[32:])
        return carry

    lax.fori_loop(0, NG // SPAN, backward, 0, unroll=True)


def near_term(own, near, table, mixed, kernel):
    return pl.pallas_call(
        near_body,
        out_shape=(
            jax.ShapeDtypeStruct((HALF * NG, 128), jnp.bfloat16),
            jax.ShapeDtypeStruct((ROWS, 128), jnp.float32),
        ),
        in_specs=[VMEM] * 5,
        out_specs=(VMEM, VMEM),
        scratch_shapes=[
            pltpu.VMEM((NG * NG, 128), jnp.bfloat16),
            pltpu.VMEM((NG * PITCH, 128), jnp.float32),
        ],
        compiler_params=pltpu.CompilerParams(vmem_limit_bytes=24 * 1024 * 1024),
        cost_estimate=pl.CostEstimate(
            flops=NEAR_FLOPS, bytes_accessed=4 * 1024 * 1024, transcendentals=0
        ),
        name="near_term",
    )(own, near, table, mixed, kernel)


def exchange_body(
    far_ref, owner_ref, term_ref, both_ref, table_ref, mixed_ref, halves_ref, kernel_ref,
    out_ref, visitors, grid, tiles, left,
):
    f32, bf16 = jnp.float32, jnp.bfloat16
    low = low_lanes(HALF)

    for step in range(HALF // SPAN):
        planes = [step * SPAN + part for part in range(SPAN)]
        densities = []
        for plane in planes:
            far = two_planes(far_ref, plane, low)
            wide = plane_rows(plane, 64)
            visitors[wide, :] = far.astype(bf16)
            densities.append((far * owner_ref[wide, :].astype(f32)).astype(bf16))
        values = dot(beside(densities), table_ref[...]).astype(bf16)
        values = dot(mixed_ref[...], values)
        for part, plane in enumerate(planes):
            grid[pitched(plane), :] = part_of(values, part)

    def crossed(value):
        return jnp.concatenate([value, pltpu.roll(value, 64, 1)], axis=0).astype(bf16)

    def joined(value):
        return jnp.where(low, value[:HALF], value[HALF:])

    for step in range(NG // SPAN):
        lines = [step * SPAN + part for part in range(SPAN)]
        rows = [pl.ds(line, HALF, stride=PITCH) for line in lines]
        values = dot(halves_ref[...], beside([crossed(grid[row, :]) for row in rows]))
        values = beside(
            [
                crossed(joined(part_of(values, part)) * joined(kernel_ref[line]))
                for part, line in enumerate(lines)
            ]
        )
        values = dot(halves_ref[...], values)
        for part, row in enumerate(rows):
            grid[row, :] = joined(part_of(values, part))

    fill = fill_of(far_ref)

    def tile_copies(step):
        copies = []
        for half in range(2):
            peers = pl.ds(step * 2 * SPAN + half * NG, 2 * SPAN)
            copies.append(
                pltpu.make_async_copy(
                    tiles.at[peers], out_ref.at[peers, pl.ds(16, 16), :], left.at[half, step]
                )
            )
        return copies

    for step in range(HALF // SPAN):
        planes = [step * SPAN + part for part in range(SPAN)]
        values = beside([grid[pitched(plane), :].astype(bf16) for plane in planes])
        values = dot(mixed_ref[...], values).astype(bf16)
        values = dot(values, table_ref[...])
        for part, plane in enumerate(planes):
            weight = visitors[plane_rows(plane, 64), :].astype(f32) * fill
            total = part_of(values, part) * weight
            turned = pltpu.roll(total, 64, 1)
            first = jnp.where(low, total[:HALF], turned[HALF:])
            second = jnp.where(low, turned[:HALF], total[HALF:])
            for index, value in ((plane, first), (plane + HALF, second)):
                value = value + term_ref[plane_rows(index, 32), :]
                tiles[pl.ds(2 * index, 2)] = value.astype(bf16).reshape(2, 16, 128)
        for copy in tile_copies(step):
            copy.start()
    for step in range(HALF // SPAN):
        for copy in tile_copies(step):
            copy.wait()


def exchange_of(far, owner, term, both, table, mixed, halves, kernel):
    return pl.pallas_call(
        exchange_body,
        out_shape=jax.ShapeDtypeStruct((128, 32, 128), jnp.bfloat16),
        in_specs=[VMEM] * 3 + [pl.BlockSpec(memory_space=pltpu.HBM)] + [VMEM] * 4,
        out_specs=pl.BlockSpec(memory_space=pltpu.HBM),
        input_output_aliases={3: 0},
        scratch_shapes=[
            pltpu.VMEM((HALF * NG, 128), jnp.bfloat16),
            pltpu.VMEM((HALF * PITCH, 128), jnp.float32),
            pltpu.VMEM((128, 16, 128), jnp.bfloat16),
            pltpu.SemaphoreType.DMA((2, HALF // SPAN)),
        ],
        compiler_params=pltpu.CompilerParams(vmem_limit_bytes=24 * 1024 * 1024),
        name="exchange",
    )(far, owner, term, both, table, mixed, halves, kernel)


def unpack_body(tiles_ref, flat_ref, token_ref):
    def part(step, carry):
        columns = pl.ds(pl.multiple_of(step * 16384, 16384), 16384)
        tiles = [tiles_ref[pl.ds(step * 256 + peer * 32 + 16, 16), :] for peer in range(8)]
        value = jnp.concatenate(tiles, axis=0).astype(jnp.float32).reshape(1, 16384)
        flat_ref[0:1, columns] = value.astype(jnp.bfloat16)
        return carry

    lax.fori_loop(0, 16, part, 0)
    token_ref[...] = tiles_ref[pl.ds(0, 16), :]


def unpacked(tiles):
    return pl.pallas_call(
        unpack_body,
        out_shape=(
            jax.ShapeDtypeStruct((1, G), jnp.bfloat16),
            jax.ShapeDtypeStruct((16, 128), jnp.bfloat16),
        ),
        in_specs=[VMEM],
        out_specs=(VMEM, VMEM),
        compiler_params=pltpu.CompilerParams(vmem_limit_bytes=16 * 1024 * 1024),
        name="unpack",
    )(tiles)


def intersection_body(tiles_ref, token_ref, core_ref, lines_ref, mine_ref, other_ref, wide):
    bf16 = jnp.bfloat16
    for peer in range(128):
        wide[pl.ds(peer * WIDE, 32), :] = tiles_ref[pl.ds(peer * 32, 32), :].astype(jnp.float32)
    total = jnp.zeros((128, 128), jnp.float32)
    for line in range(16):
        trial = wide[pl.ds(line, 128, stride=WIDE), :].astype(bf16)
        value = wide[pl.ds(line + 16, 128, stride=WIDE), :].astype(bf16)
        lines_ref[pl.ds(line * 128, 128), :] = value
        total = total + lax.dot_general(
            trial, value, (((1,), (1,)), ((), ())), preferred_element_type=jnp.float32
        )
    total = total * (1.0 / math.sqrt(G))
    first = core_ref[0] == 0
    mine_ref[...] = jnp.where(first, total[:64], total[64:])
    other_ref[...] = jnp.where(first, total[64:], total[:64])


def intersection_of(tiles, token, core):
    half = jax.ShapeDtypeStruct((64, 128), jnp.float32)
    return pl.pallas_call(
        intersection_body,
        out_shape=(jax.ShapeDtypeStruct((ROWS, 128), jnp.bfloat16), half, half),
        in_specs=[VMEM, pl.BlockSpec(memory_space=pl.ANY), SMEM],
        out_specs=(VMEM, VMEM, VMEM),
        scratch_shapes=[pltpu.VMEM((128 * WIDE, 128), jnp.float32)],
        compiler_params=pltpu.CompilerParams(vmem_limit_bytes=16 * 1024 * 1024),
        name="intersection",
    )(tiles, token, core)


def projected_body(lines_ref, mine_ref, other_ref, core_ref, out_ref, result, left):
    first = core_ref[0] == 0
    mine, other = mine_ref[...].astype(jnp.float32), other_ref[...].astype(jnp.float32)
    table = jnp.concatenate(
        [jnp.where(first, mine, other), jnp.where(first, other, mine)], axis=0
    ).astype(jnp.bfloat16)

    def copy(part):
        columns = pl.ds(part * 512, 512)
        return pltpu.make_async_copy(result.at[:, columns], out_ref.at[:, columns], left.at[part])

    for part in range(4):
        for line in range(part * 4, part * 4 + 4):
            rows = pl.ds(line * 128, 128)
            value = dot(table, lines_ref[rows, :]) * (-1.0 / math.sqrt(128))
            result[:, rows] = value.astype(jnp.bfloat16)
        copy(part).start()
    for part in range(4):
        copy(part).wait()


def projected_of(lines, mine, other, core):
    return pl.pallas_call(
        projected_body,
        out_shape=jax.ShapeDtypeStruct((128, ROWS), jnp.bfloat16),
        in_specs=[VMEM, VMEM, VMEM, SMEM],
        out_specs=pl.BlockSpec(memory_space=pltpu.HBM),
        scratch_shapes=[
            pltpu.VMEM((128, ROWS), jnp.bfloat16),
            pltpu.SemaphoreType.DMA((4,)),
        ],
        compiler_params=pltpu.CompilerParams(vmem_limit_bytes=16 * 1024 * 1024),
        name="projected",
    )(lines, mine, other, core)


def from_far(value):
    count = lax.axis_size(BAND)
    pairs = [(i, (i - 1 if i % 2 == 0 else i + 1) % count) for i in range(count)]
    return lax.ppermute(value, BAND, pairs)


def swapped(value):
    return lax.ppermute(value, "core", [(0, 1), (1, 0)])


def summed_over(value, axes):
    peers = lax.axis_size(axes)
    copies = jnp.broadcast_to(value[None], (peers,) + value.shape)
    tiles = lax.all_to_all(copies, axes, 0, 0, tiled=True)
    return jnp.sum(tiles.astype(jnp.float32), axis=0).astype(jnp.bfloat16)


def local(orbitals, trial, occupations):
    own = packed_with_flag(orbitals, occupations)
    far = from_far(own)
    again = copied(own)
    near = swapped(again)
    table, mixed, halves = (jnp.asarray(value) for value in constants())
    kernel = screened_kernel(again)
    both = packed_after(trial, kernel)
    owner, term = near_term(own, near, table, mixed, kernel)
    both = exchange_of(far, owner, term, both, table, mixed, halves, kernel)
    tiles = lax.all_to_all(both, BAND, 0, 0, tiled=True)
    flat, token = unpacked(both.reshape(2 * ROWS, 128))
    core = lax.axis_index("core").astype(jnp.int32).reshape(1)
    lines, mine, other = intersection_of(tiles.reshape(2 * ROWS, 128), token, core)
    half = (mine + swapped(other)).astype(jnp.bfloat16)
    half = summed_over(half, ("x", "y"))
    half = summed_over(half, "z")
    return flat, projected_of(lines, half, swapped(half), core)


def solution(mesh):
    finer = Mesh(mesh.devices.reshape(mesh.shape["spin"], 4, 2, 8, 2), SPIN_BAND)
    return jax.shard_map(
        local,
        mesh=finer,
        in_specs=(P(SPIN_BAND, None), P(SPIN_BAND, None), P(SPIN_BAND)),
        out_specs=(P(SPIN_BAND, None), P("spin", BAND)),
        check_vma=False,
    )
```

```python
import math

import jax
import jax.numpy as jnp
import ml_dtypes
import numpy as np
from jax import lax
from jax.experimental import pallas as pl
from jax.experimental.pallas import tpu as pltpu
from jax.sharding import Mesh
from jax.sharding import PartitionSpec as P

NG = 64
G = NG**3
ROWS = G // 128
FRACTION = 0.25
OMEGA = 1.0
BAND = ("y", "x", "z", "core")
SPIN_BAND = ("spin",) + BAND
ORDER = np.concatenate([np.arange(0, NG, 2), np.arange(1, NG, 2)])
STEP = 4
SPAN = 2 * STEP
PITCH = 72
WIDE = 40
HALF = NG // 2
NEAR_FLOPS = 10**10
VMEM = pl.BlockSpec(memory_space=pltpu.VMEM)
SMEM = pl.BlockSpec(memory_space=pltpu.SMEM)


def cas_table():
    indices = np.arange(NG)
    phases = (indices[:, None] * indices[None, :] % NG) * (2.0 * math.pi / NG)
    return (np.cos(phases) + np.sin(phases)).astype(np.float32).astype(ml_dtypes.bfloat16)


def squared_modes(index):
    modes = jnp.where(2 * index < NG, index, index - NG)
    wavenum = modes.astype(jnp.float32) * (2.0 * math.pi / NG)
    return wavenum * wavenum


def screened_body(earlier_ref, kernel_ref):
    first = squared_modes(lax.broadcasted_iota(jnp.int32, (NG, 128), 0))
    third = squared_modes(lax.rem(lax.broadcasted_iota(jnp.int32, (NG, 128), 1), NG))

    def one_line(line, carry):
        second = 2 * lax.rem(line, NG // 2) + lax.div(line, NG // 2)
        norm_sq = first + squared_modes(jnp.full((NG, 128), second, jnp.int32)) + third
        bounded = jnp.where(norm_sq > 0, norm_sq, 1.0)
        screened = jnp.where(
            norm_sq > 0,
            4.0 * math.pi / bounded * (1.0 - jnp.exp(-bounded / (4.0 * OMEGA * OMEGA))),
            math.pi / (OMEGA * OMEGA),
        )
        kernel_ref[line] = screened * (1.0 / G)
        return carry

    lax.fori_loop(0, NG, one_line, 0, unroll=2)


def screened_kernel(earlier):
    return pl.pallas_call(
        screened_body,
        out_shape=jax.ShapeDtypeStruct((NG, NG, 128), jnp.float32),
        in_specs=[pl.BlockSpec(memory_space=pl.ANY)],
        out_specs=VMEM,
        compiler_params=pltpu.CompilerParams(vmem_limit_bytes=16 * 1024 * 1024),
        cost_estimate=pl.CostEstimate(
            flops=NEAR_FLOPS, bytes_accessed=2 * 1024 * 1024, transcendentals=0
        ),
        name="screened_kernel",
    )(earlier)


def repeated(table):
    return np.kron(np.eye(STEP, dtype=np.float32), table.astype(np.float32)).astype(table.dtype)


def constants():
    table = cas_table()
    mixed = table[ORDER][:, ORDER]
    crossed = np.concatenate([table[HALF:, HALF:], table[HALF:, :HALF]], axis=1)
    halves = np.concatenate([table[:HALF], crossed], axis=0)
    return repeated(table), repeated(mixed), repeated(halves)


def dot(left, right):
    return lax.dot_general(
        left, right, (((1,), (0,)), ((), ())), preferred_element_type=jnp.float32
    )


def pack_body(flat_ref, tiles_ref):
    def part(step, carry):
        columns = pl.ds(pl.multiple_of(step * 16384, 16384), 16384)
        rows = pl.ds(pl.multiple_of(step * 128, 128), 128)
        tiles_ref[rows, :] = flat_ref[0:1, columns].reshape(128, 128)
        return carry

    lax.fori_loop(0, 16, part, 0)


def pack_flagged_body(flat_ref, flag_ref, tiles_ref):
    pack_body(flat_ref, tiles_ref)
    flag = jnp.broadcast_to(flag_ref[...], (16, 128))
    tiles_ref[pl.ds(ROWS, 16), :] = flag.astype(jnp.float32).astype(jnp.bfloat16)


def pack_after_body(flat_ref, earlier_ref, both_ref):
    both_ref[...] = flat_ref[...].reshape(256, 128).reshape(16, 16, 128)


def packed_after(flat, earlier):
    return pl.pallas_call(
        pack_after_body,
        grid=(8,),
        out_shape=jax.ShapeDtypeStruct((128, 32, 128), jnp.bfloat16),
        in_specs=[
            pl.BlockSpec((1, G // 8), lambda part: (0, part)),
            pl.BlockSpec(memory_space=pl.ANY),
        ],
        out_specs=pl.BlockSpec((16, 16, 128), lambda part: (part, 0, 0)),
        compiler_params=pltpu.CompilerParams(vmem_limit_bytes=16 * 1024 * 1024),
        name="pack",
    )(flat, earlier)


def again_body(tiles_ref, again_ref):
    again_ref[...] = tiles_ref[...]


def copied(tiles):
    return pl.pallas_call(
        again_body,
        out_shape=jax.ShapeDtypeStruct(tiles.shape, tiles.dtype),
        in_specs=[VMEM],
        out_specs=VMEM,
        compiler_params=pltpu.CompilerParams(vmem_limit_bytes=16 * 1024 * 1024),
        name="again",
    )(tiles)


def packed_with_flag(flat, flag):
    return pl.pallas_call(
        pack_flagged_body,
        out_shape=jax.ShapeDtypeStruct((ROWS + 16, 128), jnp.bfloat16),
        in_specs=[VMEM, VMEM],
        out_specs=VMEM,
        compiler_params=pltpu.CompilerParams(vmem_limit_bytes=16 * 1024 * 1024),
        name="pack_flagged",
    )(flat, flag.reshape(1, 1))


def plane_rows(plane, height):
    if isinstance(plane, int):
        return pl.ds(plane * height, height)
    return pl.ds(pl.multiple_of(plane * height, height), height)


def pitched(plane):
    if isinstance(plane, int):
        return pl.ds(plane * PITCH, NG)
    return pl.ds(pl.multiple_of(plane * PITCH, 8), NG)


def beside(parts):
    return jnp.concatenate(
        [jnp.concatenate(parts[:STEP], axis=0), jnp.concatenate(parts[STEP:], axis=0)], axis=1
    )


def part_of(values, part):
    rows = slice(part % STEP * NG, part % STEP * NG + NG)
    return values[rows, :128] if part < STEP else values[rows, 128:]


def passes_there(density_of, table_ref, mixed_ref, kernel_ref, grid):
    bf16 = jnp.bfloat16

    def forward(step, carry):
        planes = [step * SPAN + part for part in range(SPAN)]
        values = beside([density_of(plane) for plane in planes])
        values = dot(values, table_ref[...]).astype(bf16)
        values = dot(mixed_ref[...], values)
        for part, plane in enumerate(planes):
            grid[pitched(plane), :] = part_of(values, part)
        return carry

    lax.fori_loop(0, NG // SPAN, forward, 0, unroll=True)

    def across(step, carry):
        lines = [step * SPAN + part for part in range(SPAN)]
        rows = [pl.ds(line, NG, stride=PITCH) for line in lines]
        values = beside([grid[row, :].astype(bf16) for row in rows])
        values = dot(table_ref[...], values)
        values = (values * beside([kernel_ref[line] for line in lines])).astype(bf16)
        values = dot(table_ref[...], values)
        for part, row in enumerate(rows):
            grid[row, :] = part_of(values, part)
        return carry

    lax.fori_loop(0, NG // SPAN, across, 0, unroll=True)

    def potentials(step):
        planes = [step * SPAN + part for part in range(SPAN)]
        values = beside([grid[pitched(plane), :].astype(bf16) for plane in planes])
        values = dot(mixed_ref[...], values).astype(bf16)
        values = dot(values, table_ref[...])
        return [(plane, part_of(values, part)) for part, plane in enumerate(planes)]

    return potentials


def fill_of(ref):
    return ref[pl.ds(ROWS, 16), :].astype(jnp.float32)[:1] * -FRACTION


def two_planes(ref, plane, low):
    first, second = (
        ref[plane_rows(index, 32), :].astype(jnp.float32) for index in (plane, plane + HALF)
    )
    first_turned, second_turned = (pltpu.roll(value, 64, 1) for value in (first, second))
    return jnp.concatenate(
        [jnp.where(low, first, second_turned), jnp.where(low, first_turned, second)], axis=0
    )


def low_lanes(height):
    return lax.broadcasted_iota(jnp.int32, (height, 128), 1) < 64


def near_body(
    own_ref, near_ref, table_ref, mixed_ref, kernel_ref, owner_ref, term_ref, visitors, grid
):
    f32, bf16 = jnp.float32, jnp.bfloat16
    low = low_lanes(NG // 2)

    def density_of(plane):
        own, near = (ref[plane_rows(plane, 32), :].astype(f32) for ref in (own_ref, near_ref))
        own_turned, near_turned = (pltpu.roll(value, 64, 1) for value in (own, near))
        mine = jnp.concatenate(
            [jnp.where(low, own, own_turned), jnp.where(low, own_turned, own)], axis=0
        )
        pairs = jnp.concatenate(
            [jnp.where(low, own, near_turned), jnp.where(low, own_turned, near)], axis=0
        )
        wide = plane_rows(plane, 64)
        visitors[wide, :] = pairs.astype(bf16)
        return (mine * pairs).astype(bf16)

    potentials = passes_there(density_of, table_ref, mixed_ref, kernel_ref, grid)
    fill = jnp.where(low_lanes(NG), fill_of(own_ref), fill_of(near_ref))
    for plane in range(HALF):
        owner_ref[plane_rows(plane, 64), :] = two_planes(own_ref, plane, low).astype(bf16)

    def backward(step, carry):
        for plane, potential in potentials(step):
            total = potential * (visitors[plane_rows(plane, 64), :].astype(f32) * fill)
            total = total + pltpu.roll(total, 64, 1)
            term_ref[plane_rows(plane, 32), :] = jnp.where(low, total[:32], total[32:])
        return carry

    lax.fori_loop(0, NG // SPAN, backward, 0, unroll=True)


def near_term(own, near, table, mixed, kernel):
    return pl.pallas_call(
        near_body,
        out_shape=(
            jax.ShapeDtypeStruct((HALF * NG, 128), jnp.bfloat16),
            jax.ShapeDtypeStruct((ROWS, 128), jnp.float32),
        ),
        in_specs=[VMEM] * 5,
        out_specs=(VMEM, VMEM),
        scratch_shapes=[
            pltpu.VMEM((NG * NG, 128), jnp.bfloat16),
            pltpu.VMEM((NG * PITCH, 128), jnp.float32),
        ],
        compiler_params=pltpu.CompilerParams(vmem_limit_bytes=24 * 1024 * 1024),
        cost_estimate=pl.CostEstimate(
            flops=NEAR_FLOPS, bytes_accessed=4 * 1024 * 1024, transcendentals=0
        ),
        name="near_term",
    )(own, near, table, mixed, kernel)


def exchange_body(
    far_ref, owner_ref, term_ref, both_ref, table_ref, mixed_ref, halves_ref, kernel_ref,
    out_ref, visitors, grid, tiles, left,
):
    f32, bf16 = jnp.float32, jnp.bfloat16
    low = low_lanes(HALF)

    for step in range(HALF // SPAN):
        planes = [step * SPAN + part for part in range(SPAN)]
        densities = []
        for plane in planes:
            far = two_planes(far_ref, plane, low)
            wide = plane_rows(plane, 64)
            visitors[wide, :] = far.astype(bf16)
            densities.append((far * owner_ref[wide, :].astype(f32)).astype(bf16))
        values = dot(beside(densities), table_ref[...]).astype(bf16)
        values = dot(mixed_ref[...], values)
        for part, plane in enumerate(planes):
            grid[pitched(plane), :] = part_of(values, part)

    def crossed(value):
        return jnp.concatenate([value, pltpu.roll(value, 64, 1)], axis=0).astype(bf16)

    def joined(value):
        return jnp.where(low, value[:HALF], value[HALF:])

    for step in range(NG // SPAN):
        lines = [step * SPAN + part for part in range(SPAN)]
        rows = [pl.ds(line, HALF, stride=PITCH) for line in lines]
        values = dot(halves_ref[...], beside([crossed(grid[row, :]) for row in rows]))
        values = beside(
            [
                crossed(joined(part_of(values, part)) * joined(kernel_ref[line]))
                for part, line in enumerate(lines)
            ]
        )
        values = dot(halves_ref[...], values)
        for part, row in enumerate(rows):
            grid[row, :] = joined(part_of(values, part))

    fill = fill_of(far_ref)

    def tile_copies(step):
        copies = []
        for half in range(2):
            peers = pl.ds(step * 2 * SPAN + half * NG, 2 * SPAN)
            copies.append(
                pltpu.make_async_copy(
                    tiles.at[peers], out_ref.at[peers, pl.ds(16, 16), :], left.at[half, step]
                )
            )
        return copies

    for step in range(HALF // SPAN):
        planes = [step * SPAN + part for part in range(SPAN)]
        values = beside([grid[pitched(plane), :].astype(bf16) for plane in planes])
        values = dot(mixed_ref[...], values).astype(bf16)
        values = dot(values, table_ref[...])
        for part, plane in enumerate(planes):
            weight = visitors[plane_rows(plane, 64), :].astype(f32) * fill
            total = part_of(values, part) * weight
            turned = pltpu.roll(total, 64, 1)
            first = jnp.where(low, total[:HALF], turned[HALF:])
            second = jnp.where(low, turned[:HALF], total[HALF:])
            for index, value in ((plane, first), (plane + HALF, second)):
                value = value + term_ref[plane_rows(index, 32), :]
                tiles[pl.ds(2 * index, 2)] = value.astype(bf16).reshape(2, 16, 128)
        for copy in tile_copies(step):
            copy.start()
    for step in range(HALF // SPAN):
        for copy in tile_copies(step):
            copy.wait()


def exchange_of(far, owner, term, both, table, mixed, halves, kernel):
    return pl.pallas_call(
        exchange_body,
        out_shape=jax.ShapeDtypeStruct((128, 32, 128), jnp.bfloat16),
        in_specs=[VMEM] * 3 + [pl.BlockSpec(memory_space=pltpu.HBM)] + [VMEM] * 4,
        out_specs=pl.BlockSpec(memory_space=pltpu.HBM),
        input_output_aliases={3: 0},
        scratch_shapes=[
            pltpu.VMEM((HALF * NG, 128), jnp.bfloat16),
            pltpu.VMEM((HALF * PITCH, 128), jnp.float32),
            pltpu.VMEM((128, 16, 128), jnp.bfloat16),
            pltpu.SemaphoreType.DMA((2, HALF // SPAN)),
        ],
        compiler_params=pltpu.CompilerParams(vmem_limit_bytes=24 * 1024 * 1024),
        name="exchange",
    )(far, owner, term, both, table, mixed, halves, kernel)


def unpack_body(tiles_ref, flat_ref, token_ref):
    def part(step, carry):
        columns = pl.ds(pl.multiple_of(step * 16384, 16384), 16384)
        tiles = [tiles_ref[pl.ds(step * 256 + peer * 32 + 16, 16), :] for peer in range(8)]
        value = jnp.concatenate(tiles, axis=0).astype(jnp.float32).reshape(1, 16384)
        flat_ref[0:1, columns] = value.astype(jnp.bfloat16)
        return carry

    lax.fori_loop(0, 16, part, 0)
    token_ref[...] = tiles_ref[pl.ds(0, 16), :]


def unpacked(tiles):
    return pl.pallas_call(
        unpack_body,
        out_shape=(
            jax.ShapeDtypeStruct((1, G), jnp.bfloat16),
            jax.ShapeDtypeStruct((16, 128), jnp.bfloat16),
        ),
        in_specs=[VMEM],
        out_specs=(VMEM, VMEM),
        compiler_params=pltpu.CompilerParams(vmem_limit_bytes=16 * 1024 * 1024),
        name="unpack",
    )(tiles)


def intersection_body(tiles_ref, token_ref, core_ref, lines_ref, mine_ref, other_ref, wide):
    bf16 = jnp.bfloat16
    for peer in range(128):
        wide[pl.ds(peer * WIDE, 32), :] = tiles_ref[pl.ds(peer * 32, 32), :].astype(jnp.float32)
    total = jnp.zeros((128, 128), jnp.float32)
    for line in range(16):
        trial = wide[pl.ds(line, 128, stride=WIDE), :].astype(bf16)
        value = wide[pl.ds(line + 16, 128, stride=WIDE), :].astype(bf16)
        lines_ref[pl.ds(line * 128, 128), :] = value
        total = total + lax.dot_general(
            trial, value, (((1,), (1,)), ((), ())), preferred_element_type=jnp.float32
        )
    total = total * (1.0 / math.sqrt(G))
    first = core_ref[0] == 0
    mine_ref[...] = jnp.where(first, total[:64], total[64:])
    other_ref[...] = jnp.where(first, total[64:], total[:64])


def intersection_of(tiles, token, core):
    half = jax.ShapeDtypeStruct((64, 128), jnp.float32)
    return pl.pallas_call(
        intersection_body,
        out_shape=(jax.ShapeDtypeStruct((ROWS, 128), jnp.bfloat16), half, half),
        in_specs=[VMEM, pl.BlockSpec(memory_space=pl.ANY), SMEM],
        out_specs=(VMEM, VMEM, VMEM),
        scratch_shapes=[pltpu.VMEM((128 * WIDE, 128), jnp.float32)],
        compiler_params=pltpu.CompilerParams(vmem_limit_bytes=16 * 1024 * 1024),
        name="intersection",
    )(tiles, token, core)


def projected_body(lines_ref, mine_ref, other_ref, core_ref, out_ref, result, left):
    first = core_ref[0] == 0
    mine, other = mine_ref[...].astype(jnp.float32), other_ref[...].astype(jnp.float32)
    table = jnp.concatenate(
        [jnp.where(first, mine, other), jnp.where(first, other, mine)], axis=0
    ).astype(jnp.bfloat16)

    def copy(part):
        columns = pl.ds(part * 512, 512)
        return pltpu.make_async_copy(result.at[:, columns], out_ref.at[:, columns], left.at[part])

    for part in range(4):
        for line in range(part * 4, part * 4 + 4):
            rows = pl.ds(line * 128, 128)
            value = dot(table, lines_ref[rows, :]) * (-1.0 / math.sqrt(128))
            result[:, rows] = value.astype(jnp.bfloat16)
        copy(part).start()
    for part in range(4):
        copy(part).wait()


def projected_of(lines, mine, other, core):
    return pl.pallas_call(
        projected_body,
        out_shape=jax.ShapeDtypeStruct((128, ROWS), jnp.bfloat16),
        in_specs=[VMEM, VMEM, VMEM, SMEM],
        out_specs=pl.BlockSpec(memory_space=pltpu.HBM),
        scratch_shapes=[
            pltpu.VMEM((128, ROWS), jnp.bfloat16),
            pltpu.SemaphoreType.DMA((4,)),
        ],
        compiler_params=pltpu.CompilerParams(vmem_limit_bytes=16 * 1024 * 1024),
        name="projected",
    )(lines, mine, other, core)


def from_far(value):
    count = lax.axis_size(BAND)
    pairs = [(i, (i - 1 if i % 2 == 0 else i + 1) % count) for i in range(count)]
    return lax.ppermute(value, BAND, pairs)


def swapped(value):
    return lax.ppermute(value, "core", [(0, 1), (1, 0)])


def summed_over(value, axes):
    peers = lax.axis_size(axes)
    copies = jnp.broadcast_to(value[None], (peers,) + value.shape)
    tiles = lax.all_to_all(copies, axes, 0, 0, tiled=True)
    return jnp.sum(tiles.astype(jnp.float32), axis=0).astype(jnp.bfloat16)


def local(orbitals, trial, occupations):
    own = packed_with_flag(orbitals, occupations)
    far = from_far(own)
    again = copied(own)
    near = swapped(again)
    table, mixed, halves = (jnp.asarray(value) for value in constants())
    kernel = screened_kernel(again)
    both = packed_after(trial, kernel)
    owner, term = near_term(own, near, table, mixed, kernel)
    both = exchange_of(far, owner, term, both, table, mixed, halves, kernel)
    tiles = lax.all_to_all(both, BAND, 0, 0, tiled=True)
    flat, token = unpacked(both.reshape(2 * ROWS, 128))
    core = lax.axis_index("core").astype(jnp.int32).reshape(1)
    lines, mine, other = intersection_of(tiles.reshape(2 * ROWS, 128), token, core)
    half = (mine + swapped(other)).astype(jnp.bfloat16)
    half = summed_over(half, "z")
    half = summed_over(half, ("x", "y"))
    return flat, projected_of(lines, half, swapped(half), core)


def solution(mesh):
    finer = Mesh(mesh.devices.reshape(mesh.shape["spin"], 4, 2, 8, 2), SPIN_BAND)
    return jax.shard_map(
        local,
        mesh=finer,
        in_specs=(P(SPIN_BAND, None), P(SPIN_BAND, None), P(SPIN_BAND)),
        out_specs=(P(SPIN_BAND, None), P("spin", BAND)),
        check_vma=False,
    )
```

```python
import math

import jax
import jax.numpy as jnp
import ml_dtypes
import numpy as np
from jax import lax
from jax.experimental import pallas as pl
from jax.experimental.pallas import tpu as pltpu
from jax.sharding import Mesh
from jax.sharding import PartitionSpec as P

NG = 64
G = NG**3
ROWS = G // 128
FRACTION = 0.25
OMEGA = 1.0
BAND = ("y", "x", "z", "core")
SPIN_BAND = ("spin",) + BAND
ORDER = np.concatenate([np.arange(0, NG, 2), np.arange(1, NG, 2)])
STEP = 4
SPAN = 2 * STEP
PITCH = 72
WIDE = 40
HALF = NG // 2
NEAR_FLOPS = 10**10
VMEM = pl.BlockSpec(memory_space=pltpu.VMEM)
SMEM = pl.BlockSpec(memory_space=pltpu.SMEM)


def cas_table():
    indices = np.arange(NG)
    phases = (indices[:, None] * indices[None, :] % NG) * (2.0 * math.pi / NG)
    return (np.cos(phases) + np.sin(phases)).astype(np.float32).astype(ml_dtypes.bfloat16)


def squared_modes(index):
    modes = jnp.where(2 * index < NG, index, index - NG)
    wavenum = modes.astype(jnp.float32) * (2.0 * math.pi / NG)
    return wavenum * wavenum


def screened_body(earlier_ref, kernel_ref):
    first = squared_modes(lax.broadcasted_iota(jnp.int32, (NG, 128), 0))
    third = squared_modes(lax.rem(lax.broadcasted_iota(jnp.int32, (NG, 128), 1), NG))

    def one_line(line, carry):
        second = 2 * lax.rem(line, NG // 2) + lax.div(line, NG // 2)
        norm_sq = first + squared_modes(jnp.full((NG, 128), second, jnp.int32)) + third
        bounded = jnp.where(norm_sq > 0, norm_sq, 1.0)
        screened = jnp.where(
            norm_sq > 0,
            4.0 * math.pi / bounded * (1.0 - jnp.exp(-bounded / (4.0 * OMEGA * OMEGA))),
            math.pi / (OMEGA * OMEGA),
        )
        kernel_ref[line] = screened * (1.0 / G)
        return carry

    lax.fori_loop(0, NG, one_line, 0, unroll=2)


def screened_kernel(earlier):
    return pl.pallas_call(
        screened_body,
        out_shape=jax.ShapeDtypeStruct((NG, NG, 128), jnp.float32),
        in_specs=[pl.BlockSpec(memory_space=pl.ANY)],
        out_specs=VMEM,
        compiler_params=pltpu.CompilerParams(vmem_limit_bytes=16 * 1024 * 1024),
        cost_estimate=pl.CostEstimate(
            flops=NEAR_FLOPS, bytes_accessed=2 * 1024 * 1024, transcendentals=0
        ),
        name="screened_kernel",
    )(earlier)


def repeated(table):
    return np.kron(np.eye(STEP, dtype=np.float32), table.astype(np.float32)).astype(table.dtype)


def constants():
    table = cas_table()
    mixed = table[ORDER][:, ORDER]
    crossed = np.concatenate([table[HALF:, HALF:], table[HALF:, :HALF]], axis=1)
    halves = np.concatenate([table[:HALF], crossed], axis=0)
    return repeated(table), repeated(mixed), repeated(halves)


def dot(left, right):
    return lax.dot_general(
        left, right, (((1,), (0,)), ((), ())), preferred_element_type=jnp.float32
    )


def pack_body(flat_ref, tiles_ref):
    def part(step, carry):
        columns = pl.ds(pl.multiple_of(step * 16384, 16384), 16384)
        rows = pl.ds(pl.multiple_of(step * 128, 128), 128)
        tiles_ref[rows, :] = flat_ref[0:1, columns].reshape(128, 128)
        return carry

    lax.fori_loop(0, 16, part, 0)


def seed_body(seed_ref):
    seed_ref[...] = jnp.zeros(seed_ref.shape, seed_ref.dtype)


def seed():
    return pl.pallas_call(
        seed_body,
        out_shape=jax.ShapeDtypeStruct((8, 128), jnp.int32),
        out_specs=VMEM,
        cost_estimate=pl.CostEstimate(
            flops=NEAR_FLOPS, bytes_accessed=4096, transcendentals=0
        ),
        name="seed",
    )()


def flag_body(flag_ref, seed_ref, rows_ref):
    flag = jnp.broadcast_to(flag_ref[...], (16, 128)) + seed_ref[pl.ds(0, 1), :]
    rows_ref[...] = flag.astype(jnp.float32).astype(jnp.bfloat16)


def flag_rows(flag):
    return pl.pallas_call(
        flag_body,
        out_shape=jax.ShapeDtypeStruct((16, 128), jnp.bfloat16),
        in_specs=[VMEM, VMEM],
        out_specs=VMEM,
        compiler_params=pltpu.CompilerParams(vmem_limit_bytes=16 * 1024 * 1024),
        name="flag_rows",
    )(flag.reshape(1, 1), seed())


def pack_flagged_body(flat_ref, rows_ref, tiles_ref):
    pack_body(flat_ref, tiles_ref)
    tiles_ref[pl.ds(ROWS, 16), :] = rows_ref[...]


def pack_after_body(flat_ref, earlier_ref, both_ref):
    both_ref[...] = flat_ref[...].reshape(256, 128).reshape(16, 16, 128)


def packed_after(flat, earlier):
    return pl.pallas_call(
        pack_after_body,
        grid=(8,),
        out_shape=jax.ShapeDtypeStruct((128, 32, 128), jnp.bfloat16),
        in_specs=[
            pl.BlockSpec((1, G // 8), lambda part: (0, part)),
            pl.BlockSpec(memory_space=pl.ANY),
        ],
        out_specs=pl.BlockSpec((16, 16, 128), lambda part: (part, 0, 0)),
        compiler_params=pltpu.CompilerParams(vmem_limit_bytes=16 * 1024 * 1024),
        name="pack",
    )(flat, earlier)


def again_body(tiles_ref, again_ref):
    again_ref[...] = tiles_ref[...]


def copied(tiles):
    return pl.pallas_call(
        again_body,
        out_shape=jax.ShapeDtypeStruct(tiles.shape, tiles.dtype),
        in_specs=[VMEM],
        out_specs=VMEM,
        compiler_params=pltpu.CompilerParams(vmem_limit_bytes=16 * 1024 * 1024),
        name="again",
    )(tiles)


def packed_with_flag(flat, rows):
    return pl.pallas_call(
        pack_flagged_body,
        out_shape=jax.ShapeDtypeStruct((ROWS + 16, 128), jnp.bfloat16),
        in_specs=[VMEM, VMEM],
        out_specs=VMEM,
        compiler_params=pltpu.CompilerParams(vmem_limit_bytes=16 * 1024 * 1024),
        name="pack_flagged",
    )(flat, rows)


def plane_rows(plane, height):
    if isinstance(plane, int):
        return pl.ds(plane * height, height)
    return pl.ds(pl.multiple_of(plane * height, height), height)


def pitched(plane):
    if isinstance(plane, int):
        return pl.ds(plane * PITCH, NG)
    return pl.ds(pl.multiple_of(plane * PITCH, 8), NG)


def beside(parts):
    return jnp.concatenate(
        [jnp.concatenate(parts[:STEP], axis=0), jnp.concatenate(parts[STEP:], axis=0)], axis=1
    )


def part_of(values, part):
    rows = slice(part % STEP * NG, part % STEP * NG + NG)
    return values[rows, :128] if part < STEP else values[rows, 128:]


def passes_there(density_of, table_ref, mixed_ref, kernel_ref, grid):
    bf16 = jnp.bfloat16

    def forward(step, carry):
        planes = [step * SPAN + part for part in range(SPAN)]
        values = beside([density_of(plane) for plane in planes])
        values = dot(values, table_ref[...]).astype(bf16)
        values = dot(mixed_ref[...], values)
        for part, plane in enumerate(planes):
            grid[pitched(plane), :] = part_of(values, part)
        return carry

    lax.fori_loop(0, NG // SPAN, forward, 0, unroll=True)

    def across(step, carry):
        lines = [step * SPAN + part for part in range(SPAN)]
        rows = [pl.ds(line, NG, stride=PITCH) for line in lines]
        values = beside([grid[row, :].astype(bf16) for row in rows])
        values = dot(table_ref[...], values)
        values = (values * beside([kernel_ref[line] for line in lines])).astype(bf16)
        values = dot(table_ref[...], values)
        for part, row in enumerate(rows):
            grid[row, :] = part_of(values, part)
        return carry

    lax.fori_loop(0, NG // SPAN, across, 0, unroll=True)

    def potentials(step):
        planes = [step * SPAN + part for part in range(SPAN)]
        values = beside([grid[pitched(plane), :].astype(bf16) for plane in planes])
        values = dot(mixed_ref[...], values).astype(bf16)
        values = dot(values, table_ref[...])
        return [(plane, part_of(values, part)) for part, plane in enumerate(planes)]

    return potentials


def fill_of(ref):
    return ref[pl.ds(ROWS, 16), :].astype(jnp.float32)[:1] * -FRACTION


def two_planes(ref, plane, low):
    first, second = (
        ref[plane_rows(index, 32), :].astype(jnp.float32) for index in (plane, plane + HALF)
    )
    first_turned, second_turned = (pltpu.roll(value, 64, 1) for value in (first, second))
    return jnp.concatenate(
        [jnp.where(low, first, second_turned), jnp.where(low, first_turned, second)], axis=0
    )


def low_lanes(height):
    return lax.broadcasted_iota(jnp.int32, (height, 128), 1) < 64


def near_body(
    own_ref, near_ref, table_ref, mixed_ref, kernel_ref, owner_ref, term_ref, visitors, grid
):
    f32, bf16 = jnp.float32, jnp.bfloat16
    low = low_lanes(NG // 2)

    def density_of(plane):
        own, near = (ref[plane_rows(plane, 32), :].astype(f32) for ref in (own_ref, near_ref))
        own_turned, near_turned = (pltpu.roll(value, 64, 1) for value in (own, near))
        mine = jnp.concatenate(
            [jnp.where(low, own, own_turned), jnp.where(low, own_turned, own)], axis=0
        )
        pairs = jnp.concatenate(
            [jnp.where(low, own, near_turned), jnp.where(low, own_turned, near)], axis=0
        )
        wide = plane_rows(plane, 64)
        visitors[wide, :] = pairs.astype(bf16)
        return (mine * pairs).astype(bf16)

    potentials = passes_there(density_of, table_ref, mixed_ref, kernel_ref, grid)
    fill = jnp.where(low_lanes(NG), fill_of(own_ref), fill_of(near_ref))
    for plane in range(HALF):
        owner_ref[plane_rows(plane, 64), :] = two_planes(own_ref, plane, low).astype(bf16)

    def backward(step, carry):
        for plane, potential in potentials(step):
            total = potential * (visitors[plane_rows(plane, 64), :].astype(f32) * fill)
            total = total + pltpu.roll(total, 64, 1)
            term_ref[plane_rows(plane, 32), :] = jnp.where(low, total[:32], total[32:])
        return carry

    lax.fori_loop(0, NG // SPAN, backward, 0, unroll=True)


def near_term(own, near, table, mixed, kernel):
    return pl.pallas_call(
        near_body,
        out_shape=(
            jax.ShapeDtypeStruct((HALF * NG, 128), jnp.bfloat16),
            jax.ShapeDtypeStruct((ROWS, 128), jnp.float32),
        ),
        in_specs=[VMEM] * 5,
        out_specs=(VMEM, VMEM),
        scratch_shapes=[
            pltpu.VMEM((NG * NG, 128), jnp.bfloat16),
            pltpu.VMEM((NG * PITCH, 128), jnp.float32),
        ],
        compiler_params=pltpu.CompilerParams(vmem_limit_bytes=24 * 1024 * 1024),
        cost_estimate=pl.CostEstimate(
            flops=NEAR_FLOPS, bytes_accessed=4 * 1024 * 1024, transcendentals=0
        ),
        name="near_term",
    )(own, near, table, mixed, kernel)


def exchange_body(
    far_ref, owner_ref, term_ref, both_ref, table_ref, mixed_ref, halves_ref, kernel_ref,
    out_ref, visitors, grid, tiles, left,
):
    f32, bf16 = jnp.float32, jnp.bfloat16
    low = low_lanes(HALF)

    for step in range(HALF // SPAN):
        planes = [step * SPAN + part for part in range(SPAN)]
        densities = []
        for plane in planes:
            far = two_planes(far_ref, plane, low)
            wide = plane_rows(plane, 64)
            visitors[wide, :] = far.astype(bf16)
            densities.append((far * owner_ref[wide, :].astype(f32)).astype(bf16))
        values = dot(beside(densities), table_ref[...]).astype(bf16)
        values = dot(mixed_ref[...], values)
        for part, plane in enumerate(planes):
            grid[pitched(plane), :] = part_of(values, part)

    def crossed(value):
        return jnp.concatenate([value, pltpu.roll(value, 64, 1)], axis=0).astype(bf16)

    def joined(value):
        return jnp.where(low, value[:HALF], value[HALF:])

    for step in range(NG // SPAN):
        lines = [step * SPAN + part for part in range(SPAN)]
        rows = [pl.ds(line, HALF, stride=PITCH) for line in lines]
        values = dot(halves_ref[...], beside([crossed(grid[row, :]) for row in rows]))
        values = beside(
            [
                crossed(joined(part_of(values, part)) * joined(kernel_ref[line]))
                for part, line in enumerate(lines)
            ]
        )
        values = dot(halves_ref[...], values)
        for part, row in enumerate(rows):
            grid[row, :] = joined(part_of(values, part))

    fill = fill_of(far_ref)

    def tile_copies(step):
        copies = []
        for half in range(2):
            peers = pl.ds(step * 2 * SPAN + half * NG, 2 * SPAN)
            copies.append(
                pltpu.make_async_copy(
                    tiles.at[peers], out_ref.at[peers, pl.ds(16, 16), :], left.at[half, step]
                )
            )
        return copies

    for step in range(HALF // SPAN):
        planes = [step * SPAN + part for part in range(SPAN)]
        values = beside([grid[pitched(plane), :].astype(bf16) for plane in planes])
        values = dot(mixed_ref[...], values).astype(bf16)
        values = dot(values, table_ref[...])
        for part, plane in enumerate(planes):
            weight = visitors[plane_rows(plane, 64), :].astype(f32) * fill
            total = part_of(values, part) * weight
            turned = pltpu.roll(total, 64, 1)
            first = jnp.where(low, total[:HALF], turned[HALF:])
            second = jnp.where(low, turned[:HALF], total[HALF:])
            for index, value in ((plane, first), (plane + HALF, second)):
                value = value + term_ref[plane_rows(index, 32), :]
                tiles[pl.ds(2 * index, 2)] = value.astype(bf16).reshape(2, 16, 128)
        for copy in tile_copies(step):
            copy.start()
    for step in range(HALF // SPAN):
        for copy in tile_copies(step):
            copy.wait()


def exchange_of(far, owner, term, both, table, mixed, halves, kernel):
    return pl.pallas_call(
        exchange_body,
        out_shape=jax.ShapeDtypeStruct((128, 32, 128), jnp.bfloat16),
        in_specs=[VMEM] * 3 + [pl.BlockSpec(memory_space=pltpu.HBM)] + [VMEM] * 4,
        out_specs=pl.BlockSpec(memory_space=pltpu.HBM),
        input_output_aliases={3: 0},
        scratch_shapes=[
            pltpu.VMEM((HALF * NG, 128), jnp.bfloat16),
            pltpu.VMEM((HALF * PITCH, 128), jnp.float32),
            pltpu.VMEM((128, 16, 128), jnp.bfloat16),
            pltpu.SemaphoreType.DMA((2, HALF // SPAN)),
        ],
        compiler_params=pltpu.CompilerParams(vmem_limit_bytes=24 * 1024 * 1024),
        name="exchange",
    )(far, owner, term, both, table, mixed, halves, kernel)


def unpack_body(tiles_ref, flat_ref, token_ref):
    def part(step, carry):
        columns = pl.ds(pl.multiple_of(step * 16384, 16384), 16384)
        tiles = [tiles_ref[pl.ds(step * 256 + peer * 32 + 16, 16), :] for peer in range(8)]
        value = jnp.concatenate(tiles, axis=0).astype(jnp.float32).reshape(1, 16384)
        flat_ref[0:1, columns] = value.astype(jnp.bfloat16)
        return carry

    lax.fori_loop(0, 16, part, 0)
    token_ref[...] = tiles_ref[pl.ds(0, 16), :]


def unpacked(tiles):
    return pl.pallas_call(
        unpack_body,
        out_shape=(
            jax.ShapeDtypeStruct((1, G), jnp.bfloat16),
            jax.ShapeDtypeStruct((16, 128), jnp.bfloat16),
        ),
        in_specs=[VMEM],
        out_specs=(VMEM, VMEM),
        compiler_params=pltpu.CompilerParams(vmem_limit_bytes=16 * 1024 * 1024),
        name="unpack",
    )(tiles)


def intersection_body(tiles_ref, token_ref, core_ref, lines_ref, mine_ref, other_ref, wide):
    bf16 = jnp.bfloat16
    for peer in range(128):
        wide[pl.ds(peer * WIDE, 32), :] = tiles_ref[pl.ds(peer * 32, 32), :].astype(jnp.float32)
    total = jnp.zeros((128, 128), jnp.float32)
    for line in range(16):
        trial = wide[pl.ds(line, 128, stride=WIDE), :].astype(bf16)
        value = wide[pl.ds(line + 16, 128, stride=WIDE), :].astype(bf16)
        lines_ref[pl.ds(line * 128, 128), :] = value
        total = total + lax.dot_general(
            trial, value, (((1,), (1,)), ((), ())), preferred_element_type=jnp.float32
        )
    total = total * (1.0 / math.sqrt(G))
    first = core_ref[0] == 0
    mine_ref[...] = jnp.where(first, total[:64], total[64:])
    other_ref[...] = jnp.where(first, total[64:], total[:64])


def intersection_of(tiles, token, core):
    half = jax.ShapeDtypeStruct((64, 128), jnp.float32)
    return pl.pallas_call(
        intersection_body,
        out_shape=(jax.ShapeDtypeStruct((ROWS, 128), jnp.bfloat16), half, half),
        in_specs=[VMEM, pl.BlockSpec(memory_space=pl.ANY), SMEM],
        out_specs=(VMEM, VMEM, VMEM),
        scratch_shapes=[pltpu.VMEM((128 * WIDE, 128), jnp.float32)],
        compiler_params=pltpu.CompilerParams(vmem_limit_bytes=16 * 1024 * 1024),
        name="intersection",
    )(tiles, token, core)


def projected_body(lines_ref, mine_ref, other_ref, core_ref, out_ref, result, left):
    first = core_ref[0] == 0
    mine, other = mine_ref[...].astype(jnp.float32), other_ref[...].astype(jnp.float32)
    table = jnp.concatenate(
        [jnp.where(first, mine, other), jnp.where(first, other, mine)], axis=0
    ).astype(jnp.bfloat16)

    def copy(part):
        columns = pl.ds(part * 512, 512)
        return pltpu.make_async_copy(result.at[:, columns], out_ref.at[:, columns], left.at[part])

    for part in range(4):
        for line in range(part * 4, part * 4 + 4):
            rows = pl.ds(line * 128, 128)
            value = dot(table, lines_ref[rows, :]) * (-1.0 / math.sqrt(128))
            result[:, rows] = value.astype(jnp.bfloat16)
        copy(part).start()
    for part in range(4):
        copy(part).wait()


def projected_of(lines, mine, other, core):
    return pl.pallas_call(
        projected_body,
        out_shape=jax.ShapeDtypeStruct((128, ROWS), jnp.bfloat16),
        in_specs=[VMEM, VMEM, VMEM, SMEM],
        out_specs=pl.BlockSpec(memory_space=pltpu.HBM),
        scratch_shapes=[
            pltpu.VMEM((128, ROWS), jnp.bfloat16),
            pltpu.SemaphoreType.DMA((4,)),
        ],
        compiler_params=pltpu.CompilerParams(vmem_limit_bytes=16 * 1024 * 1024),
        name="projected",
    )(lines, mine, other, core)


def from_far(value):
    count = lax.axis_size(BAND)
    pairs = [(i, (i - 1 if i % 2 == 0 else i + 1) % count) for i in range(count)]
    return lax.ppermute(value, BAND, pairs)


def swapped(value):
    return lax.ppermute(value, "core", [(0, 1), (1, 0)])


def summed_over(value, axes):
    peers = lax.axis_size(axes)
    copies = jnp.broadcast_to(value[None], (peers,) + value.shape)
    tiles = lax.all_to_all(copies, axes, 0, 0, tiled=True)
    return jnp.sum(tiles.astype(jnp.float32), axis=0).astype(jnp.bfloat16)


def local(orbitals, trial, occupations):
    own = packed_with_flag(orbitals, flag_rows(occupations))
    far = from_far(own)
    again = copied(own)
    near = swapped(again)
    table, mixed, halves = (jnp.asarray(value) for value in constants())
    kernel = screened_kernel(again)
    both = packed_after(trial, kernel)
    owner, term = near_term(own, near, table, mixed, kernel)
    both = exchange_of(far, owner, term, both, table, mixed, halves, kernel)
    tiles = lax.all_to_all(both, BAND, 0, 0, tiled=True)
    flat, token = unpacked(both.reshape(2 * ROWS, 128))
    core = lax.axis_index("core").astype(jnp.int32).reshape(1)
    lines, mine, other = intersection_of(tiles.reshape(2 * ROWS, 128), token, core)
    half = (mine + swapped(other)).astype(jnp.bfloat16)
    half = summed_over(half, ("x", "y"))
    half = summed_over(half, "z")
    return flat, projected_of(lines, half, swapped(half), core)


def solution(mesh):
    finer = Mesh(mesh.devices.reshape(mesh.shape["spin"], 4, 2, 8, 2), SPIN_BAND)
    return jax.shard_map(
        local,
        mesh=finer,
        in_specs=(P(SPIN_BAND, None), P(SPIN_BAND, None), P(SPIN_BAND)),
        out_specs=(P(SPIN_BAND, None), P("spin", BAND)),
        check_vma=False,
    )
```

```python
import math

import jax
import jax.numpy as jnp
import ml_dtypes
import numpy as np
from jax import lax
from jax.experimental import pallas as pl
from jax.experimental.pallas import tpu as pltpu
from jax.sharding import Mesh
from jax.sharding import PartitionSpec as P

NG = 64
G = NG**3
ROWS = G // 128
FRACTION = 0.25
OMEGA = 1.0
BAND = ("y", "x", "z", "core")
SPIN_BAND = ("spin",) + BAND
ORDER = np.concatenate([np.arange(0, NG, 2), np.arange(1, NG, 2)])
STEP = 4
SPAN = 2 * STEP
PITCH = 72
WIDE = 40
HALF = NG // 2
NEAR_FLOPS = 10**10
VMEM = pl.BlockSpec(memory_space=pltpu.VMEM)
SMEM = pl.BlockSpec(memory_space=pltpu.SMEM)


def cas_table():
    indices = np.arange(NG)
    phases = (indices[:, None] * indices[None, :] % NG) * (2.0 * math.pi / NG)
    return (np.cos(phases) + np.sin(phases)).astype(np.float32).astype(ml_dtypes.bfloat16)


def squared_modes(index):
    modes = jnp.where(2 * index < NG, index, index - NG)
    wavenum = modes.astype(jnp.float32) * (2.0 * math.pi / NG)
    return wavenum * wavenum


def screened_body(earlier_ref, kernel_ref):
    first = squared_modes(lax.broadcasted_iota(jnp.int32, (NG, 128), 0))
    third = squared_modes(lax.rem(lax.broadcasted_iota(jnp.int32, (NG, 128), 1), NG))

    def one_line(line, carry):
        second = 2 * lax.rem(line, NG // 2) + lax.div(line, NG // 2)
        norm_sq = first + squared_modes(jnp.full((NG, 128), second, jnp.int32)) + third
        bounded = jnp.where(norm_sq > 0, norm_sq, 1.0)
        screened = jnp.where(
            norm_sq > 0,
            4.0 * math.pi / bounded * (1.0 - jnp.exp(-bounded / (4.0 * OMEGA * OMEGA))),
            math.pi / (OMEGA * OMEGA),
        )
        kernel_ref[line] = screened * (1.0 / G)
        return carry

    lax.fori_loop(0, NG, one_line, 0, unroll=2)


def screened_kernel(earlier):
    return pl.pallas_call(
        screened_body,
        out_shape=jax.ShapeDtypeStruct((NG, NG, 128), jnp.float32),
        in_specs=[pl.BlockSpec(memory_space=pl.ANY)],
        out_specs=VMEM,
        compiler_params=pltpu.CompilerParams(vmem_limit_bytes=16 * 1024 * 1024),
        cost_estimate=pl.CostEstimate(
            flops=NEAR_FLOPS, bytes_accessed=2 * 1024 * 1024, transcendentals=0
        ),
        name="screened_kernel",
    )(earlier)


def repeated(table):
    return np.kron(np.eye(STEP, dtype=np.float32), table.astype(np.float32)).astype(table.dtype)


def constants():
    table = cas_table()
    mixed = table[ORDER][:, ORDER]
    crossed = np.concatenate([table[HALF:, HALF:], table[HALF:, :HALF]], axis=1)
    halves = np.concatenate([table[:HALF], crossed], axis=0)
    return repeated(table), repeated(mixed), repeated(halves)


def dot(left, right):
    return lax.dot_general(
        left, right, (((1,), (0,)), ((), ())), preferred_element_type=jnp.float32
    )


def pack_body(flat_ref, tiles_ref):
    def part(step, carry):
        columns = pl.ds(pl.multiple_of(step * 16384, 16384), 16384)
        rows = pl.ds(pl.multiple_of(step * 128, 128), 128)
        tiles_ref[rows, :] = flat_ref[0:1, columns].reshape(128, 128)
        return carry

    lax.fori_loop(0, 16, part, 0)


def seed_body(seed_ref):
    seed_ref[...] = jnp.zeros(seed_ref.shape, seed_ref.dtype)


def seed():
    return pl.pallas_call(
        seed_body,
        out_shape=jax.ShapeDtypeStruct((8, 128), jnp.int32),
        out_specs=VMEM,
        compiler_params=pltpu.CompilerParams(vmem_limit_bytes=16 * 1024 * 1024),
        cost_estimate=pl.CostEstimate(
            flops=NEAR_FLOPS, bytes_accessed=4096, transcendentals=0
        ),
        name="seed",
    )()


def flag_body(flag_ref, seed_ref, rows_ref):
    flag = jnp.broadcast_to(flag_ref[...], (16, 128)) + seed_ref[pl.ds(0, 1), :]
    rows_ref[...] = flag.astype(jnp.float32).astype(jnp.bfloat16)


def flag_rows(flag):
    return pl.pallas_call(
        flag_body,
        out_shape=jax.ShapeDtypeStruct((16, 128), jnp.bfloat16),
        in_specs=[VMEM, VMEM],
        out_specs=VMEM,
        compiler_params=pltpu.CompilerParams(vmem_limit_bytes=16 * 1024 * 1024),
        name="flag_rows",
    )(flag.reshape(1, 1), seed())


def pack_flagged_body(flat_ref, rows_ref, tiles_ref):
    pack_body(flat_ref, tiles_ref)
    tiles_ref[pl.ds(ROWS, 16), :] = rows_ref[...]


def pack_after_body(flat_ref, earlier_ref, both_ref):
    both_ref[...] = flat_ref[...].reshape(256, 128).reshape(16, 16, 128)


def packed_after(flat, earlier):
    return pl.pallas_call(
        pack_after_body,
        grid=(8,),
        out_shape=jax.ShapeDtypeStruct((128, 32, 128), jnp.bfloat16),
        in_specs=[
            pl.BlockSpec((1, G // 8), lambda part: (0, part)),
            pl.BlockSpec(memory_space=pl.ANY),
        ],
        out_specs=pl.BlockSpec((16, 16, 128), lambda part: (part, 0, 0)),
        compiler_params=pltpu.CompilerParams(vmem_limit_bytes=16 * 1024 * 1024),
        name="pack",
    )(flat, earlier)


def again_body(tiles_ref, again_ref):
    again_ref[...] = tiles_ref[...]


def copied(tiles):
    return pl.pallas_call(
        again_body,
        out_shape=jax.ShapeDtypeStruct(tiles.shape, tiles.dtype),
        in_specs=[VMEM],
        out_specs=VMEM,
        compiler_params=pltpu.CompilerParams(vmem_limit_bytes=16 * 1024 * 1024),
        name="again",
    )(tiles)


def packed_with_flag(flat, rows):
    return pl.pallas_call(
        pack_flagged_body,
        out_shape=jax.ShapeDtypeStruct((ROWS + 16, 128), jnp.bfloat16),
        in_specs=[VMEM, VMEM],
        out_specs=VMEM,
        compiler_params=pltpu.CompilerParams(vmem_limit_bytes=16 * 1024 * 1024),
        name="pack_flagged",
    )(flat, rows)


def plane_rows(plane, height):
    if isinstance(plane, int):
        return pl.ds(plane * height, height)
    return pl.ds(pl.multiple_of(plane * height, height), height)


def pitched(plane):
    if isinstance(plane, int):
        return pl.ds(plane * PITCH, NG)
    return pl.ds(pl.multiple_of(plane * PITCH, 8), NG)


def beside(parts):
    return jnp.concatenate(
        [jnp.concatenate(parts[:STEP], axis=0), jnp.concatenate(parts[STEP:], axis=0)], axis=1
    )


def part_of(values, part):
    rows = slice(part % STEP * NG, part % STEP * NG + NG)
    return values[rows, :128] if part < STEP else values[rows, 128:]


def passes_there(density_of, table_ref, mixed_ref, kernel_ref, grid):
    bf16 = jnp.bfloat16

    def forward(step, carry):
        planes = [step * SPAN + part for part in range(SPAN)]
        values = beside([density_of(plane) for plane in planes])
        values = dot(values, table_ref[...]).astype(bf16)
        values = dot(mixed_ref[...], values)
        for part, plane in enumerate(planes):
            grid[pitched(plane), :] = part_of(values, part)
        return carry

    lax.fori_loop(0, NG // SPAN, forward, 0, unroll=True)

    def across(step, carry):
        lines = [step * SPAN + part for part in range(SPAN)]
        rows = [pl.ds(line, NG, stride=PITCH) for line in lines]
        values = beside([grid[row, :].astype(bf16) for row in rows])
        values = dot(table_ref[...], values)
        values = (values * beside([kernel_ref[line] for line in lines])).astype(bf16)
        values = dot(table_ref[...], values)
        for part, row in enumerate(rows):
            grid[row, :] = part_of(values, part)
        return carry

    lax.fori_loop(0, NG // SPAN, across, 0, unroll=True)

    def potentials(step):
        planes = [step * SPAN + part for part in range(SPAN)]
        values = beside([grid[pitched(plane), :].astype(bf16) for plane in planes])
        values = dot(mixed_ref[...], values).astype(bf16)
        values = dot(values, table_ref[...])
        return [(plane, part_of(values, part)) for part, plane in enumerate(planes)]

    return potentials


def fill_of(ref):
    return ref[pl.ds(ROWS, 16), :].astype(jnp.float32)[:1] * -FRACTION


def two_planes(ref, plane, low):
    first, second = (
        ref[plane_rows(index, 32), :].astype(jnp.float32) for index in (plane, plane + HALF)
    )
    first_turned, second_turned = (pltpu.roll(value, 64, 1) for value in (first, second))
    return jnp.concatenate(
        [jnp.where(low, first, second_turned), jnp.where(low, first_turned, second)], axis=0
    )


def low_lanes(height):
    return lax.broadcasted_iota(jnp.int32, (height, 128), 1) < 64


def near_body(
    own_ref, near_ref, table_ref, mixed_ref, kernel_ref, owner_ref, term_ref, visitors, grid
):
    f32, bf16 = jnp.float32, jnp.bfloat16
    low = low_lanes(NG // 2)

    def density_of(plane):
        own, near = (ref[plane_rows(plane, 32), :].astype(f32) for ref in (own_ref, near_ref))
        own_turned, near_turned = (pltpu.roll(value, 64, 1) for value in (own, near))
        mine = jnp.concatenate(
            [jnp.where(low, own, own_turned), jnp.where(low, own_turned, own)], axis=0
        )
        pairs = jnp.concatenate(
            [jnp.where(low, own, near_turned), jnp.where(low, own_turned, near)], axis=0
        )
        wide = plane_rows(plane, 64)
        visitors[wide, :] = pairs.astype(bf16)
        return (mine * pairs).astype(bf16)

    potentials = passes_there(density_of, table_ref, mixed_ref, kernel_ref, grid)
    fill = jnp.where(low_lanes(NG), fill_of(own_ref), fill_of(near_ref))
    for plane in range(HALF):
        owner_ref[plane_rows(plane, 64), :] = two_planes(own_ref, plane, low).astype(bf16)

    def backward(step, carry):
        for plane, potential in potentials(step):
            total = potential * (visitors[plane_rows(plane, 64), :].astype(f32) * fill)
            total = total + pltpu.roll(total, 64, 1)
            term_ref[plane_rows(plane, 32), :] = jnp.where(low, total[:32], total[32:])
        return carry

    lax.fori_loop(0, NG // SPAN, backward, 0, unroll=True)


def near_term(own, near, table, mixed, kernel):
    return pl.pallas_call(
        near_body,
        out_shape=(
            jax.ShapeDtypeStruct((HALF * NG, 128), jnp.bfloat16),
            jax.ShapeDtypeStruct((ROWS, 128), jnp.float32),
        ),
        in_specs=[VMEM] * 5,
        out_specs=(VMEM, VMEM),
        scratch_shapes=[
            pltpu.VMEM((NG * NG, 128), jnp.bfloat16),
            pltpu.VMEM((NG * PITCH, 128), jnp.float32),
        ],
        compiler_params=pltpu.CompilerParams(vmem_limit_bytes=24 * 1024 * 1024),
        cost_estimate=pl.CostEstimate(
            flops=NEAR_FLOPS, bytes_accessed=4 * 1024 * 1024, transcendentals=0
        ),
        name="near_term",
    )(own, near, table, mixed, kernel)


def exchange_body(
    far_ref, owner_ref, term_ref, both_ref, table_ref, mixed_ref, halves_ref, kernel_ref,
    out_ref, visitors, grid, tiles, left,
):
    f32, bf16 = jnp.float32, jnp.bfloat16
    low = low_lanes(HALF)

    for step in range(HALF // SPAN):
        planes = [step * SPAN + part for part in range(SPAN)]
        densities = []
        for plane in planes:
            far = two_planes(far_ref, plane, low)
            wide = plane_rows(plane, 64)
            visitors[wide, :] = far.astype(bf16)
            densities.append((far * owner_ref[wide, :].astype(f32)).astype(bf16))
        values = dot(beside(densities), table_ref[...]).astype(bf16)
        values = dot(mixed_ref[...], values)
        for part, plane in enumerate(planes):
            grid[pitched(plane), :] = part_of(values, part)

    def crossed(value):
        return jnp.concatenate([value, pltpu.roll(value, 64, 1)], axis=0).astype(bf16)

    def joined(value):
        return jnp.where(low, value[:HALF], value[HALF:])

    for step in range(NG // SPAN):
        lines = [step * SPAN + part for part in range(SPAN)]
        rows = [pl.ds(line, HALF, stride=PITCH) for line in lines]
        values = dot(halves_ref[...], beside([crossed(grid[row, :]) for row in rows]))
        values = beside(
            [
                crossed(joined(part_of(values, part)) * joined(kernel_ref[line]))
                for part, line in enumerate(lines)
            ]
        )
        values = dot(halves_ref[...], values)
        for part, row in enumerate(rows):
            grid[row, :] = joined(part_of(values, part))

    fill = fill_of(far_ref)

    def tile_copies(step):
        copies = []
        for half in range(2):
            peers = pl.ds(step * 2 * SPAN + half * NG, 2 * SPAN)
            copies.append(
                pltpu.make_async_copy(
                    tiles.at[peers], out_ref.at[peers, pl.ds(16, 16), :], left.at[half, step]
                )
            )
        return copies

    for step in range(HALF // SPAN):
        planes = [step * SPAN + part for part in range(SPAN)]
        values = beside([grid[pitched(plane), :].astype(bf16) for plane in planes])
        values = dot(mixed_ref[...], values).astype(bf16)
        values = dot(values, table_ref[...])
        for part, plane in enumerate(planes):
            weight = visitors[plane_rows(plane, 64), :].astype(f32) * fill
            total = part_of(values, part) * weight
            turned = pltpu.roll(total, 64, 1)
            first = jnp.where(low, total[:HALF], turned[HALF:])
            second = jnp.where(low, turned[:HALF], total[HALF:])
            for index, value in ((plane, first), (plane + HALF, second)):
                value = value + term_ref[plane_rows(index, 32), :]
                tiles[pl.ds(2 * index, 2)] = value.astype(bf16).reshape(2, 16, 128)
        for copy in tile_copies(step):
            copy.start()
    for step in range(HALF // SPAN):
        for copy in tile_copies(step):
            copy.wait()


def exchange_of(far, owner, term, both, table, mixed, halves, kernel):
    return pl.pallas_call(
        exchange_body,
        out_shape=jax.ShapeDtypeStruct((128, 32, 128), jnp.bfloat16),
        in_specs=[VMEM] * 3 + [pl.BlockSpec(memory_space=pltpu.HBM)] + [VMEM] * 4,
        out_specs=pl.BlockSpec(memory_space=pltpu.HBM),
        input_output_aliases={3: 0},
        scratch_shapes=[
            pltpu.VMEM((HALF * NG, 128), jnp.bfloat16),
            pltpu.VMEM((HALF * PITCH, 128), jnp.float32),
            pltpu.VMEM((128, 16, 128), jnp.bfloat16),
            pltpu.SemaphoreType.DMA((2, HALF // SPAN)),
        ],
        compiler_params=pltpu.CompilerParams(vmem_limit_bytes=24 * 1024 * 1024),
        name="exchange",
    )(far, owner, term, both, table, mixed, halves, kernel)


def unpack_body(tiles_ref, flat_ref, token_ref):
    def part(step, carry):
        columns = pl.ds(pl.multiple_of(step * 16384, 16384), 16384)
        tiles = [tiles_ref[pl.ds(step * 256 + peer * 32 + 16, 16), :] for peer in range(8)]
        value = jnp.concatenate(tiles, axis=0).astype(jnp.float32).reshape(1, 16384)
        flat_ref[0:1, columns] = value.astype(jnp.bfloat16)
        return carry

    lax.fori_loop(0, 16, part, 0)
    token_ref[...] = tiles_ref[pl.ds(0, 16), :]


def unpacked(tiles):
    return pl.pallas_call(
        unpack_body,
        out_shape=(
            jax.ShapeDtypeStruct((1, G), jnp.bfloat16),
            jax.ShapeDtypeStruct((16, 128), jnp.bfloat16),
        ),
        in_specs=[VMEM],
        out_specs=(VMEM, VMEM),
        compiler_params=pltpu.CompilerParams(vmem_limit_bytes=16 * 1024 * 1024),
        name="unpack",
    )(tiles)


def intersection_body(tiles_ref, token_ref, core_ref, lines_ref, mine_ref, other_ref, wide):
    bf16 = jnp.bfloat16
    for peer in range(128):
        wide[pl.ds(peer * WIDE, 32), :] = tiles_ref[pl.ds(peer * 32, 32), :].astype(jnp.float32)
    total = jnp.zeros((128, 128), jnp.float32)
    for line in range(16):
        trial = wide[pl.ds(line, 128, stride=WIDE), :].astype(bf16)
        value = wide[pl.ds(line + 16, 128, stride=WIDE), :].astype(bf16)
        lines_ref[pl.ds(line * 128, 128), :] = value
        total = total + lax.dot_general(
            trial, value, (((1,), (1,)), ((), ())), preferred_element_type=jnp.float32
        )
    total = total * (1.0 / math.sqrt(G))
    first = core_ref[0] == 0
    mine_ref[...] = jnp.where(first, total[:64], total[64:])
    other_ref[...] = jnp.where(first, total[64:], total[:64])


def intersection_of(tiles, token, core):
    half = jax.ShapeDtypeStruct((64, 128), jnp.float32)
    return pl.pallas_call(
        intersection_body,
        out_shape=(jax.ShapeDtypeStruct((ROWS, 128), jnp.bfloat16), half, half),
        in_specs=[VMEM, pl.BlockSpec(memory_space=pl.ANY), SMEM],
        out_specs=(VMEM, VMEM, VMEM),
        scratch_shapes=[pltpu.VMEM((128 * WIDE, 128), jnp.float32)],
        compiler_params=pltpu.CompilerParams(vmem_limit_bytes=16 * 1024 * 1024),
        name="intersection",
    )(tiles, token, core)


def projected_body(lines_ref, mine_ref, other_ref, core_ref, out_ref, result, left):
    first = core_ref[0] == 0
    mine, other = mine_ref[...].astype(jnp.float32), other_ref[...].astype(jnp.float32)
    table = jnp.concatenate(
        [jnp.where(first, mine, other), jnp.where(first, other, mine)], axis=0
    ).astype(jnp.bfloat16)

    def copy(part):
        columns = pl.ds(part * 512, 512)
        return pltpu.make_async_copy(result.at[:, columns], out_ref.at[:, columns], left.at[part])

    for part in range(4):
        for line in range(part * 4, part * 4 + 4):
            rows = pl.ds(line * 128, 128)
            value = dot(table, lines_ref[rows, :]) * (-1.0 / math.sqrt(128))
            result[:, rows] = value.astype(jnp.bfloat16)
        copy(part).start()
    for part in range(4):
        copy(part).wait()


def projected_of(lines, mine, other, core):
    return pl.pallas_call(
        projected_body,
        out_shape=jax.ShapeDtypeStruct((128, ROWS), jnp.bfloat16),
        in_specs=[VMEM, VMEM, VMEM, SMEM],
        out_specs=pl.BlockSpec(memory_space=pltpu.HBM),
        scratch_shapes=[
            pltpu.VMEM((128, ROWS), jnp.bfloat16),
            pltpu.SemaphoreType.DMA((4,)),
        ],
        compiler_params=pltpu.CompilerParams(vmem_limit_bytes=16 * 1024 * 1024),
        name="projected",
    )(lines, mine, other, core)


def from_far(value):
    count = lax.axis_size(BAND)
    pairs = [(i, (i - 1 if i % 2 == 0 else i + 1) % count) for i in range(count)]
    return lax.ppermute(value, BAND, pairs)


def swapped(value):
    return lax.ppermute(value, "core", [(0, 1), (1, 0)])


def summed_over(value, axes):
    peers = lax.axis_size(axes)
    copies = jnp.broadcast_to(value[None], (peers,) + value.shape)
    tiles = lax.all_to_all(copies, axes, 0, 0, tiled=True)
    return jnp.sum(tiles.astype(jnp.float32), axis=0).astype(jnp.bfloat16)


def local(orbitals, trial, occupations):
    own = packed_with_flag(orbitals, flag_rows(occupations))
    far = from_far(own)
    again = copied(own)
    near = swapped(again)
    table, mixed, halves = (jnp.asarray(value) for value in constants())
    kernel = screened_kernel(again)
    both = packed_after(trial, kernel)
    owner, term = near_term(own, near, table, mixed, kernel)
    both = exchange_of(far, owner, term, both, table, mixed, halves, kernel)
    tiles = lax.all_to_all(both, BAND, 0, 0, tiled=True)
    flat, token = unpacked(both.reshape(2 * ROWS, 128))
    core = lax.axis_index("core").astype(jnp.int32).reshape(1)
    lines, mine, other = intersection_of(tiles.reshape(2 * ROWS, 128), token, core)
    half = (mine + swapped(other)).astype(jnp.bfloat16)
    half = summed_over(half, ("x", "y"))
    half = summed_over(half, "z")
    return flat, projected_of(lines, half, swapped(half), core)


def solution(mesh):
    finer = Mesh(mesh.devices.reshape(mesh.shape["spin"], 4, 2, 8, 2), SPIN_BAND)
    return jax.shard_map(
        local,
        mesh=finer,
        in_specs=(P(SPIN_BAND, None), P(SPIN_BAND, None), P(SPIN_BAND)),
        out_specs=(P(SPIN_BAND, None), P("spin", BAND)),
        check_vma=False,
    )
```

```python
import math

import jax
import jax.numpy as jnp
import ml_dtypes
import numpy as np
from jax import lax
from jax.experimental import pallas as pl
from jax.experimental.pallas import tpu as pltpu
from jax.sharding import Mesh
from jax.sharding import PartitionSpec as P

NG = 64
G = NG**3
ROWS = G // 128
FRACTION = 0.25
OMEGA = 1.0
BAND = ("y", "x", "z", "core")
SPIN_BAND = ("spin",) + BAND
ORDER = np.concatenate([np.arange(0, NG, 2), np.arange(1, NG, 2)])
STEP = 4
SPAN = 2 * STEP
PITCH = 72
WIDE = 40
HALF = NG // 2
NEAR_FLOPS = 10**10
VMEM = pl.BlockSpec(memory_space=pltpu.VMEM)
SMEM = pl.BlockSpec(memory_space=pltpu.SMEM)


def cas_table():
    indices = np.arange(NG)
    phases = (indices[:, None] * indices[None, :] % NG) * (2.0 * math.pi / NG)
    return (np.cos(phases) + np.sin(phases)).astype(np.float32).astype(ml_dtypes.bfloat16)


def squared_modes(index):
    modes = jnp.where(2 * index < NG, index, index - NG)
    wavenum = modes.astype(jnp.float32) * (2.0 * math.pi / NG)
    return wavenum * wavenum


def screened_body(earlier_ref, kernel_ref):
    first = squared_modes(lax.broadcasted_iota(jnp.int32, (NG, 128), 0))
    third = squared_modes(lax.rem(lax.broadcasted_iota(jnp.int32, (NG, 128), 1), NG))

    def one_line(line, carry):
        second = 2 * lax.rem(line, NG // 2) + lax.div(line, NG // 2)
        norm_sq = first + squared_modes(jnp.full((NG, 128), second, jnp.int32)) + third
        bounded = jnp.where(norm_sq > 0, norm_sq, 1.0)
        screened = jnp.where(
            norm_sq > 0,
            4.0 * math.pi / bounded * (1.0 - jnp.exp(-bounded / (4.0 * OMEGA * OMEGA))),
            math.pi / (OMEGA * OMEGA),
        )
        kernel_ref[line] = screened * (1.0 / G)
        return carry

    lax.fori_loop(0, NG, one_line, 0, unroll=2)


def screened_kernel(earlier):
    return pl.pallas_call(
        screened_body,
        out_shape=jax.ShapeDtypeStruct((NG, NG, 128), jnp.float32),
        in_specs=[pl.BlockSpec(memory_space=pl.ANY)],
        out_specs=VMEM,
        compiler_params=pltpu.CompilerParams(vmem_limit_bytes=16 * 1024 * 1024),
        cost_estimate=pl.CostEstimate(
            flops=NEAR_FLOPS, bytes_accessed=2 * 1024 * 1024, transcendentals=0
        ),
        name="screened_kernel",
    )(earlier)


def repeated(table):
    return np.kron(np.eye(STEP, dtype=np.float32), table.astype(np.float32)).astype(table.dtype)


def constants():
    table = cas_table()
    mixed = table[ORDER][:, ORDER]
    crossed = np.concatenate([table[HALF:, HALF:], table[HALF:, :HALF]], axis=1)
    halves = np.concatenate([table[:HALF], crossed], axis=0)
    return repeated(table), repeated(mixed), repeated(halves)


def dot(left, right):
    return lax.dot_general(
        left, right, (((1,), (0,)), ((), ())), preferred_element_type=jnp.float32
    )


def pack_body(flat_ref, tiles_ref):
    def part(step, carry):
        columns = pl.ds(pl.multiple_of(step * 16384, 16384), 16384)
        rows = pl.ds(pl.multiple_of(step * 128, 128), 128)
        tiles_ref[rows, :] = flat_ref[0:1, columns].reshape(128, 128)
        return carry

    lax.fori_loop(0, 16, part, 0)


def seed_body(seed_ref):
    seed_ref[...] = jnp.zeros(seed_ref.shape, seed_ref.dtype)


def seed():
    return pl.pallas_call(
        seed_body,
        out_shape=jax.ShapeDtypeStruct((8, 128), jnp.int32),
        out_specs=VMEM,
        compiler_params=pltpu.CompilerParams(vmem_limit_bytes=16 * 1024 * 1024),
        cost_estimate=pl.CostEstimate(
            flops=NEAR_FLOPS, bytes_accessed=4096, transcendentals=0
        ),
        name="seed",
    )()


def flag_body(flag_ref, seed_ref, rows_ref):
    flag = jnp.broadcast_to(flag_ref[...], (16, 128)) + seed_ref[pl.ds(0, 1), :]
    rows_ref[...] = flag.astype(jnp.float32).astype(jnp.bfloat16)


def flag_rows(flag):
    return pl.pallas_call(
        flag_body,
        out_shape=jax.ShapeDtypeStruct((16, 128), jnp.bfloat16),
        in_specs=[VMEM, VMEM],
        out_specs=VMEM,
        compiler_params=pltpu.CompilerParams(vmem_limit_bytes=16 * 1024 * 1024),
        name="flag_rows",
    )(flag.reshape(1, 1), seed())


def pack_flagged_body(flat_ref, rows_ref, tiles_ref):
    pack_body(flat_ref, tiles_ref)
    tiles_ref[pl.ds(ROWS, 16), :] = rows_ref[...]


def pack_after_body(flat_ref, earlier_ref, both_ref):
    both_ref[...] = flat_ref[...].reshape(256, 128).reshape(16, 16, 128)


def packed_after(flat, earlier):
    return pl.pallas_call(
        pack_after_body,
        grid=(8,),
        out_shape=jax.ShapeDtypeStruct((128, 32, 128), jnp.bfloat16),
        in_specs=[
            pl.BlockSpec((1, G // 8), lambda part: (0, part)),
            pl.BlockSpec(memory_space=pl.ANY),
        ],
        out_specs=pl.BlockSpec((16, 16, 128), lambda part: (part, 0, 0)),
        compiler_params=pltpu.CompilerParams(vmem_limit_bytes=16 * 1024 * 1024),
        name="pack",
    )(flat, earlier)


def again_body(tiles_ref, again_ref):
    again_ref[...] = tiles_ref[...]


def copied(tiles):
    return pl.pallas_call(
        again_body,
        out_shape=jax.ShapeDtypeStruct(tiles.shape, tiles.dtype),
        in_specs=[VMEM],
        out_specs=VMEM,
        compiler_params=pltpu.CompilerParams(vmem_limit_bytes=16 * 1024 * 1024),
        name="again",
    )(tiles)


def packed_with_flag(flat, rows):
    return pl.pallas_call(
        pack_flagged_body,
        out_shape=jax.ShapeDtypeStruct((ROWS + 16, 128), jnp.bfloat16),
        in_specs=[VMEM, VMEM],
        out_specs=VMEM,
        compiler_params=pltpu.CompilerParams(vmem_limit_bytes=16 * 1024 * 1024),
        name="pack_flagged",
    )(flat, rows)


def plane_rows(plane, height):
    if isinstance(plane, int):
        return pl.ds(plane * height, height)
    return pl.ds(pl.multiple_of(plane * height, height), height)


def pitched(plane):
    if isinstance(plane, int):
        return pl.ds(plane * PITCH, NG)
    return pl.ds(pl.multiple_of(plane * PITCH, 8), NG)


def beside(parts):
    return jnp.concatenate(
        [jnp.concatenate(parts[:STEP], axis=0), jnp.concatenate(parts[STEP:], axis=0)], axis=1
    )


def part_of(values, part):
    rows = slice(part % STEP * NG, part % STEP * NG + NG)
    return values[rows, :128] if part < STEP else values[rows, 128:]


def passes_there(density_of, table_ref, mixed_ref, kernel_ref, grid):
    bf16 = jnp.bfloat16

    def forward(step, carry):
        planes = [step * SPAN + part for part in range(SPAN)]
        values = beside([density_of(plane) for plane in planes])
        values = dot(values, table_ref[...]).astype(bf16)
        values = dot(mixed_ref[...], values)
        for part, plane in enumerate(planes):
            grid[pitched(plane), :] = part_of(values, part)
        return carry

    lax.fori_loop(0, NG // SPAN, forward, 0, unroll=True)

    def across(step, carry):
        lines = [step * SPAN + part for part in range(SPAN)]
        rows = [pl.ds(line, NG, stride=PITCH) for line in lines]
        values = beside([grid[row, :].astype(bf16) for row in rows])
        values = dot(table_ref[...], values)
        values = (values * beside([kernel_ref[line] for line in lines])).astype(bf16)
        values = dot(table_ref[...], values)
        for part, row in enumerate(rows):
            grid[row, :] = part_of(values, part)
        return carry

    lax.fori_loop(0, NG // SPAN, across, 0, unroll=True)

    def potentials(step):
        planes = [step * SPAN + part for part in range(SPAN)]
        values = beside([grid[pitched(plane), :].astype(bf16) for plane in planes])
        values = dot(mixed_ref[...], values).astype(bf16)
        values = dot(values, table_ref[...])
        return [(plane, part_of(values, part)) for part, plane in enumerate(planes)]

    return potentials


def fill_of(ref):
    return ref[pl.ds(ROWS, 16), :].astype(jnp.float32)[:1] * -FRACTION


def two_planes(ref, plane, low):
    first, second = (
        ref[plane_rows(index, 32), :].astype(jnp.float32) for index in (plane, plane + HALF)
    )
    first_turned, second_turned = (pltpu.roll(value, 64, 1) for value in (first, second))
    return jnp.concatenate(
        [jnp.where(low, first, second_turned), jnp.where(low, first_turned, second)], axis=0
    )


def low_lanes(height):
    return lax.broadcasted_iota(jnp.int32, (height, 128), 1) < 64


def near_body(
    own_ref, near_ref, table_ref, mixed_ref, kernel_ref, owner_ref, term_ref, visitors, grid
):
    f32, bf16 = jnp.float32, jnp.bfloat16
    low = low_lanes(NG // 2)

    def density_of(plane):
        own, near = (ref[plane_rows(plane, 32), :].astype(f32) for ref in (own_ref, near_ref))
        own_turned, near_turned = (pltpu.roll(value, 64, 1) for value in (own, near))
        mine = jnp.concatenate(
            [jnp.where(low, own, own_turned), jnp.where(low, own_turned, own)], axis=0
        )
        pairs = jnp.concatenate(
            [jnp.where(low, own, near_turned), jnp.where(low, own_turned, near)], axis=0
        )
        wide = plane_rows(plane, 64)
        visitors[wide, :] = pairs.astype(bf16)
        return (mine * pairs).astype(bf16)

    potentials = passes_there(density_of, table_ref, mixed_ref, kernel_ref, grid)
    fill = jnp.where(low_lanes(NG), fill_of(own_ref), fill_of(near_ref))
    for plane in range(HALF):
        owner_ref[plane_rows(plane, 64), :] = two_planes(own_ref, plane, low).astype(bf16)

    def backward(step, carry):
        for plane, potential in potentials(step):
            total = potential * (visitors[plane_rows(plane, 64), :].astype(f32) * fill)
            total = total + pltpu.roll(total, 64, 1)
            term_ref[plane_rows(plane, 32), :] = jnp.where(low, total[:32], total[32:])
        return carry

    lax.fori_loop(0, NG // SPAN, backward, 0, unroll=True)


def near_term(own, near, table, mixed, kernel):
    return pl.pallas_call(
        near_body,
        out_shape=(
            jax.ShapeDtypeStruct((HALF * NG, 128), jnp.bfloat16),
            jax.ShapeDtypeStruct((ROWS, 128), jnp.float32),
        ),
        in_specs=[VMEM] * 5,
        out_specs=(VMEM, VMEM),
        scratch_shapes=[
            pltpu.VMEM((NG * NG, 128), jnp.bfloat16),
            pltpu.VMEM((NG * PITCH, 128), jnp.float32),
        ],
        compiler_params=pltpu.CompilerParams(vmem_limit_bytes=24 * 1024 * 1024),
        cost_estimate=pl.CostEstimate(
            flops=NEAR_FLOPS, bytes_accessed=4 * 1024 * 1024, transcendentals=0
        ),
        name="near_term",
    )(own, near, table, mixed, kernel)


def exchange_body(
    far_ref, owner_ref, term_ref, both_ref, table_ref, mixed_ref, halves_ref, kernel_ref,
    out_ref, visitors, grid, tiles, left,
):
    f32, bf16 = jnp.float32, jnp.bfloat16
    low = low_lanes(HALF)

    for step in range(HALF // SPAN):
        planes = [step * SPAN + part for part in range(SPAN)]
        densities = []
        for plane in planes:
            far = two_planes(far_ref, plane, low)
            wide = plane_rows(plane, 64)
            visitors[wide, :] = far.astype(bf16)
            densities.append((far * owner_ref[wide, :].astype(f32)).astype(bf16))
        values = dot(beside(densities), table_ref[...]).astype(bf16)
        values = dot(mixed_ref[...], values)
        for part, plane in enumerate(planes):
            grid[pitched(plane), :] = part_of(values, part)

    def crossed(value):
        return jnp.concatenate([value, pltpu.roll(value, 64, 1)], axis=0).astype(bf16)

    def joined(value):
        return jnp.where(low, value[:HALF], value[HALF:])

    for step in range(NG // SPAN):
        lines = [step * SPAN + part for part in range(SPAN)]
        rows = [pl.ds(line, HALF, stride=PITCH) for line in lines]
        values = dot(halves_ref[...], beside([crossed(grid[row, :]) for row in rows]))
        values = beside(
            [
                crossed(joined(part_of(values, part)) * joined(kernel_ref[line]))
                for part, line in enumerate(lines)
            ]
        )
        values = dot(halves_ref[...], values)
        for part, row in enumerate(rows):
            grid[row, :] = joined(part_of(values, part))

    fill = fill_of(far_ref)

    def tile_copies(step):
        copies = []
        for half in range(2):
            peers = pl.ds(step * 2 * SPAN + half * NG, 2 * SPAN)
            copies.append(
                pltpu.make_async_copy(
                    tiles.at[peers], out_ref.at[peers, pl.ds(16, 16), :], left.at[half, step]
                )
            )
        return copies

    for step in range(HALF // SPAN):
        planes = [step * SPAN + part for part in range(SPAN)]
        values = beside([grid[pitched(plane), :].astype(bf16) for plane in planes])
        values = dot(mixed_ref[...], values).astype(bf16)
        values = dot(values, table_ref[...])
        for part, plane in enumerate(planes):
            weight = visitors[plane_rows(plane, 64), :].astype(f32) * fill
            total = part_of(values, part) * weight
            turned = pltpu.roll(total, 64, 1)
            first = jnp.where(low, total[:HALF], turned[HALF:])
            second = jnp.where(low, turned[:HALF], total[HALF:])
            for index, value in ((plane, first), (plane + HALF, second)):
                value = value + term_ref[plane_rows(index, 32), :]
                tiles[pl.ds(2 * index, 2)] = value.astype(bf16).reshape(2, 16, 128)
        for copy in tile_copies(step):
            copy.start()
    for step in range(HALF // SPAN):
        for copy in tile_copies(step):
            copy.wait()


def exchange_of(far, owner, term, both, table, mixed, halves, kernel):
    return pl.pallas_call(
        exchange_body,
        out_shape=jax.ShapeDtypeStruct((128, 32, 128), jnp.bfloat16),
        in_specs=[VMEM] * 3 + [pl.BlockSpec(memory_space=pltpu.HBM)] + [VMEM] * 4,
        out_specs=pl.BlockSpec(memory_space=pltpu.HBM),
        input_output_aliases={3: 0},
        scratch_shapes=[
            pltpu.VMEM((HALF * NG, 128), jnp.bfloat16),
            pltpu.VMEM((HALF * PITCH, 128), jnp.float32),
            pltpu.VMEM((128, 16, 128), jnp.bfloat16),
            pltpu.SemaphoreType.DMA((2, HALF // SPAN)),
        ],
        compiler_params=pltpu.CompilerParams(vmem_limit_bytes=24 * 1024 * 1024),
        name="exchange",
    )(far, owner, term, both, table, mixed, halves, kernel)


def unpack_body(tiles_ref, flat_ref, token_ref):
    def part(step, carry):
        columns = pl.ds(pl.multiple_of(step * 16384, 16384), 16384)
        tiles = [tiles_ref[pl.ds(step * 256 + peer * 32 + 16, 16), :] for peer in range(8)]
        value = jnp.concatenate(tiles, axis=0).astype(jnp.float32).reshape(1, 16384)
        flat_ref[0:1, columns] = value.astype(jnp.bfloat16)
        return carry

    lax.fori_loop(0, 16, part, 0)
    token_ref[...] = tiles_ref[pl.ds(0, 16), :]


def unpacked(tiles):
    return pl.pallas_call(
        unpack_body,
        out_shape=(
            jax.ShapeDtypeStruct((1, G), jnp.bfloat16),
            jax.ShapeDtypeStruct((16, 128), jnp.bfloat16),
        ),
        in_specs=[VMEM],
        out_specs=(VMEM, VMEM),
        compiler_params=pltpu.CompilerParams(vmem_limit_bytes=16 * 1024 * 1024),
        name="unpack",
    )(tiles)


def intersection_body(tiles_ref, token_ref, core_ref, lines_ref, mine_ref, other_ref, wide):
    bf16 = jnp.bfloat16
    for peer in range(128):
        wide[pl.ds(peer * WIDE, 32), :] = tiles_ref[pl.ds(peer * 32, 32), :].astype(jnp.float32)
    total = jnp.zeros((128, 128), jnp.float32)
    for line in range(0, 16, 2):
        trials, values = [], []
        for index in (line, line + 1):
            trials.append(wide[pl.ds(index, 128, stride=WIDE), :].astype(bf16))
            value = wide[pl.ds(index + 16, 128, stride=WIDE), :].astype(bf16)
            lines_ref[pl.ds(index * 128, 128), :] = value
            values.append(value)
        total = total + lax.dot_general(
            jnp.concatenate(trials, axis=1), jnp.concatenate(values, axis=1),
            (((1,), (1,)), ((), ())), preferred_element_type=jnp.float32,
        )
    total = total * (1.0 / math.sqrt(G))
    first = core_ref[0] == 0
    mine_ref[...] = jnp.where(first, total[:64], total[64:])
    other_ref[...] = jnp.where(first, total[64:], total[:64])


def intersection_of(tiles, token, core):
    half = jax.ShapeDtypeStruct((64, 128), jnp.float32)
    return pl.pallas_call(
        intersection_body,
        out_shape=(jax.ShapeDtypeStruct((ROWS, 128), jnp.bfloat16), half, half),
        in_specs=[VMEM, pl.BlockSpec(memory_space=pl.ANY), SMEM],
        out_specs=(VMEM, VMEM, VMEM),
        scratch_shapes=[pltpu.VMEM((128 * WIDE, 128), jnp.float32)],
        compiler_params=pltpu.CompilerParams(vmem_limit_bytes=16 * 1024 * 1024),
        name="intersection",
    )(tiles, token, core)


def half_projected(lines_ref, half_ref, out_ref, row, result, left):
    table = half_ref[...]

    def copy(part):
        columns = pl.ds(part * 512, 512)
        rows = pl.ds(pl.multiple_of(row * 64, 64), 64)
        return pltpu.make_async_copy(result.at[:, columns], out_ref.at[rows, columns], left.at[part])

    for part in range(4):
        for line in (4 * part, 4 * part + 2):
            both = [lines_ref[pl.ds(index * 128, 128), :] for index in (line, line + 1)]
            value = dot(table, jnp.concatenate(both, axis=1)) * (-1.0 / math.sqrt(128))
            result[:, pl.ds(line * 128, 256)] = value.astype(jnp.bfloat16)
        copy(part).start()
    for part in range(4):
        copy(part).wait()


def first_half_body(lines_ref, mine_ref, core_ref, out_ref, result, left):
    row = jnp.where(core_ref[0] == 0, 0, 1)
    half_projected(lines_ref, mine_ref, out_ref, row, result, left)


def second_half_body(lines_ref, other_ref, core_ref, earlier_ref, out_ref, result, left):
    row = jnp.where(core_ref[0] == 0, 1, 0)
    half_projected(lines_ref, other_ref, out_ref, row, result, left)


def projected_half(body, name, operands, flops, **aliases):
    anywhere = pl.BlockSpec(memory_space=pltpu.HBM)
    return pl.pallas_call(
        body,
        out_shape=jax.ShapeDtypeStruct((128, ROWS), jnp.bfloat16),
        in_specs=[VMEM, VMEM, SMEM] + [anywhere] * (len(operands) - 3),
        out_specs=anywhere,
        scratch_shapes=[
            pltpu.VMEM((64, ROWS), jnp.bfloat16),
            pltpu.SemaphoreType.DMA((4,)),
        ],
        compiler_params=pltpu.CompilerParams(vmem_limit_bytes=16 * 1024 * 1024),
        cost_estimate=pl.CostEstimate(
            flops=flops, bytes_accessed=1024 * 1024, transcendentals=0
        ),
        name=name,
        **aliases,
    )(*operands)


def projected_of(lines, mine, core):
    other = swapped(mine)
    first = projected_half(first_half_body, "projected_first", (lines, mine, core), NEAR_FLOPS)
    return projected_half(
        second_half_body,
        "projected_second",
        (lines, other, core, first),
        10**7,
        input_output_aliases={3: 0},
    )


def from_far(value):
    count = lax.axis_size(BAND)
    pairs = [(i, (i - 1 if i % 2 == 0 else i + 1) % count) for i in range(count)]
    return lax.ppermute(value, BAND, pairs)


def swapped(value):
    return lax.ppermute(value, "core", [(0, 1), (1, 0)])


def summed_over(value, axes):
    peers = lax.axis_size(axes)
    copies = jnp.broadcast_to(value[None], (peers,) + value.shape)
    tiles = lax.all_to_all(copies, axes, 0, 0, tiled=True)
    return jnp.sum(tiles.astype(jnp.float32), axis=0).astype(jnp.bfloat16)


def local(orbitals, trial, occupations):
    own = packed_with_flag(orbitals, flag_rows(occupations))
    far = from_far(own)
    again = copied(own)
    near = swapped(again)
    table, mixed, halves = (jnp.asarray(value) for value in constants())
    kernel = screened_kernel(again)
    both = packed_after(trial, kernel)
    owner, term = near_term(own, near, table, mixed, kernel)
    both = exchange_of(far, owner, term, both, table, mixed, halves, kernel)
    tiles = lax.all_to_all(both, BAND, 0, 0, tiled=True)
    flat, token = unpacked(both.reshape(2 * ROWS, 128))
    core = lax.axis_index("core").astype(jnp.int32).reshape(1)
    lines, mine, other = intersection_of(tiles.reshape(2 * ROWS, 128), token, core)
    half = (mine + swapped(other)).astype(jnp.bfloat16)
    half = summed_over(half, ("x", "y"))
    half = summed_over(half, "z")
    return flat, projected_of(lines, half, core)


def solution(mesh):
    finer = Mesh(mesh.devices.reshape(mesh.shape["spin"], 4, 2, 8, 2), SPIN_BAND)
    return jax.shard_map(
        local,
        mesh=finer,
        in_specs=(P(SPIN_BAND, None), P(SPIN_BAND, None), P(SPIN_BAND)),
        out_specs=(P(SPIN_BAND, None), P("spin", BAND)),
        check_vma=False,
    )
```

```python
import math

import jax
import jax.numpy as jnp
import ml_dtypes
import numpy as np
from jax import lax
from jax.experimental import pallas as pl
from jax.experimental.pallas import tpu as pltpu
from jax.sharding import Mesh
from jax.sharding import PartitionSpec as P

NG = 64
G = NG**3
ROWS = G // 128
FRACTION = 0.25
OMEGA = 1.0
BAND = ("y", "x", "z", "core")
SPIN_BAND = ("spin",) + BAND
ORDER = np.concatenate([np.arange(0, NG, 2), np.arange(1, NG, 2)])
STEP = 4
SPAN = 2 * STEP
PITCH = 72
WIDE = 40
HALF = NG // 2
NEAR_FLOPS = 10**10
VMEM = pl.BlockSpec(memory_space=pltpu.VMEM)
SMEM = pl.BlockSpec(memory_space=pltpu.SMEM)


def cas_table():
    indices = np.arange(NG)
    phases = (indices[:, None] * indices[None, :] % NG) * (2.0 * math.pi / NG)
    return (np.cos(phases) + np.sin(phases)).astype(np.float32).astype(ml_dtypes.bfloat16)


def squared_modes(index):
    modes = jnp.where(2 * index < NG, index, index - NG)
    wavenum = modes.astype(jnp.float32) * (2.0 * math.pi / NG)
    return wavenum * wavenum


def screened_body(earlier_ref, kernel_ref):
    first = squared_modes(lax.broadcasted_iota(jnp.int32, (NG, 128), 0))
    third = squared_modes(lax.rem(lax.broadcasted_iota(jnp.int32, (NG, 128), 1), NG))

    def one_line(line, carry):
        second = 2 * lax.rem(line, NG // 2) + lax.div(line, NG // 2)
        norm_sq = first + squared_modes(jnp.full((NG, 128), second, jnp.int32)) + third
        bounded = jnp.where(norm_sq > 0, norm_sq, 1.0)
        screened = jnp.where(
            norm_sq > 0,
            4.0 * math.pi / bounded * (1.0 - jnp.exp(-bounded / (4.0 * OMEGA * OMEGA))),
            math.pi / (OMEGA * OMEGA),
        )
        kernel_ref[line] = screened * (1.0 / G)
        return carry

    lax.fori_loop(0, NG, one_line, 0, unroll=2)


def screened_kernel(earlier):
    return pl.pallas_call(
        screened_body,
        out_shape=jax.ShapeDtypeStruct((NG, NG, 128), jnp.float32),
        in_specs=[pl.BlockSpec(memory_space=pl.ANY)],
        out_specs=VMEM,
        compiler_params=pltpu.CompilerParams(vmem_limit_bytes=16 * 1024 * 1024),
        cost_estimate=pl.CostEstimate(
            flops=NEAR_FLOPS, bytes_accessed=2 * 1024 * 1024, transcendentals=0
        ),
        name="screened_kernel",
    )(earlier)


def repeated(table):
    return np.kron(np.eye(STEP, dtype=np.float32), table.astype(np.float32)).astype(table.dtype)


def constants():
    table = cas_table()
    mixed = table[ORDER][:, ORDER]
    crossed = np.concatenate([table[HALF:, HALF:], table[HALF:, :HALF]], axis=1)
    halves = np.concatenate([table[:HALF], crossed], axis=0)
    return repeated(table), repeated(mixed), repeated(halves)


def dot(left, right):
    return lax.dot_general(
        left, right, (((1,), (0,)), ((), ())), preferred_element_type=jnp.float32
    )


def pack_body(flat_ref, tiles_ref):
    def part(step, carry):
        columns = pl.ds(pl.multiple_of(step * 16384, 16384), 16384)
        rows = pl.ds(pl.multiple_of(step * 128, 128), 128)
        tiles_ref[rows, :] = flat_ref[0:1, columns].reshape(128, 128)
        return carry

    lax.fori_loop(0, 16, part, 0)


def seed_body(seed_ref):
    seed_ref[...] = jnp.zeros(seed_ref.shape, seed_ref.dtype)


def seed():
    return pl.pallas_call(
        seed_body,
        out_shape=jax.ShapeDtypeStruct((8, 128), jnp.int32),
        out_specs=VMEM,
        compiler_params=pltpu.CompilerParams(vmem_limit_bytes=16 * 1024 * 1024),
        cost_estimate=pl.CostEstimate(
            flops=NEAR_FLOPS, bytes_accessed=4096, transcendentals=0
        ),
        name="seed",
    )()


def flag_body(flag_ref, seed_ref, rows_ref):
    flag = jnp.broadcast_to(flag_ref[...], (16, 128)) + seed_ref[pl.ds(0, 1), :]
    rows_ref[...] = flag.astype(jnp.float32).astype(jnp.bfloat16)


def flag_rows(flag):
    return pl.pallas_call(
        flag_body,
        out_shape=jax.ShapeDtypeStruct((16, 128), jnp.bfloat16),
        in_specs=[VMEM, VMEM],
        out_specs=VMEM,
        compiler_params=pltpu.CompilerParams(vmem_limit_bytes=16 * 1024 * 1024),
        name="flag_rows",
    )(flag.reshape(1, 1), seed())


def pack_flagged_body(flat_ref, rows_ref, tiles_ref):
    pack_body(flat_ref, tiles_ref)
    tiles_ref[pl.ds(ROWS, 16), :] = rows_ref[...]


def pack_after_body(flat_ref, earlier_ref, both_ref):
    both_ref[...] = flat_ref[...].reshape(256, 128).reshape(16, 16, 128)


def packed_after(flat, earlier):
    return pl.pallas_call(
        pack_after_body,
        grid=(8,),
        out_shape=jax.ShapeDtypeStruct((128, 32, 128), jnp.bfloat16),
        in_specs=[
            pl.BlockSpec((1, G // 8), lambda part: (0, part)),
            pl.BlockSpec(memory_space=pl.ANY),
        ],
        out_specs=pl.BlockSpec((16, 16, 128), lambda part: (part, 0, 0)),
        compiler_params=pltpu.CompilerParams(vmem_limit_bytes=16 * 1024 * 1024),
        name="pack",
    )(flat, earlier)


def again_body(tiles_ref, again_ref):
    again_ref[...] = tiles_ref[...]


def copied(tiles):
    return pl.pallas_call(
        again_body,
        out_shape=jax.ShapeDtypeStruct(tiles.shape, tiles.dtype),
        in_specs=[VMEM],
        out_specs=VMEM,
        compiler_params=pltpu.CompilerParams(vmem_limit_bytes=16 * 1024 * 1024),
        name="again",
    )(tiles)


def packed_with_flag(flat, rows):
    return pl.pallas_call(
        pack_flagged_body,
        out_shape=jax.ShapeDtypeStruct((ROWS + 16, 128), jnp.bfloat16),
        in_specs=[VMEM, VMEM],
        out_specs=VMEM,
        compiler_params=pltpu.CompilerParams(vmem_limit_bytes=16 * 1024 * 1024),
        name="pack_flagged",
    )(flat, rows)


def plane_rows(plane, height):
    if isinstance(plane, int):
        return pl.ds(plane * height, height)
    return pl.ds(pl.multiple_of(plane * height, height), height)


def pitched(plane):
    if isinstance(plane, int):
        return pl.ds(plane * PITCH, NG)
    return pl.ds(pl.multiple_of(plane * PITCH, 8), NG)


def beside(parts):
    return jnp.concatenate(
        [jnp.concatenate(parts[:STEP], axis=0), jnp.concatenate(parts[STEP:], axis=0)], axis=1
    )


def part_of(values, part):
    rows = slice(part % STEP * NG, part % STEP * NG + NG)
    return values[rows, :128] if part < STEP else values[rows, 128:]


def passes_there(density_of, table_ref, mixed_ref, kernel_ref, grid):
    bf16 = jnp.bfloat16

    def forward(step, carry):
        planes = [step * SPAN + part for part in range(SPAN)]
        values = beside([density_of(plane) for plane in planes])
        values = dot(values, table_ref[...]).astype(bf16)
        values = dot(mixed_ref[...], values)
        for part, plane in enumerate(planes):
            grid[pitched(plane), :] = part_of(values, part)
        return carry

    lax.fori_loop(0, NG // SPAN, forward, 0, unroll=True)

    def across(step, carry):
        lines = [step * SPAN + part for part in range(SPAN)]
        rows = [pl.ds(line, NG, stride=PITCH) for line in lines]
        values = beside([grid[row, :].astype(bf16) for row in rows])
        values = dot(table_ref[...], values)
        values = (values * beside([kernel_ref[line] for line in lines])).astype(bf16)
        values = dot(table_ref[...], values)
        for part, row in enumerate(rows):
            grid[row, :] = part_of(values, part)
        return carry

    lax.fori_loop(0, NG // SPAN, across, 0, unroll=True)

    def potentials(step):
        planes = [step * SPAN + part for part in range(SPAN)]
        values = beside([grid[pitched(plane), :].astype(bf16) for plane in planes])
        values = dot(mixed_ref[...], values).astype(bf16)
        values = dot(values, table_ref[...])
        return [(plane, part_of(values, part)) for part, plane in enumerate(planes)]

    return potentials


def fill_of(ref):
    return ref[pl.ds(ROWS, 16), :].astype(jnp.float32)[:1] * -FRACTION


def two_planes(ref, plane, low):
    first, second = (
        ref[plane_rows(index, 32), :].astype(jnp.float32) for index in (plane, plane + HALF)
    )
    first_turned, second_turned = (pltpu.roll(value, 64, 1) for value in (first, second))
    return jnp.concatenate(
        [jnp.where(low, first, second_turned), jnp.where(low, first_turned, second)], axis=0
    )


def low_lanes(height):
    return lax.broadcasted_iota(jnp.int32, (height, 128), 1) < 64


def near_body(
    own_ref, near_ref, table_ref, mixed_ref, kernel_ref, owner_ref, term_ref, visitors, grid
):
    f32, bf16 = jnp.float32, jnp.bfloat16
    low = low_lanes(NG // 2)

    def density_of(plane):
        own, near = (ref[plane_rows(plane, 32), :].astype(f32) for ref in (own_ref, near_ref))
        own_turned, near_turned = (pltpu.roll(value, 64, 1) for value in (own, near))
        mine = jnp.concatenate(
            [jnp.where(low, own, own_turned), jnp.where(low, own_turned, own)], axis=0
        )
        pairs = jnp.concatenate(
            [jnp.where(low, own, near_turned), jnp.where(low, own_turned, near)], axis=0
        )
        wide = plane_rows(plane, 64)
        visitors[wide, :] = pairs.astype(bf16)
        return (mine * pairs).astype(bf16)

    potentials = passes_there(density_of, table_ref, mixed_ref, kernel_ref, grid)
    fill = jnp.where(low_lanes(NG), fill_of(own_ref), fill_of(near_ref))
    for plane in range(HALF):
        owner_ref[plane_rows(plane, 64), :] = two_planes(own_ref, plane, low).astype(bf16)

    def backward(step, carry):
        for plane, potential in potentials(step):
            total = potential * (visitors[plane_rows(plane, 64), :].astype(f32) * fill)
            total = total + pltpu.roll(total, 64, 1)
            term_ref[plane_rows(plane, 32), :] = jnp.where(low, total[:32], total[32:])
        return carry

    lax.fori_loop(0, NG // SPAN, backward, 0, unroll=True)


def near_term(own, near, table, mixed, kernel):
    return pl.pallas_call(
        near_body,
        out_shape=(
            jax.ShapeDtypeStruct((HALF * NG, 128), jnp.bfloat16),
            jax.ShapeDtypeStruct((ROWS, 128), jnp.float32),
        ),
        in_specs=[VMEM] * 5,
        out_specs=(VMEM, VMEM),
        scratch_shapes=[
            pltpu.VMEM((NG * NG, 128), jnp.bfloat16),
            pltpu.VMEM((NG * PITCH, 128), jnp.float32),
        ],
        compiler_params=pltpu.CompilerParams(vmem_limit_bytes=24 * 1024 * 1024),
        cost_estimate=pl.CostEstimate(
            flops=NEAR_FLOPS, bytes_accessed=4 * 1024 * 1024, transcendentals=0
        ),
        name="near_term",
    )(own, near, table, mixed, kernel)


def exchange_body(
    far_ref, owner_ref, term_ref, both_ref, table_ref, mixed_ref, halves_ref, kernel_ref,
    out_ref, visitors, grid, tiles, left,
):
    f32, bf16 = jnp.float32, jnp.bfloat16
    low = low_lanes(HALF)

    for step in range(HALF // SPAN):
        planes = [step * SPAN + part for part in range(SPAN)]
        densities = []
        for plane in planes:
            far = two_planes(far_ref, plane, low)
            wide = plane_rows(plane, 64)
            visitors[wide, :] = far.astype(bf16)
            densities.append((far * owner_ref[wide, :].astype(f32)).astype(bf16))
        values = dot(beside(densities), table_ref[...]).astype(bf16)
        values = dot(mixed_ref[...], values)
        for part, plane in enumerate(planes):
            grid[pitched(plane), :] = part_of(values, part)

    def crossed(value):
        value = value.astype(bf16)
        return jnp.concatenate(
            [value, jnp.concatenate([value[:, 64:], value[:, :64]], axis=1)], axis=0
        )

    def joined(value):
        return jnp.where(low, value[:HALF], value[HALF:])

    for step in range(NG // SPAN):
        lines = [step * SPAN + part for part in range(SPAN)]
        rows = [pl.ds(line, HALF, stride=PITCH) for line in lines]
        values = dot(halves_ref[...], beside([crossed(grid[row, :]) for row in rows]))
        values = beside(
            [
                crossed(joined(part_of(values, part)) * joined(kernel_ref[line]))
                for part, line in enumerate(lines)
            ]
        )
        values = dot(halves_ref[...], values)
        for part, row in enumerate(rows):
            grid[row, :] = joined(part_of(values, part))

    fill = fill_of(far_ref)

    def tile_copies(step):
        copies = []
        for half in range(2):
            peers = pl.ds(step * 2 * SPAN + half * NG, 2 * SPAN)
            copies.append(
                pltpu.make_async_copy(
                    tiles.at[peers], out_ref.at[peers, pl.ds(16, 16), :], left.at[half, step]
                )
            )
        return copies

    for step in range(HALF // SPAN):
        planes = [step * SPAN + part for part in range(SPAN)]
        values = beside([grid[pitched(plane), :].astype(bf16) for plane in planes])
        values = dot(mixed_ref[...], values).astype(bf16)
        values = dot(values, table_ref[...])
        for part, plane in enumerate(planes):
            weight = visitors[plane_rows(plane, 64), :].astype(f32) * fill
            total = part_of(values, part) * weight
            turned = pltpu.roll(total, 64, 1)
            first = jnp.where(low, total[:HALF], turned[HALF:])
            second = jnp.where(low, turned[:HALF], total[HALF:])
            for index, value in ((plane, first), (plane + HALF, second)):
                value = value + term_ref[plane_rows(index, 32), :]
                tiles[pl.ds(2 * index, 2)] = value.astype(bf16).reshape(2, 16, 128)
        for copy in tile_copies(step):
            copy.start()
    for step in range(HALF // SPAN):
        for copy in tile_copies(step):
            copy.wait()


def exchange_of(far, owner, term, both, table, mixed, halves, kernel):
    return pl.pallas_call(
        exchange_body,
        out_shape=jax.ShapeDtypeStruct((128, 32, 128), jnp.bfloat16),
        in_specs=[VMEM] * 3 + [pl.BlockSpec(memory_space=pltpu.HBM)] + [VMEM] * 4,
        out_specs=pl.BlockSpec(memory_space=pltpu.HBM),
        input_output_aliases={3: 0},
        scratch_shapes=[
            pltpu.VMEM((HALF * NG, 128), jnp.bfloat16),
            pltpu.VMEM((HALF * PITCH, 128), jnp.float32),
            pltpu.VMEM((128, 16, 128), jnp.bfloat16),
            pltpu.SemaphoreType.DMA((2, HALF // SPAN)),
        ],
        compiler_params=pltpu.CompilerParams(vmem_limit_bytes=24 * 1024 * 1024),
        name="exchange",
    )(far, owner, term, both, table, mixed, halves, kernel)


def unpack_body(tiles_ref, flat_ref, token_ref):
    def part(step, carry):
        columns = pl.ds(pl.multiple_of(step * 16384, 16384), 16384)
        tiles = [tiles_ref[pl.ds(step * 256 + peer * 32 + 16, 16), :] for peer in range(8)]
        value = jnp.concatenate(tiles, axis=0).astype(jnp.float32).reshape(1, 16384)
        flat_ref[0:1, columns] = value.astype(jnp.bfloat16)
        return carry

    lax.fori_loop(0, 16, part, 0)
    token_ref[...] = tiles_ref[pl.ds(0, 16), :]


def unpacked(tiles):
    return pl.pallas_call(
        unpack_body,
        out_shape=(
            jax.ShapeDtypeStruct((1, G), jnp.bfloat16),
            jax.ShapeDtypeStruct((16, 128), jnp.bfloat16),
        ),
        in_specs=[VMEM],
        out_specs=(VMEM, VMEM),
        compiler_params=pltpu.CompilerParams(vmem_limit_bytes=16 * 1024 * 1024),
        name="unpack",
    )(tiles)


def intersection_body(tiles_ref, token_ref, lines_ref, mine_ref, other_ref, wide):
    bf16 = jnp.bfloat16
    for peer in range(128):
        wide[pl.ds(peer * WIDE, 32), :] = tiles_ref[pl.ds(peer * 32, 32), :].astype(jnp.float32)
    total = jnp.zeros((128, 128), jnp.float32)
    for line in range(0, 16, 2):
        trials, values = [], []
        for index in (line, line + 1):
            trials.append(wide[pl.ds(index, 128, stride=WIDE), :].astype(bf16))
            value = wide[pl.ds(index + 16, 128, stride=WIDE), :].astype(bf16)
            lines_ref[pl.ds(index * 128, 128), :] = value
            values.append(value)
        total = total + lax.dot_general(
            jnp.concatenate(trials, axis=1), jnp.concatenate(values, axis=1),
            (((1,), (1,)), ((), ())), preferred_element_type=jnp.float32,
        )
    total = total * (1.0 / math.sqrt(G))
    first = lax.axis_index("core") == 0
    mine_ref[...] = jnp.where(first, total[:64], total[64:])
    other_ref[...] = jnp.where(first, total[64:], total[:64])


def intersection_of(tiles, token):
    half = jax.ShapeDtypeStruct((64, 128), jnp.float32)
    return pl.pallas_call(
        intersection_body,
        out_shape=(jax.ShapeDtypeStruct((ROWS, 128), jnp.bfloat16), half, half),
        in_specs=[VMEM, pl.BlockSpec(memory_space=pl.ANY)],
        out_specs=(VMEM, VMEM, VMEM),
        scratch_shapes=[pltpu.VMEM((128 * WIDE, 128), jnp.float32)],
        compiler_params=pltpu.CompilerParams(vmem_limit_bytes=16 * 1024 * 1024),
        name="intersection",
    )(tiles, token)


def half_projected(lines_ref, half_ref, out_ref, row, result, left):
    table = half_ref[...]

    def copy(part):
        columns = pl.ds(part * 512, 512)
        rows = pl.ds(pl.multiple_of(row * 64, 64), 64)
        return pltpu.make_async_copy(result.at[:, columns], out_ref.at[rows, columns], left.at[part])

    for part in range(4):
        for line in (4 * part, 4 * part + 2):
            both = [lines_ref[pl.ds(index * 128, 128), :] for index in (line, line + 1)]
            value = dot(table, jnp.concatenate(both, axis=1)) * (-1.0 / math.sqrt(128))
            result[:, pl.ds(line * 128, 256)] = value.astype(jnp.bfloat16)
        copy(part).start()
    for part in range(4):
        copy(part).wait()


def first_half_body(lines_ref, mine_ref, out_ref, result, left):
    row = lax.axis_index("core")
    half_projected(lines_ref, mine_ref, out_ref, row, result, left)


def second_half_body(lines_ref, other_ref, earlier_ref, out_ref, result, left):
    row = 1 - lax.axis_index("core")
    half_projected(lines_ref, other_ref, out_ref, row, result, left)


def projected_half(body, name, operands, flops, **aliases):
    anywhere = pl.BlockSpec(memory_space=pltpu.HBM)
    return pl.pallas_call(
        body,
        out_shape=jax.ShapeDtypeStruct((128, ROWS), jnp.bfloat16),
        in_specs=[VMEM, VMEM] + [anywhere] * (len(operands) - 2),
        out_specs=anywhere,
        scratch_shapes=[
            pltpu.VMEM((64, ROWS), jnp.bfloat16),
            pltpu.SemaphoreType.DMA((4,)),
        ],
        compiler_params=pltpu.CompilerParams(vmem_limit_bytes=16 * 1024 * 1024),
        cost_estimate=pl.CostEstimate(
            flops=flops, bytes_accessed=1024 * 1024, transcendentals=0
        ),
        name=name,
        **aliases,
    )(*operands)


def projected_of(lines, mine):
    other = swapped(mine)
    first = projected_half(first_half_body, "projected_first", (lines, mine), NEAR_FLOPS)
    return projected_half(
        second_half_body,
        "projected_second",
        (lines, other, first),
        10**7,
        input_output_aliases={2: 0},
    )


def from_far(value):
    count = lax.axis_size(BAND)
    pairs = [(i, (i - 1 if i % 2 == 0 else i + 1) % count) for i in range(count)]
    return lax.ppermute(value, BAND, pairs)


def swapped(value):
    return lax.ppermute(value, "core", [(0, 1), (1, 0)])


def summed_over(value, axes):
    peers = lax.axis_size(axes)
    copies = jnp.broadcast_to(value[None], (peers,) + value.shape)
    tiles = lax.all_to_all(copies, axes, 0, 0, tiled=True)
    return jnp.sum(tiles.astype(jnp.float32), axis=0).astype(jnp.bfloat16)


def local(orbitals, trial, occupations):
    own = packed_with_flag(orbitals, flag_rows(occupations))
    far = from_far(own)
    again = copied(own)
    near = swapped(again)
    table, mixed, halves = (jnp.asarray(value) for value in constants())
    kernel = screened_kernel(again)
    both = packed_after(trial, kernel)
    owner, term = near_term(own, near, table, mixed, kernel)
    both = exchange_of(far, owner, term, both, table, mixed, halves, kernel)
    tiles = lax.all_to_all(both, BAND, 0, 0, tiled=True)
    flat, token = unpacked(both.reshape(2 * ROWS, 128))
    lines, mine, other = intersection_of(tiles.reshape(2 * ROWS, 128), token)
    half = (mine + swapped(other)).astype(jnp.bfloat16)
    half = summed_over(half, ("x", "y"))
    half = summed_over(half, "z")
    return flat, projected_of(lines, half)


def solution(mesh):
    finer = Mesh(mesh.devices.reshape(mesh.shape["spin"], 4, 2, 8, 2), SPIN_BAND)
    return jax.shard_map(
        local,
        mesh=finer,
        in_specs=(P(SPIN_BAND, None), P(SPIN_BAND, None), P(SPIN_BAND)),
        out_specs=(P(SPIN_BAND, None), P("spin", BAND)),
        check_vma=False,
    )
```

```python
import math

import jax
import jax.numpy as jnp
import ml_dtypes
import numpy as np
from jax import lax
from jax.experimental import pallas as pl
from jax.experimental.pallas import tpu as pltpu
from jax.sharding import Mesh
from jax.sharding import PartitionSpec as P

NG = 64
G = NG**3
ROWS = G // 128
FRACTION = 0.25
OMEGA = 1.0
BAND = ("y", "x", "z", "core")
SPIN_BAND = ("spin",) + BAND
ORDER = np.concatenate([np.arange(0, NG, 2), np.arange(1, NG, 2)])
STEP = 4
SPAN = 2 * STEP
PITCH = 72
WIDE = 40
HALF = NG // 2
NEAR_FLOPS = 10**10
VMEM = pl.BlockSpec(memory_space=pltpu.VMEM)
SMEM = pl.BlockSpec(memory_space=pltpu.SMEM)


def cas_table():
    indices = np.arange(NG)
    phases = (indices[:, None] * indices[None, :] % NG) * (2.0 * math.pi / NG)
    return (np.cos(phases) + np.sin(phases)).astype(np.float32).astype(ml_dtypes.bfloat16)


def squared_modes(index):
    modes = jnp.where(2 * index < NG, index, index - NG)
    wavenum = modes.astype(jnp.float32) * (2.0 * math.pi / NG)
    return wavenum * wavenum


def screened_body(earlier_ref, kernel_ref):
    first = squared_modes(lax.broadcasted_iota(jnp.int32, (NG, 128), 0))
    third = squared_modes(lax.rem(lax.broadcasted_iota(jnp.int32, (NG, 128), 1), NG))

    def one_line(line, carry):
        second = 2 * lax.rem(line, NG // 2) + lax.div(line, NG // 2)
        norm_sq = first + squared_modes(jnp.full((NG, 128), second, jnp.int32)) + third
        bounded = jnp.where(norm_sq > 0, norm_sq, 1.0)
        screened = jnp.where(
            norm_sq > 0,
            4.0 * math.pi / bounded * (1.0 - jnp.exp(-bounded / (4.0 * OMEGA * OMEGA))),
            math.pi / (OMEGA * OMEGA),
        )
        kernel_ref[line] = screened * (1.0 / G)
        return carry

    lax.fori_loop(0, NG, one_line, 0, unroll=2)


def screened_kernel(earlier):
    return pl.pallas_call(
        screened_body,
        out_shape=jax.ShapeDtypeStruct((NG, NG, 128), jnp.float32),
        in_specs=[pl.BlockSpec(memory_space=pl.ANY)],
        out_specs=VMEM,
        compiler_params=pltpu.CompilerParams(vmem_limit_bytes=16 * 1024 * 1024),
        cost_estimate=pl.CostEstimate(
            flops=NEAR_FLOPS, bytes_accessed=2 * 1024 * 1024, transcendentals=0
        ),
        name="screened_kernel",
    )(earlier)


def repeated(table):
    return np.kron(np.eye(STEP, dtype=np.float32), table.astype(np.float32)).astype(table.dtype)


def constants():
    table = cas_table()
    mixed = table[ORDER][:, ORDER]
    crossed = np.concatenate([table[HALF:, HALF:], table[HALF:, :HALF]], axis=1)
    halves = np.concatenate([table[:HALF], crossed], axis=0)
    return repeated(table), repeated(mixed), repeated(halves)


def dot(left, right):
    return lax.dot_general(
        left, right, (((1,), (0,)), ((), ())), preferred_element_type=jnp.float32
    )


def pack_body(flat_ref, tiles_ref):
    def part(step, carry):
        columns = pl.ds(pl.multiple_of(step * 16384, 16384), 16384)
        rows = pl.ds(pl.multiple_of(step * 128, 128), 128)
        tiles_ref[rows, :] = flat_ref[0:1, columns].reshape(128, 128)
        return carry

    lax.fori_loop(0, 16, part, 0)


def seed_body(seed_ref):
    seed_ref[...] = jnp.zeros(seed_ref.shape, seed_ref.dtype)


def seed():
    return pl.pallas_call(
        seed_body,
        out_shape=jax.ShapeDtypeStruct((8, 128), jnp.int32),
        out_specs=VMEM,
        compiler_params=pltpu.CompilerParams(vmem_limit_bytes=16 * 1024 * 1024),
        cost_estimate=pl.CostEstimate(
            flops=NEAR_FLOPS, bytes_accessed=4096, transcendentals=0
        ),
        name="seed",
    )()


def flag_body(flag_ref, seed_ref, rows_ref):
    flag = jnp.broadcast_to(flag_ref[...], (16, 128)) + seed_ref[pl.ds(0, 1), :]
    rows_ref[...] = flag.astype(jnp.float32).astype(jnp.bfloat16)


def flag_rows(flag):
    return pl.pallas_call(
        flag_body,
        out_shape=jax.ShapeDtypeStruct((16, 128), jnp.bfloat16),
        in_specs=[VMEM, VMEM],
        out_specs=VMEM,
        compiler_params=pltpu.CompilerParams(vmem_limit_bytes=16 * 1024 * 1024),
        name="flag_rows",
    )(flag.reshape(1, 1), seed())


def pack_flagged_body(flat_ref, rows_ref, tiles_ref):
    pack_body(flat_ref, tiles_ref)
    tiles_ref[pl.ds(ROWS, 16), :] = rows_ref[...]


def pack_after_body(flat_ref, earlier_ref, both_ref):
    both_ref[...] = flat_ref[...].reshape(256, 128).reshape(16, 16, 128)


def packed_after(flat, earlier):
    return pl.pallas_call(
        pack_after_body,
        grid=(8,),
        out_shape=jax.ShapeDtypeStruct((128, 32, 128), jnp.bfloat16),
        in_specs=[
            pl.BlockSpec((1, G // 8), lambda part: (0, part)),
            pl.BlockSpec(memory_space=pl.ANY),
        ],
        out_specs=pl.BlockSpec((16, 16, 128), lambda part: (part, 0, 0)),
        compiler_params=pltpu.CompilerParams(vmem_limit_bytes=16 * 1024 * 1024),
        name="pack",
    )(flat, earlier)


def again_body(tiles_ref, again_ref):
    again_ref[...] = tiles_ref[...]


def copied(tiles):
    return pl.pallas_call(
        again_body,
        out_shape=jax.ShapeDtypeStruct(tiles.shape, tiles.dtype),
        in_specs=[VMEM],
        out_specs=VMEM,
        compiler_params=pltpu.CompilerParams(vmem_limit_bytes=16 * 1024 * 1024),
        name="again",
    )(tiles)


def packed_with_flag(flat, rows):
    return pl.pallas_call(
        pack_flagged_body,
        out_shape=jax.ShapeDtypeStruct((ROWS + 16, 128), jnp.bfloat16),
        in_specs=[VMEM, VMEM],
        out_specs=VMEM,
        compiler_params=pltpu.CompilerParams(vmem_limit_bytes=16 * 1024 * 1024),
        name="pack_flagged",
    )(flat, rows)


def plane_rows(plane, height):
    if isinstance(plane, int):
        return pl.ds(plane * height, height)
    return pl.ds(pl.multiple_of(plane * height, height), height)


def pitched(plane):
    if isinstance(plane, int):
        return pl.ds(plane * PITCH, NG)
    return pl.ds(pl.multiple_of(plane * PITCH, 8), NG)


def beside(parts):
    return jnp.concatenate(
        [jnp.concatenate(parts[:STEP], axis=0), jnp.concatenate(parts[STEP:], axis=0)], axis=1
    )


def part_of(values, part):
    rows = slice(part % STEP * NG, part % STEP * NG + NG)
    return values[rows, :128] if part < STEP else values[rows, 128:]


def passes_there(density_of, table_ref, mixed_ref, kernel_ref, grid):
    bf16 = jnp.bfloat16

    def forward(step, carry):
        planes = [step * SPAN + part for part in range(SPAN)]
        values = beside([density_of(plane) for plane in planes])
        values = dot(values, table_ref[...]).astype(bf16)
        values = dot(mixed_ref[...], values)
        for part, plane in enumerate(planes):
            grid[pitched(plane), :] = part_of(values, part)
        return carry

    lax.fori_loop(0, NG // SPAN, forward, 0, unroll=True)

    def across(step, carry):
        lines = [step * SPAN + part for part in range(SPAN)]
        rows = [pl.ds(line, NG, stride=PITCH) for line in lines]
        values = beside([grid[row, :].astype(bf16) for row in rows])
        values = dot(table_ref[...], values)
        values = (values * beside([kernel_ref[line] for line in lines])).astype(bf16)
        values = dot(table_ref[...], values)
        for part, row in enumerate(rows):
            grid[row, :] = part_of(values, part)
        return carry

    lax.fori_loop(0, NG // SPAN, across, 0, unroll=True)

    def potentials(step):
        planes = [step * SPAN + part for part in range(SPAN)]
        values = beside([grid[pitched(plane), :].astype(bf16) for plane in planes])
        values = dot(mixed_ref[...], values).astype(bf16)
        values = dot(values, table_ref[...])
        return [(plane, part_of(values, part)) for part, plane in enumerate(planes)]

    return potentials


def fill_of(ref):
    return ref[pl.ds(ROWS, 16), :].astype(jnp.float32)[:1] * -FRACTION


def two_planes(ref, plane, low):
    first, second = (
        ref[plane_rows(index, 32), :].astype(jnp.float32) for index in (plane, plane + HALF)
    )
    first_turned, second_turned = (pltpu.roll(value, 64, 1) for value in (first, second))
    return jnp.concatenate(
        [jnp.where(low, first, second_turned), jnp.where(low, first_turned, second)], axis=0
    )


def low_lanes(height):
    return lax.broadcasted_iota(jnp.int32, (height, 128), 1) < 64


def near_body(
    own_ref, near_ref, table_ref, mixed_ref, kernel_ref, owner_ref, term_ref, visitors, grid
):
    f32, bf16 = jnp.float32, jnp.bfloat16
    low = low_lanes(NG // 2)

    def density_of(plane):
        own, near = (ref[plane_rows(plane, 32), :].astype(f32) for ref in (own_ref, near_ref))
        own_turned, near_turned = (pltpu.roll(value, 64, 1) for value in (own, near))
        mine = jnp.concatenate(
            [jnp.where(low, own, own_turned), jnp.where(low, own_turned, own)], axis=0
        )
        pairs = jnp.concatenate(
            [jnp.where(low, own, near_turned), jnp.where(low, own_turned, near)], axis=0
        )
        wide = plane_rows(plane, 64)
        visitors[wide, :] = pairs.astype(bf16)
        return (mine * pairs).astype(bf16)

    potentials = passes_there(density_of, table_ref, mixed_ref, kernel_ref, grid)
    fill = jnp.where(low_lanes(NG), fill_of(own_ref), fill_of(near_ref))
    for plane in range(HALF):
        owner_ref[plane_rows(plane, 64), :] = two_planes(own_ref, plane, low).astype(bf16)

    def backward(step, carry):
        for plane, potential in potentials(step):
            total = potential * (visitors[plane_rows(plane, 64), :].astype(f32) * fill)
            total = total + pltpu.roll(total, 64, 1)
            term_ref[plane_rows(plane, 32), :] = jnp.where(low, total[:32], total[32:])
        return carry

    lax.fori_loop(0, NG // SPAN, backward, 0, unroll=True)


def near_term(own, near, table, mixed, kernel):
    return pl.pallas_call(
        near_body,
        out_shape=(
            jax.ShapeDtypeStruct((HALF * NG, 128), jnp.bfloat16),
            jax.ShapeDtypeStruct((ROWS, 128), jnp.float32),
        ),
        in_specs=[VMEM] * 5,
        out_specs=(VMEM, VMEM),
        scratch_shapes=[
            pltpu.VMEM((NG * NG, 128), jnp.bfloat16),
            pltpu.VMEM((NG * PITCH, 128), jnp.float32),
        ],
        compiler_params=pltpu.CompilerParams(vmem_limit_bytes=24 * 1024 * 1024),
        cost_estimate=pl.CostEstimate(
            flops=NEAR_FLOPS, bytes_accessed=4 * 1024 * 1024, transcendentals=0
        ),
        name="near_term",
    )(own, near, table, mixed, kernel)


def exchange_body(
    far_ref, owner_ref, term_ref, both_ref, table_ref, mixed_ref, halves_ref, kernel_ref,
    out_ref, visitors, grid, tiles, left,
):
    f32, bf16 = jnp.float32, jnp.bfloat16
    low = low_lanes(HALF)

    for step in range(HALF // SPAN):
        planes = [step * SPAN + part for part in range(SPAN)]
        densities = []
        for plane in planes:
            far = two_planes(far_ref, plane, low)
            wide = plane_rows(plane, 64)
            visitors[wide, :] = far.astype(bf16)
            densities.append((far * owner_ref[wide, :].astype(f32)).astype(bf16))
        values = dot(beside(densities), table_ref[...]).astype(bf16)
        values = dot(mixed_ref[...], values)
        for part, plane in enumerate(planes):
            grid[pitched(plane), :] = part_of(values, part)

    def crossed(value):
        value = value.astype(bf16)
        return jnp.concatenate(
            [value, jnp.concatenate([value[:, 64:], value[:, :64]], axis=1)], axis=0
        )

    def joined(value):
        return jnp.where(low, value[:HALF], value[HALF:])

    for step in range(NG // SPAN):
        lines = [step * SPAN + part for part in range(SPAN)]
        rows = [pl.ds(line, HALF, stride=PITCH) for line in lines]
        values = dot(halves_ref[...], beside([crossed(grid[row, :]) for row in rows]))
        values = beside(
            [
                crossed(joined(part_of(values, part)) * joined(kernel_ref[line]))
                for part, line in enumerate(lines)
            ]
        )
        values = dot(halves_ref[...], values)
        for part, row in enumerate(rows):
            grid[row, :] = joined(part_of(values, part))

    fill = fill_of(far_ref)

    def tile_copies(step):
        copies = []
        for half in range(2):
            peers = pl.ds(step * 2 * SPAN + half * NG, 2 * SPAN)
            copies.append(
                pltpu.make_async_copy(
                    tiles.at[peers], out_ref.at[peers, pl.ds(16, 16), :], left.at[half, step]
                )
            )
        return copies

    for step in range(HALF // SPAN):
        planes = [step * SPAN + part for part in range(SPAN)]
        values = beside([grid[pitched(plane), :].astype(bf16) for plane in planes])
        values = dot(mixed_ref[...], values).astype(bf16)
        values = dot(values, table_ref[...])
        for part, plane in enumerate(planes):
            weight = visitors[plane_rows(plane, 64), :].astype(f32) * fill
            total = part_of(values, part) * weight
            turned = pltpu.roll(total, 64, 1)
            first = jnp.where(low, total[:HALF], turned[HALF:])
            second = jnp.where(low, turned[:HALF], total[HALF:])
            for index, value in ((plane, first), (plane + HALF, second)):
                value = value + term_ref[plane_rows(index, 32), :]
                tiles[pl.ds(2 * index, 2)] = value.astype(bf16).reshape(2, 16, 128)
        for copy in tile_copies(step):
            copy.start()
    for step in range(HALF // SPAN):
        for copy in tile_copies(step):
            copy.wait()


def exchange_of(far, owner, term, both, table, mixed, halves, kernel):
    return pl.pallas_call(
        exchange_body,
        out_shape=jax.ShapeDtypeStruct((128, 32, 128), jnp.bfloat16),
        in_specs=[VMEM] * 3 + [pl.BlockSpec(memory_space=pltpu.HBM)] + [VMEM] * 4,
        out_specs=pl.BlockSpec(memory_space=pltpu.HBM),
        input_output_aliases={3: 0},
        scratch_shapes=[
            pltpu.VMEM((HALF * NG, 128), jnp.bfloat16),
            pltpu.VMEM((HALF * PITCH, 128), jnp.float32),
            pltpu.VMEM((128, 16, 128), jnp.bfloat16),
            pltpu.SemaphoreType.DMA((2, HALF // SPAN)),
        ],
        compiler_params=pltpu.CompilerParams(vmem_limit_bytes=24 * 1024 * 1024),
        name="exchange",
    )(far, owner, term, both, table, mixed, halves, kernel)


def unpack_body(tiles_ref, flat_ref, token_ref):
    def part(step, carry):
        columns = pl.ds(pl.multiple_of(step * 16384, 16384), 16384)
        tiles = [tiles_ref[pl.ds(step * 256 + peer * 32 + 16, 16), :] for peer in range(8)]
        value = jnp.concatenate(tiles, axis=0).astype(jnp.float32).reshape(1, 16384)
        flat_ref[0:1, columns] = value.astype(jnp.bfloat16)
        return carry

    lax.fori_loop(0, 16, part, 0)
    token_ref[...] = tiles_ref[pl.ds(0, 16), :]


def unpacked(tiles):
    return pl.pallas_call(
        unpack_body,
        out_shape=(
            jax.ShapeDtypeStruct((1, G), jnp.bfloat16),
            jax.ShapeDtypeStruct((16, 128), jnp.bfloat16),
        ),
        in_specs=[VMEM],
        out_specs=(VMEM, VMEM),
        compiler_params=pltpu.CompilerParams(vmem_limit_bytes=16 * 1024 * 1024),
        name="unpack",
    )(tiles)


def intersection_body(tiles_ref, token_ref, lines_ref, mine_ref, other_ref, wide):
    bf16 = jnp.bfloat16
    for peer in range(128):
        wide[pl.ds(peer * WIDE, 32), :] = tiles_ref[pl.ds(peer * 32, 32), :].astype(jnp.float32)
    total = jnp.zeros((128, 128), jnp.float32)
    for line in range(0, 16, 2):
        trials, values = [], []
        for index in (line, line + 1):
            trials.append(wide[pl.ds(index, 128, stride=WIDE), :].astype(bf16))
            value = wide[pl.ds(index + 16, 128, stride=WIDE), :].astype(bf16)
            lines_ref[pl.ds(index * 128, 128), :] = value
            values.append(value)
        total = total + lax.dot_general(
            jnp.concatenate(trials, axis=1), jnp.concatenate(values, axis=1),
            (((1,), (1,)), ((), ())), preferred_element_type=jnp.float32,
        )
    total = total * (1.0 / math.sqrt(G))
    first = lax.axis_index("core") == 0
    mine_ref[...] = jnp.where(first, total[:64], total[64:])
    other_ref[...] = jnp.where(first, total[64:], total[:64])


def intersection_of(tiles, token):
    half = jax.ShapeDtypeStruct((64, 128), jnp.float32)
    return pl.pallas_call(
        intersection_body,
        out_shape=(jax.ShapeDtypeStruct((ROWS, 128), jnp.bfloat16), half, half),
        in_specs=[VMEM, pl.BlockSpec(memory_space=pl.ANY)],
        out_specs=(VMEM, VMEM, VMEM),
        scratch_shapes=[pltpu.VMEM((128 * WIDE, 128), jnp.float32)],
        compiler_params=pltpu.CompilerParams(vmem_limit_bytes=16 * 1024 * 1024),
        name="intersection",
    )(tiles, token)


def half_projected(lines_ref, half_ref, out_ref, row, result, left):
    table = half_ref[...]

    def copy(part):
        columns = pl.ds(part * 256, 256)
        rows = pl.ds(pl.multiple_of(row * 64, 64), 64)
        return pltpu.make_async_copy(result.at[:, columns], out_ref.at[rows, columns], left.at[part])

    for part in range(8):
        for line in (2 * part,):
            both = [lines_ref[pl.ds(index * 128, 128), :] for index in (line, line + 1)]
            value = dot(table, jnp.concatenate(both, axis=1)) * (-1.0 / math.sqrt(128))
            result[:, pl.ds(line * 128, 256)] = value.astype(jnp.bfloat16)
        copy(part).start()
    for part in range(8):
        copy(part).wait()


def first_half_body(lines_ref, mine_ref, out_ref, result, left):
    row = lax.axis_index("core")
    half_projected(lines_ref, mine_ref, out_ref, row, result, left)


def second_half_body(lines_ref, other_ref, earlier_ref, out_ref, result, left):
    row = 1 - lax.axis_index("core")
    half_projected(lines_ref, other_ref, out_ref, row, result, left)


def projected_half(body, name, operands, flops, **aliases):
    anywhere = pl.BlockSpec(memory_space=pltpu.HBM)
    return pl.pallas_call(
        body,
        out_shape=jax.ShapeDtypeStruct((128, ROWS), jnp.bfloat16),
        in_specs=[VMEM, VMEM] + [anywhere] * (len(operands) - 2),
        out_specs=anywhere,
        scratch_shapes=[
            pltpu.VMEM((64, ROWS), jnp.bfloat16),
            pltpu.SemaphoreType.DMA((8,)),
        ],
        compiler_params=pltpu.CompilerParams(vmem_limit_bytes=16 * 1024 * 1024),
        cost_estimate=pl.CostEstimate(
            flops=flops, bytes_accessed=1024 * 1024, transcendentals=0
        ),
        name=name,
        **aliases,
    )(*operands)


def projected_of(lines, mine):
    other = swapped(mine)
    first = projected_half(first_half_body, "projected_first", (lines, mine), NEAR_FLOPS)
    return projected_half(
        second_half_body,
        "projected_second",
        (lines, other, first),
        10**7,
        input_output_aliases={2: 0},
    )


def from_far(value):
    count = lax.axis_size(BAND)
    pairs = [(i, (i - 1 if i % 2 == 0 else i + 1) % count) for i in range(count)]
    return lax.ppermute(value, BAND, pairs)


def swapped(value):
    return lax.ppermute(value, "core", [(0, 1), (1, 0)])


def summed_over(value, axes):
    peers = lax.axis_size(axes)
    copies = jnp.broadcast_to(value[None], (peers,) + value.shape)
    tiles = lax.all_to_all(copies, axes, 0, 0, tiled=True)
    return jnp.sum(tiles.astype(jnp.float32), axis=0).astype(jnp.bfloat16)


def local(orbitals, trial, occupations):
    own = packed_with_flag(orbitals, flag_rows(occupations))
    far = from_far(own)
    again = copied(own)
    near = swapped(again)
    table, mixed, halves = (jnp.asarray(value) for value in constants())
    kernel = screened_kernel(again)
    both = packed_after(trial, kernel)
    owner, term = near_term(own, near, table, mixed, kernel)
    both = exchange_of(far, owner, term, both, table, mixed, halves, kernel)
    tiles = lax.all_to_all(both, BAND, 0, 0, tiled=True)
    flat, token = unpacked(both.reshape(2 * ROWS, 128))
    lines, mine, other = intersection_of(tiles.reshape(2 * ROWS, 128), token)
    half = (mine + swapped(other)).astype(jnp.bfloat16)
    half = summed_over(half, ("x", "y"))
    half = summed_over(half, "z")
    return flat, projected_of(lines, half)


def solution(mesh):
    finer = Mesh(mesh.devices.reshape(mesh.shape["spin"], 4, 2, 8, 2), SPIN_BAND)
    return jax.shard_map(
        local,
        mesh=finer,
        in_specs=(P(SPIN_BAND, None), P(SPIN_BAND, None), P(SPIN_BAND)),
        out_specs=(P(SPIN_BAND, None), P("spin", BAND)),
        check_vma=False,
    )
```
